32 devices in a mesh: parts: 2 (over y), train: 4 (over z), layer: 2 (over x), sub: 2 (over core).
Axes of the slice: x: 2, y: 2, z: 4, core: 2. Of those that a mesh axis runs over, the one named last changes fastest.
Arguments:
- inputs: bfloat16 [2, 2048, 4096], P('layer', ('parts', 'train')), parts along dimension 1, may hold values from -6 to 6
- out_grads: bfloat16 [2, 2048, 4096], P('layer', ('parts', 'train')), parts along dimension 1, may hold values from -6 to 6
- proj_in: bfloat16 [2, 64, 4096], P('layer'), may hold values from -0.09375 to 0.09375
- proj_out: bfloat16 [2, 64, 4096], P('layer'), may hold values from -0.09375 to 0.09375
- basis_in: float32 [2, 64, 64], P('layer'), may hold values from -0.75 to 0.75
- basis_out: float32 [2, 64, 64], P('layer'), may hold values from -0.75 to 0.75
- eigen: float32 [2, 64, 64], P('layer'), may hold values from 0.25 to 4
- queries: bfloat16 [2, 2048, 4096], P('layer', ('parts', 'train', 'sub')), parts along dimension 1, may hold values from -0.0234375 to 0.0234375
Outputs:
- scores: float32 [2048, 4, 2, 128], P(('parts', 'train', 'layer'), None, 'sub'), parts along dimension 0
The draws below stay inside these ranges and needn't reach their ends.
There are 2 independent parts, one for each index of `parts`. The reference program is written for one: setup_inputs(seed, part) draws one part's arguments, and reference() takes and returns one part's arrays. A program takes and returns all parts, laid end to end along the dimension named above; an argument that names none is the same for every part. Nothing has to cross between parts.
All inputs are finite; a program needn't handle non-finite values.
Results may differ from the reference program's by a relative error of at most 0.01.
Values may be sent and summed in bfloat16 or wider, within the bound.
No kernel may reach another device: no remote copies, remote signals or barrier semaphores. Data moves between devices by JAX's collectives and lax.ppermute only.
A program may use at most 128 MiB of HBM per device.

```python
import math
import jax
import jax.numpy as jnp
from jax import lax

D = 4096
R = 64
QDEV = 128
LAYERS = 2
TOKENS = 1024
Q = 1024
N_TRAIN = 4
N_SUB = 2


def strengthened(entries, stream_key, source, target, parts, factor):
    owner, partner = [(jnp.arange(entries.shape[position]) // (entries.shape[position] // parts)).reshape([-1 if axis == position else 1 for axis in range(entries.ndim)]) for position in (source, target)]
    chosen = jax.random.permutation(stream_key, parts)[partner]
    strong = (owner == chosen) | (owner == (partner + parts // 2) % parts)
    return jnp.where(strong, factor * entries, entries)


def level_of(key, extent, shards, smallest, largest):
    def one(axis_at, shards_of):
        steps = jax.random.uniform(jax.random.fold_in(jax.random.fold_in(key, 6), axis_at), (shards_of,), jnp.float32, smallest / len(shards), largest / len(shards))
        return jnp.repeat(jnp.exp(steps), extent[axis_at] // shards_of).reshape((-1,) + (1,) * (len(extent) - axis_at - 1))

    loudness = one(*shards[0])
    for cut in shards[1:]:
        loudness = loudness * one(*cut)
    return loudness


def bell_draw(rng, dims, spread, reach, pieces=(), kind=jnp.bfloat16):
    result = jax.random.normal(rng, dims, jnp.float32) * spread
    if len(pieces) > 0:
        result = level_of(rng, dims, pieces, -0.22, 0.18) * result
    return jnp.clip(result, min=-reach, max=reach).astype(kind)


def bell_draw_with(rng, shape, deviation, reach, shards, heavy, held_as=jnp.bfloat16):
    result = deviation * jax.random.normal(rng, shape, jnp.float32)
    if shards:
        result = result * level_of(rng, shape, shards, -0.22, 0.18)
    return jnp.clip(strengthened(result, jax.random.fold_in(rng, 3), *heavy), -reach, reach).astype(held_as)


def setup_inputs(seed: int = 0, part: int = 0) -> dict:
    splits = jax.random.split(jax.random.key(seed), 9)
    part_splits = jax.random.split(jax.random.fold_in(splits[8], part), 9)
    return {
        "inputs": bell_draw(part_splits[0], (LAYERS, TOKENS, D), 1.0, 6.0, ((0, 2), (1, 4))),
        "out_grads": bell_draw_with(part_splits[1], (LAYERS, TOKENS, D), 1.0, 6.0, ((0, 2), (1, 4)), (0, 1, 2, 2.0)),
        "proj_in": bell_draw(splits[2], (LAYERS, R, D), D ** -0.5, 0.09375, ((0, 2),)),
        "proj_out": bell_draw(splits[3], (LAYERS, R, D), D ** -0.5, 0.09375, ((0, 2),)),
        "basis_in": bell_draw(splits[4], (LAYERS, R, R), R ** -0.5, 0.75, ((0, 2),), jnp.float32),
        "basis_out": bell_draw(splits[5], (LAYERS, R, R), R ** -0.5, 0.75, ((0, 2),), jnp.float32),
        "eigen": jnp.clip(jnp.exp(math.log(4.0) - 2.7725887 * jax.random.uniform(splits[6], (LAYERS, R, R), jnp.float32) ** level_of(splits[6], (LAYERS, R, R), ((0, 2),), -0.2, 0.2)), 0.25, 4.0),
        "queries": bell_draw(part_splits[7], (LAYERS, Q, R * R), (1.0 / (4 * R)), 0.0234375, ((0, 2), (1, 8))),
    }


def precondition(query_block, basis_in, basis_out, eigen):
    count = query_block.shape[0]
    rank_size = basis_in.shape[0]
    matrices = query_block.astype(jnp.float32).reshape(count, rank_size, rank_size)
    damping = 0.1 * jnp.mean(eigen)
    half_turn = jnp.einsum("ia,qij->qaj", basis_out, matrices, precision=lax.Precision.HIGHEST)
    rotated = jnp.einsum("qaj,jb->qab", half_turn, basis_in, precision=lax.Precision.HIGHEST)
    scaled = rotated / (eigen + damping)
    back_left = jnp.einsum("ia,qab->qib", basis_out, scaled, precision=lax.Precision.HIGHEST)
    back_full = jnp.einsum("qib,jb->qij", back_left, basis_in, precision=lax.Precision.HIGHEST)
    return back_full.astype(jnp.bfloat16).reshape(count, rank_size * rank_size)


def reference(inputs, out_grads, proj_in, proj_out, basis_in, basis_out, eigen, queries):
    scores = jnp.zeros((TOKENS, Q), jnp.float32)
    for layer_idx in range(LAYERS):
        feat_in = jnp.dot(inputs[layer_idx].astype(jnp.float32), proj_in[layer_idx].astype(jnp.float32).T).astype(jnp.bfloat16)
        feat_out = jnp.dot(out_grads[layer_idx].astype(jnp.float32), proj_out[layer_idx].astype(jnp.float32).T).astype(jnp.bfloat16)
        token_grads = (feat_out.astype(jnp.float32)[:, :, None] * feat_in.astype(jnp.float32)[:, None, :]).astype(jnp.bfloat16)
        token_grads = token_grads.reshape(TOKENS, R * R)
        precond = precondition(queries[layer_idx], basis_in[layer_idx], basis_out[layer_idx], eigen[layer_idx])
        scores = scores + jnp.dot(token_grads.astype(jnp.float32), precond.astype(jnp.float32).T)
    return scores.reshape(TOKENS, N_TRAIN, N_SUB, QDEV)
```

```python
import functools

import jax
import jax.numpy as jnp
from jax import lax
from jax.experimental import pallas as pl
from jax.experimental.pallas import tpu as pltpu
from jax.sharding import PartitionSpec as P

F32 = jnp.float32
BF16 = jnp.bfloat16
PACK = 4


def nt(left, right, precision=None):
    return lax.dot_general(
        left, right, (((1,), (1,)), ((), ())), precision=precision, preferred_element_type=F32
    )


def block_diagonal(matrix):
    rank = matrix.shape[0]
    wide = jnp.concatenate([matrix] * PACK, axis=1)
    tall = jnp.concatenate([wide] * PACK, axis=0)
    rows = lax.broadcasted_iota(jnp.int32, tall.shape, 0) // rank
    columns = lax.broadcasted_iota(jnp.int32, tall.shape, 1) // rank
    return jnp.where(rows == columns, tall, 0.0)


def features_kernel(chunks, inputs_hbm, grads_hbm, proj_in_hbm, proj_out_hbm, basis_in, basis_out,
                    feats, inputs, grads, proj_in, proj_out, sems):
    rank = basis_in.shape[0]
    step = inputs.shape[1] // chunks
    pairs = ((inputs_hbm, inputs), (proj_in_hbm, proj_in), (grads_hbm, grads), (proj_out_hbm, proj_out))

    def copy(which, chunk):
        source, target = pairs[which]
        columns = pl.ds(chunk * step, step)
        return pltpu.make_async_copy(
            source.at[0, :, columns], target.at[:, columns], sems.at[which, chunk]
        )

    for side in (0, 2):
        for chunk in range(chunks):
            copy(side, chunk).start()
            copy(side + 1, chunk).start()
    for side, rows, proj, basis in ((0, inputs, proj_in, basis_in), (2, grads, proj_out, basis_out)):
        total = None
        for chunk in range(chunks):
            copy(side, chunk).wait()
            copy(side + 1, chunk).wait()
            columns = slice(chunk * step, (chunk + 1) * step)
            term = nt(rows[:, columns], proj[:, columns])
            total = term if total is None else total + term
        turned = nt(basis[...].T, total, lax.Precision.HIGHEST)
        feats[side // 2 * rank:(side // 2 + 1) * rank, :] = turned.astype(BF16)


def score_block(feats, weights, rank):
    tokens = feats.shape[1]
    side_in = feats[:rank, :].astype(F32)
    side_out = feats[rank:, :].reshape(rank // 16, 16, tokens)
    total = None
    for part in range(rank // PACK):
        products = []
        for b in range(part * PACK, (part + 1) * PACK):
            row = jnp.broadcast_to(side_in[b:b + 1, :], (16, tokens)).astype(BF16)
            products.append((side_out * row[None]).reshape(rank, tokens))
        width = PACK * rank
        term = jnp.dot(
            weights[:, part * width:(part + 1) * width],
            jnp.concatenate(products, axis=0),
            preferred_element_type=F32,
        )
        total = term if total is None else total + term
    return total.T


def queries_kernel(queries, basis_in, basis_out, eigen, weights, half):
    rank = basis_in.shape[0]
    width = PACK * rank
    groups = rank // PACK
    right = block_diagonal(basis_in[...].T).astype(BF16)
    for part in range(groups):
        half[part * width:(part + 1) * width, :] = nt(
            right, queries[:, part * width:(part + 1) * width]
        )
    left = block_diagonal(basis_out[...]).astype(BF16)
    spectrum = eigen[...]
    inverse = (1.0 / (spectrum + 0.1 * jnp.mean(spectrum))).T
    for part in range(groups):
        columns = range(part * PACK, (part + 1) * PACK)
        matrix = jnp.concatenate(
            [half[pl.ds(b, rank, stride=rank), :] for b in columns], axis=0
        )
        turned = jnp.dot(matrix.T.astype(BF16), left, preferred_element_type=F32)
        scale = jnp.concatenate([inverse[b:b + 1, :] for b in columns], axis=1)
        weights[:, part * width:(part + 1) * width] = (turned * scale).astype(BF16)


def scores_kernel(train_size, layer_size, rank, weights, *refs):
    feats, blocks = refs[:-1], refs[-1]
    here = lax.axis_index("train")
    rows = blocks.shape[1]
    for offset in range(train_size):
        scores = score_block(feats[offset][...], weights, rank).astype(BF16)
        owner = lax.rem(here + offset, train_size)
        for layer in range(layer_size):
            blocks[owner * layer_size + layer] = scores[layer * rows:(layer + 1) * rows, :]


def sum_kernel(train_size, layer_size, blocks, out):
    rows = blocks.shape[1]
    for source in range(train_size):
        total = blocks[source * layer_size].astype(F32)
        for layer in range(1, layer_size):
            total = total + blocks[source * layer_size + layer].astype(F32)
        out[pl.ds(source, rows, stride=train_size), :] = total


def body(inputs, out_grads, proj_in, proj_out, basis_in, basis_out, eigen, queries):
    train_size, layer_size = lax.axis_size("train"), lax.axis_size("layer")
    tokens, width = inputs.shape[1:]
    count, entries = queries.shape[1:]
    rank = proj_in.shape[1]
    chunks = 4
    vmem, hbm = pl.BlockSpec(memory_space=pltpu.VMEM), pl.BlockSpec(memory_space=pl.ANY)
    params = pltpu.CompilerParams(vmem_limit_bytes=32 << 20)

    feats = pl.pallas_call(
        functools.partial(features_kernel, chunks),
        out_shape=jax.ShapeDtypeStruct((2 * rank, tokens), BF16),
        in_specs=[hbm] * 4 + [vmem] * 2,
        out_specs=vmem,
        scratch_shapes=[
            pltpu.VMEM((tokens, width), BF16),
            pltpu.VMEM((tokens, width), BF16),
            pltpu.VMEM((rank, width), BF16),
            pltpu.VMEM((rank, width), BF16),
            pltpu.SemaphoreType.DMA((4, chunks)),
        ],
        compiler_params=params,
        cost_estimate=pl.CostEstimate(
            flops=4 * tokens * rank * width, bytes_accessed=4 * width * (tokens + rank), transcendentals=0
        ),
        name="features",
    )(inputs, out_grads, proj_in, proj_out, basis_in[0], basis_out[0])

    gathered = [feats] + [
        lax.ppermute(
            feats, "train", [((j + offset) % train_size, j) for j in range(train_size)]
        )
        for offset in range(1, train_size)
    ]

    weights = pl.pallas_call(
        queries_kernel,
        out_shape=jax.ShapeDtypeStruct((count, entries), BF16),
        in_specs=[vmem] * 4,
        out_specs=vmem,
        scratch_shapes=[pltpu.VMEM((entries, count), F32)],
        compiler_params=params,
        cost_estimate=pl.CostEstimate(
            flops=4 * PACK * count * entries * rank, bytes_accessed=4 * count * entries, transcendentals=0
        ),
        name="queries",
    )(queries[0], basis_in[0], basis_out[0], eigen[0])

    rows = tokens // layer_size
    blocks = pl.pallas_call(
        functools.partial(scores_kernel, train_size, layer_size, rank),
        out_shape=jax.ShapeDtypeStruct((train_size * layer_size, rows, count), BF16),
        in_specs=[vmem] * (train_size + 1),
        out_specs=vmem,
        compiler_params=params,
        cost_estimate=pl.CostEstimate(
            flops=2 * train_size * tokens * entries * count, bytes_accessed=2 * count * entries, transcendentals=0
        ),
        name="scores",
    )(weights, *gathered)

    arrived = lax.all_to_all(blocks, ("train", "layer"), 0, 0, tiled=True)

    total = pl.pallas_call(
        functools.partial(sum_kernel, train_size, layer_size),
        out_shape=jax.ShapeDtypeStruct((rows * train_size, count), F32),
        in_specs=[vmem],
        out_specs=vmem,
        compiler_params=params,
        name="sum",
    )(arrived)
    return total.reshape(rows, train_size, 1, count)


def solution(mesh):
    placed = (
        P("layer", ("parts", "train"), None),
        P("layer", ("parts", "train"), None),
        P("layer", None, None),
        P("layer", None, None),
        P("layer", None, None),
        P("layer", None, None),
        P("layer", None, None),
        P("layer", ("parts", "train", "sub"), None),
    )
    return jax.shard_map(
        body,
        mesh=mesh,
        in_specs=placed,
        out_specs=P(("parts", "train", "layer"), None, "sub", None),
        check_vma=False,
    )
```

```python
import functools

import jax
import jax.numpy as jnp
from jax import lax
from jax.experimental import pallas as pl
from jax.experimental.pallas import tpu as pltpu
from jax.sharding import PartitionSpec as P

F32 = jnp.float32
BF16 = jnp.bfloat16
PACK = 4


def nt(left, right, precision=None):
    return lax.dot_general(
        left, right, (((1,), (1,)), ((), ())), precision=precision, preferred_element_type=F32
    )


def block_diagonal(matrix):
    rank = matrix.shape[0]
    wide = jnp.concatenate([matrix] * PACK, axis=1)
    tall = jnp.concatenate([wide] * PACK, axis=0)
    rows = lax.broadcasted_iota(jnp.int32, tall.shape, 0) // rank
    columns = lax.broadcasted_iota(jnp.int32, tall.shape, 1) // rank
    return jnp.where(rows == columns, tall, 0.0)


def features_kernel(chunks, *refs):
    sources, feats, targets, sems = refs[:6], refs[6], refs[7:13], refs[13]
    inputs, grads, proj_in, proj_out, basis_in, basis_out = targets
    rank = basis_in.shape[0]
    step = inputs.shape[1] // chunks

    def copy(which, chunk):
        source, target = sources[which], targets[which]
        if which >= 4:
            return pltpu.make_async_copy(source.at[0], target, sems.at[which, 0])
        columns = pl.ds(chunk * step, step)
        return pltpu.make_async_copy(
            source.at[0, :, columns], target.at[:, columns], sems.at[which, chunk]
        )

    sides = ((0, 2, 4), (1, 3, 5))
    for side in sides:
        for chunk in range(chunks):
            copy(side[0], chunk).start()
            copy(side[1], chunk).start()
        copy(side[2], 0).start()
    for place, (tokens, proj, basis) in enumerate(sides):
        total = None
        for chunk in range(chunks):
            copy(tokens, chunk).wait()
            copy(proj, chunk).wait()
            columns = slice(chunk * step, (chunk + 1) * step)
            term = nt(targets[tokens][:, columns], targets[proj][:, columns])
            total = term if total is None else total + term
        copy(basis, 0).wait()
        turned = nt(targets[basis][...].T, total, lax.Precision.HIGHEST)
        feats[place * rank:(place + 1) * rank, :] = turned.astype(BF16)


def score_block(feats, weights, rank):
    tokens = feats.shape[1]
    side_in = feats[:rank, :].astype(F32)
    side_out = feats[rank:, :].reshape(rank // 16, 16, tokens)
    total = None
    for part in range(rank // PACK):
        products = []
        for b in range(part * PACK, (part + 1) * PACK):
            row = jnp.broadcast_to(side_in[b:b + 1, :], (16, tokens)).astype(BF16)
            products.append((side_out * row[None]).reshape(rank, tokens))
        width = PACK * rank
        term = jnp.dot(
            weights[:, part * width:(part + 1) * width],
            jnp.concatenate(products, axis=0),
            preferred_element_type=F32,
        )
        total = term if total is None else total + term
    return total.T


def queries_kernel(queries, basis_in, basis_out, eigen, weights, half):
    rank = basis_in.shape[0]
    width = PACK * rank
    groups = rank // PACK
    right = block_diagonal(basis_in[...].T).astype(BF16)
    for part in range(groups):
        half[part * width:(part + 1) * width, :] = nt(
            right, queries[:, part * width:(part + 1) * width]
        )
    left = block_diagonal(basis_out[...]).astype(BF16)
    spectrum = eigen[...]
    inverse = (1.0 / (spectrum + 0.1 * jnp.mean(spectrum))).T
    for part in range(groups):
        columns = range(part * PACK, (part + 1) * PACK)
        matrix = jnp.concatenate(
            [half[pl.ds(b, rank, stride=rank), :] for b in columns], axis=0
        )
        turned = jnp.dot(matrix.T.astype(BF16), left, preferred_element_type=F32)
        scale = jnp.concatenate([inverse[b:b + 1, :] for b in columns], axis=1)
        weights[:, part * width:(part + 1) * width] = (turned * scale).astype(BF16)


def scores_kernel(train_size, layer_size, rank, weights, *refs):
    feats, blocks, scores = refs[:train_size], refs[train_size:-1], refs[-1]
    place, layer = lax.axis_index("train"), lax.axis_index("layer")
    rows = blocks[0].shape[1]
    for offset in range(train_size):
        scores[...] = score_block(feats[offset][...], weights, rank)
        owner = lax.rem(place + offset, train_size)
        for k, block in enumerate(blocks):
            first = pl.multiple_of(lax.rem(layer + k, layer_size) * rows, rows)
            block[owner] = scores[pl.ds(first, rows), :].astype(block.dtype)


def layers_kernel(own, *refs):
    others, out = refs[:-1], refs[-1]
    total = own[...]
    for other in others:
        total = total + other[...].astype(F32)
    out[...] = total.astype(BF16)


def place_kernel(train_size, blocks, out):
    rows = blocks.shape[1]
    for source in range(train_size):
        out[pl.ds(source, rows, stride=train_size), :] = blocks[source].astype(F32)


def body(inputs, out_grads, proj_in, proj_out, basis_in, basis_out, eigen, queries):
    train_size, layer_size = lax.axis_size("train"), lax.axis_size("layer")
    tokens, width = inputs.shape[1:]
    count, entries = queries.shape[1:]
    rank = proj_in.shape[1]
    chunks = 4
    vmem, hbm = pl.BlockSpec(memory_space=pltpu.VMEM), pl.BlockSpec(memory_space=pltpu.HBM)
    params = pltpu.CompilerParams(vmem_limit_bytes=32 << 20)

    feats = pl.pallas_call(
        functools.partial(features_kernel, chunks),
        out_shape=jax.ShapeDtypeStruct((2 * rank, tokens), BF16),
        in_specs=[hbm] * 6,
        out_specs=vmem,
        scratch_shapes=[
            pltpu.VMEM((tokens, width), BF16),
            pltpu.VMEM((tokens, width), BF16),
            pltpu.VMEM((rank, width), BF16),
            pltpu.VMEM((rank, width), BF16),
            pltpu.VMEM((rank, rank), F32),
            pltpu.VMEM((rank, rank), F32),
            pltpu.SemaphoreType.DMA((6, chunks)),
        ],
        compiler_params=params,
        cost_estimate=pl.CostEstimate(
            flops=4 * tokens * rank * width, bytes_accessed=4 * width * (tokens + rank), transcendentals=0
        ),
        name="features",
    )(*[
        pltpu.with_memory_space_constraint(value, pltpu.HBM)
        for value in (inputs, out_grads, proj_in, proj_out, basis_in, basis_out)
    ])

    gathered = [feats] + [
        lax.ppermute(
            feats, "train", [((j + offset) % train_size, j) for j in range(train_size)]
        )
        for offset in range(1, train_size)
    ]

    weights = pl.pallas_call(
        queries_kernel,
        out_shape=jax.ShapeDtypeStruct((count, entries), BF16),
        in_specs=[vmem] * 4,
        out_specs=vmem,
        scratch_shapes=[pltpu.VMEM((entries, count), F32)],
        compiler_params=params,
        cost_estimate=pl.CostEstimate(
            flops=4 * PACK * count * entries * rank, bytes_accessed=4 * count * entries, transcendentals=0
        ),
        name="queries",
    )(queries[0], basis_in[0], basis_out[0], eigen[0])

    rows = tokens // layer_size
    own, *away = pl.pallas_call(
        functools.partial(scores_kernel, train_size, layer_size, rank),
        out_shape=[
            jax.ShapeDtypeStruct((train_size, rows, count), BF16 if k else F32)
            for k in range(layer_size)
        ],
        in_specs=[vmem] * (train_size + 1),
        out_specs=[vmem] * layer_size,
        scratch_shapes=[pltpu.VMEM((tokens, count), F32)],
        compiler_params=params,
        cost_estimate=pl.CostEstimate(
            flops=2 * train_size * tokens * entries * count, bytes_accessed=2 * count * entries, transcendentals=0
        ),
        name="scores",
    )(weights, *gathered)

    others = [
        lax.ppermute(block, "layer", [(l, (l + k) % layer_size) for l in range(layer_size)])
        for k, block in enumerate(away, 1)
    ]
    summed = pl.pallas_call(
        layers_kernel,
        out_shape=jax.ShapeDtypeStruct((train_size, rows, count), BF16),
        in_specs=[vmem] * layer_size,
        out_specs=vmem,
        compiler_params=params,
        name="layers",
    )(own, *others)

    arrived = lax.all_to_all(summed, "train", 0, 0, tiled=True)

    total = pl.pallas_call(
        functools.partial(place_kernel, train_size),
        out_shape=jax.ShapeDtypeStruct((rows * train_size, count), F32),
        in_specs=[vmem],
        out_specs=vmem,
        compiler_params=params,
        name="place",
    )(arrived)
    return total.reshape(rows, train_size, 1, count)


def solution(mesh):
    placed = (
        P("layer", ("parts", "train"), None),
        P("layer", ("parts", "train"), None),
        P("layer", None, None),
        P("layer", None, None),
        P("layer", None, None),
        P("layer", None, None),
        P("layer", None, None),
        P("layer", ("parts", "train", "sub"), None),
    )
    return jax.shard_map(
        body,
        mesh=mesh,
        in_specs=placed,
        out_specs=P(("parts", "train", "layer"), None, "sub", None),
        check_vma=False,
    )
```

```python
import functools

import jax
import jax.numpy as jnp
from jax import lax
from jax.experimental import pallas as pl
from jax.experimental.pallas import tpu as pltpu
from jax.sharding import PartitionSpec as P

F32 = jnp.float32
BF16 = jnp.bfloat16
PACK = 4


def nt(left, right):
    return lax.dot_general(left, right, (((1,), (1,)), ((), ())), preferred_element_type=F32)


def two_terms(matrix):
    high = matrix.astype(BF16)
    return jnp.concatenate([high, (matrix - high.astype(F32)).astype(BF16)], axis=1)


def block_diagonal(matrix):
    rank = matrix.shape[0]
    wide = jnp.concatenate([matrix] * PACK, axis=1)
    tall = jnp.concatenate([wide] * PACK, axis=0)
    rows = lax.broadcasted_iota(jnp.int32, tall.shape, 0) // rank
    columns = lax.broadcasted_iota(jnp.int32, tall.shape, 1) // rank
    return jnp.where(rows == columns, tall, 0.0)


def features_kernel(chunks, *refs):
    sources, feats, targets, sems = refs[:6], refs[6], refs[7:13], refs[13]
    inputs, grads, proj_in, proj_out, basis_in, basis_out = targets
    rank = basis_in.shape[0]
    step = inputs.shape[1] // chunks

    def copy(which, chunk):
        source, target = sources[which], targets[which]
        if which >= 4:
            return pltpu.make_async_copy(source.at[0], target, sems.at[which, 0])
        columns = pl.ds(chunk * step, step)
        return pltpu.make_async_copy(
            source.at[0, :, columns], target.at[:, columns], sems.at[which, chunk]
        )

    sides = ((0, 2, 4), (1, 3, 5))
    for side in sides:
        for chunk in range(chunks):
            copy(side[0], chunk).start()
            copy(side[1], chunk).start()
        copy(side[2], 0).start()
    for place, (tokens, proj, basis) in enumerate(sides):
        total = None
        for chunk in range(chunks):
            copy(tokens, chunk).wait()
            copy(proj, chunk).wait()
            columns = slice(chunk * step, (chunk + 1) * step)
            term = nt(targets[proj][:, columns], targets[tokens][:, columns])
            total = term if total is None else total + term
        copy(basis, 0).wait()
        turned = jnp.dot(
            two_terms(targets[basis][...].T),
            jnp.concatenate([total.astype(BF16)] * 2, axis=0),
            preferred_element_type=F32,
        )
        feats[place * rank:(place + 1) * rank, :] = turned.astype(BF16)


def score_block(feats, weights, rank):
    tokens = feats.shape[1]
    side_in = feats[:rank, :].astype(F32)
    side_out = feats[rank:, :].reshape(rank // 16, 16, tokens)
    total = None
    for part in range(rank // PACK):
        products = []
        for b in range(part * PACK, (part + 1) * PACK):
            row = jnp.broadcast_to(side_in[b:b + 1, :], (16, tokens)).astype(BF16)
            products.append((side_out * row[None]).reshape(rank, tokens))
        width = PACK * rank
        term = jnp.dot(
            weights[:, part * width:(part + 1) * width],
            jnp.concatenate(products, axis=0),
            preferred_element_type=F32,
        )
        total = term if total is None else total + term
    return total.T


def queries_kernel(queries, basis_in, basis_out, eigen, weights, half):
    rank = basis_in.shape[0]
    width = PACK * rank
    groups = rank // PACK
    right = block_diagonal(basis_in[...].T).astype(BF16)
    for part in range(groups):
        half[part * width:(part + 1) * width, :] = nt(
            right, queries[:, part * width:(part + 1) * width]
        )
    left = block_diagonal(basis_out[...]).astype(BF16)
    spectrum = eigen[...]
    inverse = (1.0 / (spectrum + 0.1 * jnp.mean(spectrum))).T
    for part in range(groups):
        columns = range(part * PACK, (part + 1) * PACK)
        matrix = jnp.concatenate(
            [half[pl.ds(b, rank, stride=rank), :] for b in columns], axis=0
        )
        turned = jnp.dot(matrix.T.astype(BF16), left, preferred_element_type=F32)
        scale = jnp.concatenate([inverse[b:b + 1, :] for b in columns], axis=1)
        weights[:, part * width:(part + 1) * width] = (turned * scale).astype(BF16)


def scores_kernel(layer_size, rank, groups, weights, *refs):
    feats = refs[:groups]
    own, away, scores = refs[-layer_size - 1], refs[-layer_size:-1], refs[-1]
    layer = lax.axis_index("layer")
    rows = own.shape[1]
    for i, feat in enumerate(feats):
        scores[...] = score_block(feat[...], weights, rank)
        for k, block in enumerate((own, *away)):
            first = pl.multiple_of(lax.rem(layer + k, layer_size) * rows, rows)
            block[i] = scores[pl.ds(first, rows), :].astype(block.dtype)


def layers_kernel(layer_size, groups, own, *refs):
    others, outs = refs[:layer_size - 1], refs[-groups:]
    for i, out in enumerate(outs):
        total = own[i]
        for other in others:
            total = total + other[i].astype(F32)
        out[...] = total.astype(BF16)


def place_kernel(train_size, layer_size, own, *refs):
    others, arrived, out = refs[:layer_size - 1], refs[layer_size - 1:-1], refs[-1]
    here = lax.axis_index("train")
    rows = own.shape[1]
    total = own[0]
    for other in others:
        total = total + other[0].astype(F32)
    out[pl.ds(here, rows, stride=train_size), :] = total
    for offset, block in enumerate(arrived, 1):
        out[pl.ds(here ^ offset, rows, stride=train_size), :] = block[...].astype(F32)


def body(inputs, out_grads, proj_in, proj_out, basis_in, basis_out, eigen, queries):
    train_size, layer_size = lax.axis_size("train"), lax.axis_size("layer")
    tokens, width = inputs.shape[1:]
    count, entries = queries.shape[1:]
    rank = proj_in.shape[1]
    chunks = 4
    vmem, hbm = pl.BlockSpec(memory_space=pltpu.VMEM), pl.BlockSpec(memory_space=pltpu.HBM)
    anywhere = pl.BlockSpec(memory_space=pl.ANY)
    params = pltpu.CompilerParams(vmem_limit_bytes=32 << 20)

    feats = pl.pallas_call(
        functools.partial(features_kernel, chunks),
        out_shape=jax.ShapeDtypeStruct((2 * rank, tokens), BF16),
        in_specs=[hbm] * 6,
        out_specs=vmem,
        scratch_shapes=[
            pltpu.VMEM((tokens, width), BF16),
            pltpu.VMEM((tokens, width), BF16),
            pltpu.VMEM((rank, width), BF16),
            pltpu.VMEM((rank, width), BF16),
            pltpu.VMEM((rank, rank), F32),
            pltpu.VMEM((rank, rank), F32),
            pltpu.SemaphoreType.DMA((6, chunks)),
        ],
        compiler_params=params,
        cost_estimate=pl.CostEstimate(
            flops=4 * tokens * rank * width, bytes_accessed=4 * width * (tokens + rank), transcendentals=0
        ),
        name="features",
    )(*[
        pltpu.with_memory_space_constraint(value, pltpu.HBM)
        for value in (inputs, out_grads, proj_in, proj_out, basis_in, basis_out)
    ])

    def exchange(value, offset):
        return lax.ppermute(value, "train", [(j, j ^ offset) for j in range(train_size)])

    gathered = [feats] + [exchange(feats, offset) for offset in range(1, train_size)]

    weights = pl.pallas_call(
        queries_kernel,
        out_shape=jax.ShapeDtypeStruct((count, entries), BF16),
        in_specs=[vmem] * 4,
        out_specs=vmem,
        scratch_shapes=[pltpu.VMEM((entries, count), F32)],
        compiler_params=params,
        cost_estimate=pl.CostEstimate(
            flops=4 * PACK * count * entries * rank, bytes_accessed=4 * count * entries, transcendentals=0
        ),
        name="queries",
    )(queries[0], basis_in[0], basis_out[0], eigen[0])

    rows = tokens // layer_size

    def scored(offsets, after):
        own, *away = pl.pallas_call(
            functools.partial(scores_kernel, layer_size, rank, len(offsets)),
            out_shape=[
                jax.ShapeDtypeStruct((len(offsets), rows, count), BF16 if k else F32)
                for k in range(layer_size)
            ],
            in_specs=[vmem] * (len(offsets) + 1) + [anywhere] * len(after),
            out_specs=[vmem] * layer_size,
            scratch_shapes=[pltpu.VMEM((tokens, count), F32)],
            compiler_params=params,
            cost_estimate=pl.CostEstimate(
                flops=2 * len(offsets) * tokens * entries * count,
                bytes_accessed=2 * count * entries,
                transcendentals=0,
            ),
            name="scores",
        )(weights, *[gathered[offset] for offset in offsets], *after)
        return own, [
            lax.ppermute(block, "layer", [(l, (l + k) % layer_size) for l in range(layer_size)])
            for k, block in enumerate(away, 1)
        ]

    half = train_size // 2
    far, near = range(train_size - 1, half - 1, -1), range(half - 1, 0, -1)
    own, others = scored([0], [])
    far_terms = scored(far, [own])
    near_terms = scored(near, [far_terms[0]])
    arrived = [None] * train_size
    after = []
    for offsets, (mine, theirs) in ((far, far_terms), (near, near_terms)):
        summed = pl.pallas_call(
            functools.partial(layers_kernel, layer_size, len(offsets)),
            out_shape=[jax.ShapeDtypeStruct((rows, count), BF16)] * len(offsets),
            in_specs=[vmem] * layer_size + [anywhere] * len(after),
            out_specs=[vmem] * len(offsets),
            compiler_params=params,
            name="layers",
        )(mine, *theirs, *after)
        after = summed[-1:]
        for offset, block in zip(offsets, summed):
            arrived[offset] = exchange(block, offset)

    total = pl.pallas_call(
        functools.partial(place_kernel, train_size, layer_size),
        out_shape=jax.ShapeDtypeStruct((rows * train_size, count), F32),
        in_specs=[vmem] * (layer_size + train_size - 1),
        out_specs=vmem,
        compiler_params=params,
        name="place",
    )(own, *others, *arrived[1:])
    return total.reshape(rows, train_size, 1, count)


def solution(mesh):
    placed = (
        P("layer", ("parts", "train"), None),
        P("layer", ("parts", "train"), None),
        P("layer", None, None),
        P("layer", None, None),
        P("layer", None, None),
        P("layer", None, None),
        P("layer", None, None),
        P("layer", ("parts", "train", "sub"), None),
    )
    return jax.shard_map(
        body,
        mesh=mesh,
        in_specs=placed,
        out_specs=P(("parts", "train", "layer"), None, "sub", None),
        check_vma=False,
    )
```

```python
import functools

import jax
import jax.numpy as jnp
from jax import lax
from jax.experimental import pallas as pl
from jax.experimental.pallas import tpu as pltpu
from jax.sharding import PartitionSpec as P

F32 = jnp.float32
BF16 = jnp.bfloat16
PACK = 4


def nt(left, right):
    return lax.dot_general(left, right, (((1,), (1,)), ((), ())), preferred_element_type=F32)


def two_terms(matrix):
    high = matrix.astype(BF16)
    return jnp.concatenate([high, (matrix - high.astype(F32)).astype(BF16)], axis=1)


def block_diagonal(matrix):
    rank = matrix.shape[0]
    wide = jnp.concatenate([matrix] * PACK, axis=1)
    tall = jnp.concatenate([wide] * PACK, axis=0)
    rows = lax.broadcasted_iota(jnp.int32, tall.shape, 0) // rank
    columns = lax.broadcasted_iota(jnp.int32, tall.shape, 1) // rank
    return jnp.where(rows == columns, tall, 0.0)


def features_kernel(chunks, *refs):
    sources, feats, targets, sems = refs[:6], refs[6], refs[7:13], refs[13]
    inputs, grads, proj_in, proj_out, basis_in, basis_out = targets
    rank = basis_in.shape[0]
    tokens, width = inputs.shape
    step = width // chunks
    first = pl.multiple_of(lax.axis_index("sub") * tokens, tokens)

    def copy(which, chunk):
        source, target = sources[which], targets[which]
        if which >= 4:
            return pltpu.make_async_copy(source.at[0], target, sems.at[which, 0])
        columns = pl.ds(chunk * step, step)
        rows = pl.ds(first, tokens) if which < 2 else slice(None)
        return pltpu.make_async_copy(
            source.at[0, rows, columns], target.at[:, columns], sems.at[which, chunk]
        )

    sides = ((0, 2, 4), (1, 3, 5))
    for side in sides:
        for chunk in range(chunks):
            copy(side[0], chunk).start()
            copy(side[1], chunk).start()
        copy(side[2], 0).start()
    for place, (rows, proj, basis) in enumerate(sides):
        total = None
        for chunk in range(chunks):
            copy(rows, chunk).wait()
            copy(proj, chunk).wait()
            columns = slice(chunk * step, (chunk + 1) * step)
            term = nt(targets[proj][:, columns], targets[rows][:, columns])
            total = term if total is None else total + term
        copy(basis, 0).wait()
        turned = jnp.dot(
            two_terms(targets[basis][...].T),
            jnp.concatenate([total.astype(BF16)] * 2, axis=0),
            preferred_element_type=F32,
        )
        feats[place * rank:(place + 1) * rank, :] = turned.astype(BF16)


def pack_kernel(*refs):
    for i, ref in enumerate(refs[:-2]):
        refs[-1][i] = ref[...]


def score_block(feats, weights, rank):
    tokens = feats.shape[1]
    side_in = feats[:rank, :].astype(F32)
    side_out = feats[rank:, :].reshape(rank // 16, 16, tokens)
    total = None
    for part in range(rank // PACK):
        products = []
        for b in range(part * PACK, (part + 1) * PACK):
            row = jnp.broadcast_to(side_in[b:b + 1, :], (16, tokens)).astype(BF16)
            products.append((side_out * row[None]).reshape(rank, tokens))
        width = PACK * rank
        term = jnp.dot(
            weights[:, part * width:(part + 1) * width],
            jnp.concatenate(products, axis=0),
            preferred_element_type=F32,
        )
        total = term if total is None else total + term
    return total.T


def queries_kernel(queries, basis_in, basis_out, eigen, weights, half):
    rank = basis_in.shape[0]
    width = PACK * rank
    groups = rank // PACK
    right = block_diagonal(basis_in[...].T).astype(BF16)
    for part in range(groups):
        half[part * width:(part + 1) * width, :] = nt(
            right, queries[:, part * width:(part + 1) * width]
        )
    left = block_diagonal(basis_out[...]).astype(BF16)
    spectrum = eigen[...]
    inverse = (1.0 / (spectrum + 0.1 * jnp.mean(spectrum))).T
    for part in range(groups):
        columns = range(part * PACK, (part + 1) * PACK)
        matrix = jnp.concatenate(
            [half[pl.ds(b, rank, stride=rank), :] for b in columns], axis=0
        )
        turned = jnp.dot(matrix.T.astype(BF16), left, preferred_element_type=F32)
        scale = jnp.concatenate([inverse[b:b + 1, :] for b in columns], axis=1)
        weights[:, part * width:(part + 1) * width] = (turned * scale).astype(BF16)


def scores_kernel(layer_size, rank, offsets, weights, mine, theirs, *refs):
    own, away, scores = refs[-layer_size - 1], refs[-layer_size:-1], refs[-1]
    layer, core = lax.axis_index("layer"), lax.axis_index("sub")
    rows, half = own.shape[1], mine.shape[2]
    for i, offset in enumerate(offsets):
        feats = jnp.concatenate([mine[offset], theirs[offset]], axis=1)
        scores[...] = score_block(feats, weights, rank)
        for k, block in enumerate((own, *away)):
            first = lax.rem(lax.rem(layer + k, layer_size) * rows + core * half, 2 * half)
            block[i] = scores[pl.ds(pl.multiple_of(first, rows), rows), :].astype(block.dtype)


def layers_kernel(layer_size, groups, own, *refs):
    others, outs = refs[:layer_size - 1], refs[-groups:]
    for i, out in enumerate(outs):
        total = own[i]
        for other in others:
            total = total + other[i].astype(F32)
        out[...] = total.astype(out.dtype)


def place_kernel(train_size, *refs):
    arrived, out = refs[:-1], refs[-1]
    here = lax.axis_index("train")
    for offset, block in enumerate(arrived):
        out[pl.ds(here ^ offset, block.shape[0], stride=train_size), :] = block[...].astype(F32)


def body(inputs, out_grads, proj_in, proj_out, basis_in, basis_out, eigen, queries):
    train_size, layer_size = lax.axis_size("train"), lax.axis_size("layer")
    tokens, width = inputs.shape[1:]
    count, entries = queries.shape[1:]
    rank = proj_in.shape[1]
    half = tokens // 2
    chunks = 4
    vmem, hbm = pl.BlockSpec(memory_space=pltpu.VMEM), pl.BlockSpec(memory_space=pltpu.HBM)
    anywhere = pl.BlockSpec(memory_space=pl.ANY)
    params = pltpu.CompilerParams(vmem_limit_bytes=32 << 20)

    feats = pl.pallas_call(
        functools.partial(features_kernel, chunks),
        out_shape=jax.ShapeDtypeStruct((2 * rank, half), BF16),
        in_specs=[hbm] * 6,
        out_specs=vmem,
        scratch_shapes=[
            pltpu.VMEM((half, width), BF16),
            pltpu.VMEM((half, width), BF16),
            pltpu.VMEM((rank, width), BF16),
            pltpu.VMEM((rank, width), BF16),
            pltpu.VMEM((rank, rank), F32),
            pltpu.VMEM((rank, rank), F32),
            pltpu.SemaphoreType.DMA((6, chunks)),
        ],
        compiler_params=params,
        cost_estimate=pl.CostEstimate(
            flops=4 * half * rank * width, bytes_accessed=4 * width * (half + rank), transcendentals=0
        ),
        name="features",
    )(*[
        pltpu.with_memory_space_constraint(value, pltpu.HBM)
        for value in (inputs, out_grads, proj_in, proj_out, basis_in, basis_out)
    ])

    def exchange(value, offset):
        return lax.ppermute(value, "train", [(j, j ^ offset) for j in range(train_size)])

    gathered = [feats] + [exchange(feats, offset) for offset in range(1, train_size)]

    weights = pl.pallas_call(
        queries_kernel,
        out_shape=jax.ShapeDtypeStruct((count, entries), BF16),
        in_specs=[vmem] * 4,
        out_specs=vmem,
        scratch_shapes=[pltpu.VMEM((entries, count), F32)],
        compiler_params=params,
        cost_estimate=pl.CostEstimate(
            flops=4 * PACK * count * entries * rank, bytes_accessed=4 * count * entries, transcendentals=0
        ),
        name="queries",
    )(queries[0], basis_in[0], basis_out[0], eigen[0])

    mine = pl.pallas_call(
        pack_kernel,
        out_shape=jax.ShapeDtypeStruct((train_size, 2 * rank, half), BF16),
        in_specs=[vmem] * train_size + [anywhere],
        out_specs=vmem,
        compiler_params=params,
        name="pack",
    )(*gathered, weights)
    theirs = lax.ppermute(mine, "sub", [(0, 1), (1, 0)])

    rows = tokens // layer_size

    def scored(offsets, after):
        own, *away = pl.pallas_call(
            functools.partial(scores_kernel, layer_size, rank, offsets),
            out_shape=[
                jax.ShapeDtypeStruct((len(offsets), rows, count), BF16 if k else F32)
                for k in range(layer_size)
            ],
            in_specs=[vmem] * 3 + [anywhere] * len(after),
            out_specs=[vmem] * layer_size,
            scratch_shapes=[pltpu.VMEM((tokens, count), F32)],
            compiler_params=params,
            cost_estimate=pl.CostEstimate(
                flops=2 * len(offsets) * tokens * entries * count,
                bytes_accessed=2 * count * entries,
                transcendentals=0,
            ),
            name="scores",
        )(weights, mine, theirs, *after)
        return own, [
            lax.ppermute(block, "layer", [(l, (l + k) % layer_size) for l in range(layer_size)])
            for k, block in enumerate(away, 1)
        ]

    def summed(offsets, own, others, after):
        return pl.pallas_call(
            functools.partial(layers_kernel, layer_size, len(offsets)),
            out_shape=[jax.ShapeDtypeStruct((rows, count), BF16 if offset else F32) for offset in offsets],
            in_specs=[vmem] * layer_size + [anywhere] * len(after),
            out_specs=[vmem] * len(offsets),
            compiler_params=params,
            name="layers",
        )(own, *others, *after)

    far = tuple(range(train_size - 1, train_size // 2 - 1, -1))
    near = tuple(range(train_size // 2 - 1, -1, -1))
    far_terms = scored(far, [])
    near_terms = scored(near, far_terms[:1])
    far_sums = summed(far, *far_terms, [])
    near_sums = summed(near, *near_terms, far_sums[:1])
    arrived = {
        offset: exchange(block, offset) if offset else block
        for offset, block in (*zip(far, far_sums), *zip(near, near_sums))
    }

    total = pl.pallas_call(
        functools.partial(place_kernel, train_size),
        out_shape=jax.ShapeDtypeStruct((rows * train_size, count), F32),
        in_specs=[vmem] * train_size,
        out_specs=vmem,
        compiler_params=params,
        name="place",
    )(*[arrived[offset] for offset in range(train_size)])
    return total.reshape(rows, train_size, 1, count)


def solution(mesh):
    placed = (
        P("layer", ("parts", "train"), None),
        P("layer", ("parts", "train"), None),
        P("layer", None, None),
        P("layer", None, None),
        P("layer", None, None),
        P("layer", None, None),
        P("layer", None, None),
        P("layer", ("parts", "train", "sub"), None),
    )
    return jax.shard_map(
        body,
        mesh=mesh,
        in_specs=placed,
        out_specs=P(("parts", "train", "layer"), None, "sub", None),
        check_vma=False,
    )
```

```python
import functools

import jax
import jax.numpy as jnp
from jax import lax
from jax.experimental import pallas as pl
from jax.experimental.pallas import tpu as pltpu
from jax.sharding import PartitionSpec as P

F32 = jnp.float32
BF16 = jnp.bfloat16
PACK = 4


def nt(left, right):
    return lax.dot_general(left, right, (((1,), (1,)), ((), ())), preferred_element_type=F32)


def two_terms(matrix):
    high = matrix.astype(BF16)
    return jnp.concatenate([high, (matrix - high.astype(F32)).astype(BF16)], axis=1)


def block_diagonal(matrix):
    rank = matrix.shape[0]
    wide = jnp.concatenate([matrix] * PACK, axis=1)
    tall = jnp.concatenate([wide] * PACK, axis=0)
    rows = lax.broadcasted_iota(jnp.int32, tall.shape, 0) // rank
    columns = lax.broadcasted_iota(jnp.int32, tall.shape, 1) // rank
    return jnp.where(rows == columns, tall, 0.0)


def features_kernel(chunks, *refs):
    sources, feats, targets, sems = refs[:6], refs[6], refs[7:13], refs[13]
    tokens, width = targets[0].shape
    rank = targets[2].shape[0]
    step = width // chunks
    first = pl.multiple_of(lax.axis_index("sub") * tokens, tokens)

    def copy(which, chunk=None):
        source, target = sources[which].at[0], targets[which]
        if chunk is None:
            return pltpu.make_async_copy(source, target, sems.at[which, 0])
        columns = pl.ds(chunk * step, step)
        return pltpu.make_async_copy(
            source.at[pl.ds(first, tokens), columns], target.at[:, columns], sems.at[which, chunk]
        )

    sides = ((0, 2, 4), (1, 3, 5))
    for rows, proj, basis in sides:
        copy(proj).start()
        for chunk in range(chunks):
            copy(rows, chunk).start()
        copy(basis).start()
    for place, (rows, proj, basis) in enumerate(sides):
        copy(proj).wait()
        total = None
        for chunk in range(chunks):
            copy(rows, chunk).wait()
            columns = slice(chunk * step, (chunk + 1) * step)
            term = nt(targets[proj][:, columns], targets[rows][:, columns])
            total = term if total is None else total + term
        copy(basis).wait()
        turned = jnp.dot(
            two_terms(targets[basis][...].T),
            jnp.concatenate([total.astype(BF16)] * 2, axis=0),
            preferred_element_type=F32,
        )
        feats[place * rank:(place + 1) * rank, :] = turned.astype(BF16)


def pack_kernel(order, *refs):
    for offset, ref in zip(order, refs):
        refs[-1][offset] = ref[...]


def score_block(feats, weights, rank):
    tokens = feats.shape[1]
    side_in = feats[:rank, :].astype(F32)
    side_out = feats[rank:, :].reshape(rank // 16, 16, tokens)
    total = None
    for part in range(rank // PACK):
        products = []
        for b in range(part * PACK, (part + 1) * PACK):
            row = jnp.broadcast_to(side_in[b:b + 1, :], (16, tokens)).astype(BF16)
            products.append((side_out * row[None]).reshape(rank, tokens))
        width = PACK * rank
        term = jnp.dot(
            weights[:, part * width:(part + 1) * width],
            jnp.concatenate(products, axis=0),
            preferred_element_type=F32,
        )
        total = term if total is None else total + term
    return total.T


def queries_kernel(queries, basis_in, basis_out, eigen, weights, half):
    rank = basis_in.shape[0]
    width = PACK * rank
    groups = rank // PACK
    right = block_diagonal(basis_in[...].T).astype(BF16)
    for part in range(groups):
        half[part * width:(part + 1) * width, :] = nt(
            right, queries[:, part * width:(part + 1) * width]
        )
    left = block_diagonal(basis_out[...]).astype(BF16)
    spectrum = eigen[...]
    inverse = (1.0 / (spectrum + 0.1 * jnp.mean(spectrum))).T
    for part in range(groups):
        columns = range(part * PACK, (part + 1) * PACK)
        matrix = jnp.concatenate(
            [half[pl.ds(b, rank, stride=rank), :] for b in columns], axis=0
        )
        turned = jnp.dot(matrix.T.astype(BF16), left, preferred_element_type=F32)
        scale = jnp.concatenate([inverse[b:b + 1, :] for b in columns], axis=1)
        weights[:, part * width:(part + 1) * width] = (turned * scale).astype(BF16)


def scores_kernel(layer_size, rank, offsets, weights, mine, theirs, *refs):
    own, away, scores = refs[-layer_size - 1], refs[-layer_size:-1], refs[-1]
    layer, core = lax.axis_index("layer"), lax.axis_index("sub")
    rows, half = own.shape[1], mine.shape[2]
    for i, offset in enumerate(offsets):
        feats = jnp.concatenate([mine[offset], theirs[offset]], axis=1)
        scores[...] = score_block(feats, weights, rank)
        for k, block in enumerate((own, *away)):
            first = lax.rem(lax.rem(layer + k, layer_size) * rows + core * half, 2 * half)
            block[i] = scores[pl.ds(pl.multiple_of(first, rows), rows), :].astype(block.dtype)


def layers_kernel(layer_size, which, own, *refs):
    total = own[which]
    for other in refs[:layer_size - 1]:
        total = total + other[which].astype(F32)
    refs[-1][...] = total.astype(refs[-1].dtype)


def place_kernel(train_size, *refs):
    arrived, out = refs[:-1], refs[-1]
    here = lax.axis_index("train")
    for offset, block in enumerate(reversed(arrived)):
        out[pl.ds(here ^ offset, block.shape[0], stride=train_size), :] = block[...].astype(F32)


def body(inputs, out_grads, proj_in, proj_out, basis_in, basis_out, eigen, queries):
    train_size, layer_size = lax.axis_size("train"), lax.axis_size("layer")
    tokens, width = inputs.shape[1:]
    count, entries = queries.shape[1:]
    rank = proj_in.shape[1]
    half = tokens // 2
    chunks = 2
    vmem, hbm = pl.BlockSpec(memory_space=pltpu.VMEM), pl.BlockSpec(memory_space=pltpu.HBM)
    anywhere = pl.BlockSpec(memory_space=pl.ANY)
    params = pltpu.CompilerParams(vmem_limit_bytes=32 << 20)

    feats = pl.pallas_call(
        functools.partial(features_kernel, chunks),
        out_shape=jax.ShapeDtypeStruct((2 * rank, half), BF16),
        in_specs=[hbm] * 6,
        out_specs=vmem,
        scratch_shapes=[
            pltpu.VMEM((half, width), BF16),
            pltpu.VMEM((half, width), BF16),
            pltpu.VMEM((rank, width), BF16),
            pltpu.VMEM((rank, width), BF16),
            pltpu.VMEM((rank, rank), F32),
            pltpu.VMEM((rank, rank), F32),
            pltpu.SemaphoreType.DMA((6, chunks)),
        ],
        compiler_params=params,
        cost_estimate=pl.CostEstimate(
            flops=4 * half * rank * width, bytes_accessed=4 * width * (half + rank), transcendentals=0
        ),
        name="features",
    )(*[
        pltpu.with_memory_space_constraint(value, pltpu.HBM)
        for value in (inputs, out_grads, proj_in, proj_out, basis_in, basis_out)
    ])

    def exchange(value, offset):
        return lax.ppermute(value, "train", [(j, j ^ offset) for j in range(train_size)])

    middle = train_size // 2
    order = (0, *range(1, middle), *range(train_size - 1, middle - 1, -1))
    gathered = [exchange(feats, offset) if offset else feats for offset in order]

    weights = pl.pallas_call(
        queries_kernel,
        out_shape=jax.ShapeDtypeStruct((count, entries), BF16),
        in_specs=[vmem] * 4,
        out_specs=vmem,
        scratch_shapes=[pltpu.VMEM((entries, count), F32)],
        compiler_params=params,
        cost_estimate=pl.CostEstimate(
            flops=4 * PACK * count * entries * rank, bytes_accessed=4 * count * entries, transcendentals=0
        ),
        name="queries",
    )(queries[0], basis_in[0], basis_out[0], eigen[0])

    mine = pl.pallas_call(
        functools.partial(pack_kernel, order),
        out_shape=jax.ShapeDtypeStruct((train_size, 2 * rank, half), BF16),
        in_specs=[vmem] * train_size + [anywhere],
        out_specs=vmem,
        compiler_params=params,
        name="pack",
    )(*gathered, weights)
    theirs = lax.ppermute(mine, "sub", [(0, 1), (1, 0)])

    rows = tokens // layer_size

    def scored(offsets, after):
        own, *away = pl.pallas_call(
            functools.partial(scores_kernel, layer_size, rank, offsets),
            out_shape=[
                jax.ShapeDtypeStruct((len(offsets), rows, count), BF16 if k else F32)
                for k in range(layer_size)
            ],
            in_specs=[vmem] * 3 + [anywhere] * len(after),
            out_specs=[vmem] * layer_size,
            scratch_shapes=[pltpu.VMEM((tokens, count), F32)],
            compiler_params=params,
            cost_estimate=pl.CostEstimate(
                flops=2 * len(offsets) * tokens * entries * count,
                bytes_accessed=2 * count * entries,
                transcendentals=0,
            ),
            name="scores",
        )(weights, mine, theirs, *after)
        return own, [
            lax.ppermute(block, "layer", [(l, (l + k) % layer_size) for l in range(layer_size)])
            for k, block in enumerate(away, 1)
        ]

    def summed(which, offset, own, others, after):
        return pl.pallas_call(
            functools.partial(layers_kernel, layer_size, which),
            out_shape=jax.ShapeDtypeStruct((rows, count), BF16 if offset else F32),
            in_specs=[vmem] * layer_size + [anywhere] * len(after),
            out_specs=vmem,
            compiler_params=params,
            name="layers",
        )(own, *others, *after)

    far, near = tuple(range(train_size - 1, middle - 1, -1)), tuple(range(middle))
    far_terms = scored(far, [])
    near_terms = scored(near, far_terms[:1])
    arrived, after = {}, []
    for offsets, terms in ((far, far_terms), (near, near_terms)):
        for which, offset in enumerate(offsets):
            block = summed(which, offset, *terms, after)
            after = [block]
            arrived[offset] = exchange(block, offset) if offset else block

    total = pl.pallas_call(
        functools.partial(place_kernel, train_size),
        out_shape=jax.ShapeDtypeStruct((rows * train_size, count), F32),
        in_specs=[vmem] * train_size,
        out_specs=vmem,
        compiler_params=params,
        name="place",
    )(*[arrived[offset] for offset in reversed(range(train_size))])
    return total.reshape(rows, train_size, 1, count)


def solution(mesh):
    placed = (
        P("layer", ("parts", "train"), None),
        P("layer", ("parts", "train"), None),
        P("layer", None, None),
        P("layer", None, None),
        P("layer", None, None),
        P("layer", None, None),
        P("layer", None, None),
        P("layer", ("parts", "train", "sub"), None),
    )
    return jax.shard_map(
        body,
        mesh=mesh,
        in_specs=placed,
        out_specs=P(("parts", "train", "layer"), None, "sub", None),
        check_vma=False,
    )
```

```python
import functools

import jax
import jax.numpy as jnp
from jax import lax
from jax.experimental import pallas as pl
from jax.experimental.pallas import tpu as pltpu
from jax.sharding import PartitionSpec as P

F32 = jnp.float32
BF16 = jnp.bfloat16
PACK = 4


def nt(left, right):
    return lax.dot_general(left, right, (((1,), (1,)), ((), ())), preferred_element_type=F32)


def two_terms(matrix):
    high = matrix.astype(BF16)
    return jnp.concatenate([high, (matrix - high.astype(F32)).astype(BF16)], axis=1)


def block_diagonal(matrix):
    rank = matrix.shape[0]
    wide = jnp.concatenate([matrix] * PACK, axis=1)
    tall = jnp.concatenate([wide] * PACK, axis=0)
    rows = lax.broadcasted_iota(jnp.int32, tall.shape, 0) // rank
    columns = lax.broadcasted_iota(jnp.int32, tall.shape, 1) // rank
    return jnp.where(rows == columns, tall, 0.0)


def features_kernel(chunks, *refs):
    sources, feats, (queries, eigen, basis_in, basis_out) = refs[:8], refs[8], refs[9:13]
    targets = (*refs[13:17], basis_in, basis_out, queries, eigen)
    sems = refs[17]
    tokens, width = targets[0].shape
    rank = targets[2].shape[0]
    step = width // chunks
    first = pl.multiple_of(lax.axis_index("sub") * tokens, tokens)

    def copy(which, chunk=None):
        source, target = sources[which].at[0], targets[which]
        if chunk is None:
            return pltpu.make_async_copy(source, target, sems.at[which, 0])
        columns = pl.ds(chunk * step, step)
        return pltpu.make_async_copy(
            source.at[pl.ds(first, tokens), columns], target.at[:, columns], sems.at[which, chunk]
        )

    sides = ((0, 2, 4), (1, 3, 5))
    for rows, proj, basis in sides:
        copy(proj).start()
        for chunk in range(chunks):
            copy(rows, chunk).start()
        copy(basis).start()
    for which in (6, 7):
        copy(which).start()
    for place, (rows, proj, basis) in enumerate(sides):
        copy(proj).wait()
        total = None
        for chunk in range(chunks):
            copy(rows, chunk).wait()
            columns = slice(chunk * step, (chunk + 1) * step)
            term = nt(targets[proj][:, columns], targets[rows][:, columns])
            total = term if total is None else total + term
        copy(basis).wait()
        turned = jnp.dot(
            two_terms(targets[basis][...].T),
            jnp.concatenate([total.astype(BF16)] * 2, axis=0),
            preferred_element_type=F32,
        )
        feats[place * rank:(place + 1) * rank, :] = turned.astype(BF16)
    for which in (6, 7):
        copy(which).wait()


def pack_kernel(count, *refs):
    for i, ref in enumerate(refs[:count]):
        refs[-1][i] = ref[...]


def score_block(feats, weights, rank):
    tokens = feats.shape[1]
    side_in = feats[:rank, :].astype(F32)
    side_out = feats[rank:, :].reshape(rank // 16, 16, tokens)
    total = None
    for part in range(rank // PACK):
        products = []
        for b in range(part * PACK, (part + 1) * PACK):
            row = jnp.broadcast_to(side_in[b:b + 1, :], (16, tokens)).astype(BF16)
            products.append((side_out * row[None]).reshape(rank, tokens))
        width = PACK * rank
        term = jnp.dot(
            weights[:, part * width:(part + 1) * width],
            jnp.concatenate(products, axis=0),
            preferred_element_type=F32,
        )
        total = term if total is None else total + term
    return total.T


def queries_kernel(queries, basis_in, basis_out, eigen, *refs):
    weights, half = refs[-2:]
    rank = basis_in.shape[0]
    width = PACK * rank
    groups = rank // PACK
    right = block_diagonal(basis_in[...].T).astype(BF16)
    for part in range(groups):
        half[part * width:(part + 1) * width, :] = nt(
            right, queries[:, part * width:(part + 1) * width]
        )
    left = block_diagonal(basis_out[...]).astype(BF16)
    spectrum = eigen[...]
    inverse = (1.0 / (spectrum + 0.1 * jnp.mean(spectrum))).T
    for part in range(groups):
        columns = range(part * PACK, (part + 1) * PACK)
        matrix = jnp.concatenate(
            [half[pl.ds(b, rank, stride=rank), :] for b in columns], axis=0
        )
        turned = jnp.dot(matrix.T.astype(BF16), left, preferred_element_type=F32)
        scale = jnp.concatenate([inverse[b:b + 1, :] for b in columns], axis=1)
        weights[:, part * width:(part + 1) * width] = (turned * scale).astype(BF16)


def scores_kernel(layer_size, rank, offsets, places, weights, *refs):
    own, away, scores = refs[-layer_size - 1], refs[-layer_size:-1], refs[-1]
    layer, core = lax.axis_index("layer"), lax.axis_index("sub")
    rows, half = own.shape[1], refs[0].shape[2]
    for i, (offset, (pair, place)) in enumerate(zip(offsets, places)):
        feats = jnp.concatenate([refs[2 * pair][place], refs[2 * pair + 1][place]], axis=1)
        scores[...] = score_block(feats, weights, rank)
        held = 1 - core if offset else core
        for k, block in enumerate((own, *away)):
            first = lax.rem(lax.rem(layer + k, layer_size) * rows + held * half, 2 * half)
            block[i] = scores[pl.ds(pl.multiple_of(first, rows), rows), :].astype(block.dtype)


def layers_kernel(layer_size, which, own, *refs):
    total = own[which]
    for other in refs[:layer_size - 1]:
        total = total + other[which].astype(F32)
    refs[-1][...] = total.astype(refs[-1].dtype)


def place_kernel(train_size, *refs):
    arrived, out = refs[:-1], refs[-1]
    here = lax.axis_index("train")
    for offset, block in enumerate(reversed(arrived)):
        out[pl.ds(here ^ offset, block.shape[0], stride=train_size), :] = block[...].astype(F32)


def body(inputs, out_grads, proj_in, proj_out, basis_in, basis_out, eigen, queries):
    train_size, layer_size = lax.axis_size("train"), lax.axis_size("layer")
    tokens, width = inputs.shape[1:]
    count, entries = queries.shape[1:]
    rank = proj_in.shape[1]
    half = tokens // 2
    chunks = 2
    vmem, hbm = pl.BlockSpec(memory_space=pltpu.VMEM), pl.BlockSpec(memory_space=pltpu.HBM)
    anywhere = pl.BlockSpec(memory_space=pl.ANY)
    params = pltpu.CompilerParams(vmem_limit_bytes=32 << 20)

    sources = (inputs, out_grads, proj_in, proj_out, basis_in, basis_out, queries, eigen)
    feats, queries, eigen, basis_in, basis_out = pl.pallas_call(
        functools.partial(features_kernel, chunks),
        out_shape=[
            jax.ShapeDtypeStruct((2 * rank, half), BF16),
            jax.ShapeDtypeStruct((count, entries), BF16),
            *[jax.ShapeDtypeStruct((rank, rank), F32)] * 3,
        ],
        in_specs=[hbm] * len(sources),
        out_specs=[vmem] * 5,
        scratch_shapes=[
            pltpu.VMEM((half, width), BF16),
            pltpu.VMEM((half, width), BF16),
            pltpu.VMEM((rank, width), BF16),
            pltpu.VMEM((rank, width), BF16),
            pltpu.SemaphoreType.DMA((len(sources), chunks)),
        ],
        compiler_params=params,
        cost_estimate=pl.CostEstimate(
            flops=4 * half * rank * width, bytes_accessed=4 * width * (half + rank), transcendentals=0
        ),
        name="features",
    )(*[pltpu.with_memory_space_constraint(value, pltpu.HBM) for value in sources])

    def exchange(value, offset):
        return lax.ppermute(value, "train", [(j, j ^ offset) for j in range(train_size)])

    def exchange_across(value, offset):
        pairs = [(2 * j + s, 2 * (j ^ offset) + 1 - s) for j in range(train_size) for s in range(2)]
        return lax.ppermute(value, ("train", "sub"), pairs)

    middle = train_size // 2
    far, near = tuple(range(train_size - 1, middle - 1, -1)), tuple(range(middle))
    gathered = {offset: exchange_across(feats, offset) for offset in range(train_size - 1, 0, -1)}
    gathered[0] = feats

    halves = {}
    weights = pl.pallas_call(
        queries_kernel,
        out_shape=jax.ShapeDtypeStruct((count, entries), BF16),
        in_specs=[vmem] * 4,
        out_specs=vmem,
        scratch_shapes=[pltpu.VMEM((entries, count), F32)],
        compiler_params=params,
        cost_estimate=pl.CostEstimate(
            flops=4 * PACK * count * entries * rank, bytes_accessed=4 * count * entries, transcendentals=0
        ),
        name="queries",
    )(queries, basis_in, basis_out, eigen)

    def swapped(offsets, after):
        mine = pl.pallas_call(
            functools.partial(pack_kernel, len(offsets)),
            out_shape=jax.ShapeDtypeStruct((len(offsets), 2 * rank, half), BF16),
            in_specs=[vmem] * len(offsets) + [anywhere] * len(after),
            out_specs=vmem,
            compiler_params=params,
            name="pack",
        )(*[gathered[offset] for offset in offsets], *after)
        theirs = lax.ppermute(mine, "sub", [(0, 1), (1, 0)])
        halves.update({offset: (mine, theirs, place) for place, offset in enumerate(offsets)})

    for offsets in ((*near, *far),):
        swapped(offsets, [weights])

    rows = tokens // layer_size

    def scored(offsets, after):
        pairs = list({id(halves[offset][0]): halves[offset][:2] for offset in offsets}.values())
        places = [
            (next(i for i, pair in enumerate(pairs) if pair[0] is halves[offset][0]), halves[offset][2])
            for offset in offsets
        ]
        own, *away = pl.pallas_call(
            functools.partial(scores_kernel, layer_size, rank, offsets, places),
            out_shape=[
                jax.ShapeDtypeStruct((len(offsets), rows, count), BF16 if k else F32)
                for k in range(layer_size)
            ],
            in_specs=[vmem] * (1 + 2 * len(pairs)) + [anywhere] * len(after),
            out_specs=[vmem] * layer_size,
            scratch_shapes=[pltpu.VMEM((tokens, count), F32)],
            compiler_params=params,
            cost_estimate=pl.CostEstimate(
                flops=2 * len(offsets) * tokens * entries * count,
                bytes_accessed=2 * count * entries,
                transcendentals=0,
            ),
            name="scores",
        )(weights, *[half for pair in pairs for half in pair], *after)
        return own, [
            lax.ppermute(block, "layer", [(l, (l + k) % layer_size) for l in range(layer_size)])
            for k, block in enumerate(away, 1)
        ]

    def summed(which, offset, own, others, after):
        return pl.pallas_call(
            functools.partial(layers_kernel, layer_size, which),
            out_shape=jax.ShapeDtypeStruct((rows, count), BF16 if offset else F32),
            in_specs=[vmem] * layer_size + [anywhere] * len(after),
            out_specs=vmem,
            compiler_params=params,
            name="layers",
        )(own, *others, *after)

    terms, after = {}, []
    for offsets in (far, near):
        own, others = scored(offsets, after)
        terms.update({offset: (which, offset, own, others) for which, offset in enumerate(offsets)})
        after = [own]
    arrived, after = {}, []
    for offset in (*far, *near):
        block = summed(*terms[offset], after)
        after = [block]
        arrived[offset] = exchange(block, offset) if offset else block

    total = pl.pallas_call(
        functools.partial(place_kernel, train_size),
        out_shape=jax.ShapeDtypeStruct((rows * train_size, count), F32),
        in_specs=[vmem] * train_size,
        out_specs=vmem,
        compiler_params=params,
        name="place",
    )(*[arrived[offset] for offset in reversed(range(train_size))])
    return total.reshape(rows, train_size, 1, count)


def solution(mesh):
    placed = (
        P("layer", ("parts", "train"), None),
        P("layer", ("parts", "train"), None),
        P("layer", None, None),
        P("layer", None, None),
        P("layer", None, None),
        P("layer", None, None),
        P("layer", None, None),
        P("layer", ("parts", "train", "sub"), None),
    )
    return jax.shard_map(
        body,
        mesh=mesh,
        in_specs=placed,
        out_specs=P(("parts", "train", "layer"), None, "sub", None),
        check_vma=False,
    )
```

```python
import functools

import jax
import jax.numpy as jnp
from jax import lax
from jax.experimental import pallas as pl
from jax.experimental.pallas import tpu as pltpu
from jax.sharding import PartitionSpec as P

F32 = jnp.float32
BF16 = jnp.bfloat16
PACK = 4


def nt(left, right):
    return lax.dot_general(left, right, (((1,), (1,)), ((), ())), preferred_element_type=F32)


def two_terms(matrix):
    high = matrix.astype(BF16)
    return jnp.concatenate([high, (matrix - high.astype(F32)).astype(BF16)], axis=1)


def block_diagonal(matrix):
    rank = matrix.shape[0]
    wide = jnp.concatenate([matrix] * PACK, axis=1)
    tall = jnp.concatenate([wide] * PACK, axis=0)
    rows = lax.broadcasted_iota(jnp.int32, tall.shape, 0) // rank
    columns = lax.broadcasted_iota(jnp.int32, tall.shape, 1) // rank
    return jnp.where(rows == columns, tall, 0.0)


def features_kernel(chunks, *refs):
    sources, feats, (queries, eigen, basis_in, basis_out) = refs[:8], refs[8], refs[9:13]
    targets = (*refs[13:17], basis_in, basis_out, queries, eigen)
    sems = refs[17]
    tokens, width = targets[0].shape
    rank = targets[2].shape[0]
    step = width // chunks
    first = pl.multiple_of(lax.axis_index("sub") * tokens, tokens)

    def copy(which, chunk=None):
        source, target = sources[which].at[0], targets[which]
        if chunk is None:
            return pltpu.make_async_copy(source, target, sems.at[which, 0])
        columns = pl.ds(chunk * step, step)
        return pltpu.make_async_copy(
            source.at[pl.ds(first, tokens), columns], target.at[:, columns], sems.at[which, chunk]
        )

    sides = ((0, 2, 4), (1, 3, 5))
    for rows, proj, basis in sides:
        copy(proj).start()
        for chunk in range(chunks):
            copy(rows, chunk).start()
        copy(basis).start()
    for which in (6, 7):
        copy(which).start()
    for place, (rows, proj, basis) in enumerate(sides):
        copy(proj).wait()
        total = None
        for chunk in range(chunks):
            copy(rows, chunk).wait()
            columns = slice(chunk * step, (chunk + 1) * step)
            term = nt(targets[proj][:, columns], targets[rows][:, columns])
            total = term if total is None else total + term
        copy(basis).wait()
        turned = jnp.dot(
            two_terms(targets[basis][...].T),
            jnp.concatenate([total.astype(BF16)] * 2, axis=0),
            preferred_element_type=F32,
        )
        feats[place * rank:(place + 1) * rank, :] = turned.astype(BF16)
    for which in (6, 7):
        copy(which).wait()


def pack_kernel(count, *refs):
    for i, ref in enumerate(refs[:count]):
        refs[-1][i] = ref[...]


def score_block(feats, weights, rank):
    tokens = feats.shape[1]
    side_in = feats[:rank, :].astype(F32)
    side_out = feats[rank:, :].reshape(rank // 16, 16, tokens)
    total = None
    for part in range(rank // PACK):
        products = []
        for b in range(part * PACK, (part + 1) * PACK):
            row = jnp.broadcast_to(side_in[b:b + 1, :], (16, tokens)).astype(BF16)
            products.append((side_out * row[None]).reshape(rank, tokens))
        width = PACK * rank
        term = jnp.dot(
            weights[:, part * width:(part + 1) * width],
            jnp.concatenate(products, axis=0),
            preferred_element_type=F32,
        )
        total = term if total is None else total + term
    return total.T


def queries_kernel(queries, basis_in, basis_out, eigen, *refs):
    weights, half = refs[-2:]
    rank = basis_in.shape[0]
    width = PACK * rank
    groups = rank // PACK
    right = block_diagonal(basis_in[...].T).astype(BF16)
    for part in range(groups):
        half[part * width:(part + 1) * width, :] = nt(
            right, queries[:, part * width:(part + 1) * width]
        )
    left = block_diagonal(basis_out[...]).astype(BF16)
    spectrum = eigen[...]
    inverse = (1.0 / (spectrum + 0.1 * jnp.mean(spectrum))).T
    for part in range(groups):
        columns = range(part * PACK, (part + 1) * PACK)
        matrix = jnp.concatenate(
            [half[pl.ds(b, rank, stride=rank), :] for b in columns], axis=0
        )
        turned = jnp.dot(matrix.T.astype(BF16), left, preferred_element_type=F32)
        scale = jnp.concatenate([inverse[b:b + 1, :] for b in columns], axis=1)
        weights[:, part * width:(part + 1) * width] = (turned * scale).astype(BF16)


def scores_kernel(layer_size, rank, offsets, places, weights, mine, theirs, *refs):
    own, away, scores = refs[-layer_size - 1], refs[-layer_size:-1], refs[-1]
    layer, core = lax.axis_index("layer"), lax.axis_index("sub")
    rows, half = own.shape[1], mine.shape[2]
    for i, (offset, place) in enumerate(zip(offsets, places)):
        feats = jnp.concatenate([mine[place], theirs[place]], axis=1)
        scores[...] = score_block(feats, weights, rank)
        held = 1 - core if offset else core
        for k, block in enumerate((own, *away)):
            first = lax.rem(lax.rem(layer + k, layer_size) * rows + held * half, 2 * half)
            block[i] = scores[pl.ds(pl.multiple_of(first, rows), rows), :].astype(block.dtype)


def layers_kernel(layer_size, which, own, *refs):
    total = own[which]
    for other in refs[:layer_size - 1]:
        total = total + other[which].astype(F32)
    refs[-1][...] = total.astype(refs[-1].dtype)


def keep_kernel(block, *refs):
    refs[-1][...] = block[...].astype(F32)


def place_kernel(train_size, *refs):
    blocks, out = refs[:-1], refs[-1]
    here = lax.axis_index("train")
    for offset, block in zip((0, *range(train_size - 1, 0, -1)), blocks):
        out[pl.ds(here ^ offset, block.shape[0], stride=train_size), :] = block[...].astype(F32)


def body(inputs, out_grads, proj_in, proj_out, basis_in, basis_out, eigen, queries):
    train_size, layer_size = lax.axis_size("train"), lax.axis_size("layer")
    tokens, width = inputs.shape[1:]
    count, entries = queries.shape[1:]
    rank = proj_in.shape[1]
    half = tokens // 2
    chunks = 1
    vmem, hbm = pl.BlockSpec(memory_space=pltpu.VMEM), pl.BlockSpec(memory_space=pltpu.HBM)
    anywhere = pl.BlockSpec(memory_space=pl.ANY)
    params = pltpu.CompilerParams(vmem_limit_bytes=32 << 20)

    sources = (inputs, out_grads, proj_in, proj_out, basis_in, basis_out, queries, eigen)
    feats, queries, eigen, basis_in, basis_out = pl.pallas_call(
        functools.partial(features_kernel, chunks),
        out_shape=[
            jax.ShapeDtypeStruct((2 * rank, half), BF16),
            jax.ShapeDtypeStruct((count, entries), BF16),
            *[jax.ShapeDtypeStruct((rank, rank), F32)] * 3,
        ],
        in_specs=[hbm] * len(sources),
        out_specs=[vmem] * 5,
        scratch_shapes=[
            pltpu.VMEM((half, width), BF16),
            pltpu.VMEM((half, width), BF16),
            pltpu.VMEM((rank, width), BF16),
            pltpu.VMEM((rank, width), BF16),
            pltpu.SemaphoreType.DMA((len(sources), chunks)),
        ],
        compiler_params=params,
        cost_estimate=pl.CostEstimate(
            flops=4 * half * rank * width, bytes_accessed=4 * width * (half + rank), transcendentals=0
        ),
        name="features",
    )(*[pltpu.with_memory_space_constraint(value, pltpu.HBM) for value in sources])

    def exchange(value, offset):
        return lax.ppermute(value, "train", [(j, j ^ offset) for j in range(train_size)])

    def exchange_across(value, offset):
        pairs = [(2 * j + s, 2 * (j ^ offset) + 1 - s) for j in range(train_size) for s in range(2)]
        return lax.ppermute(value, ("train", "sub"), pairs)

    gathered = {offset: exchange_across(feats, offset) for offset in range(train_size - 1, 0, -1)}

    weights = pl.pallas_call(
        queries_kernel,
        out_shape=jax.ShapeDtypeStruct((count, entries), BF16),
        in_specs=[vmem] * 4,
        out_specs=vmem,
        scratch_shapes=[pltpu.VMEM((entries, count), F32)],
        compiler_params=params,
        cost_estimate=pl.CostEstimate(
            flops=4 * PACK * count * entries * rank, bytes_accessed=4 * count * entries, transcendentals=0
        ),
        name="queries",
    )(queries, basis_in, basis_out, eigen)

    def over_cores(value):
        return lax.ppermute(value, "sub", [(0, 1), (1, 0)])

    rows = tokens // layer_size

    def scored(offsets, places, mine, theirs, after):
        own, *away = pl.pallas_call(
            functools.partial(scores_kernel, layer_size, rank, offsets, places),
            out_shape=[
                jax.ShapeDtypeStruct((len(offsets), rows, count), BF16 if k else F32)
                for k in range(layer_size)
            ],
            in_specs=[vmem] * 3 + [anywhere] * len(after),
            out_specs=[vmem] * layer_size,
            scratch_shapes=[pltpu.VMEM((tokens, count), F32)],
            compiler_params=params,
            cost_estimate=pl.CostEstimate(
                flops=2 * len(offsets) * tokens * entries * count,
                bytes_accessed=2 * count * entries,
                transcendentals=0,
            ),
            name="scores",
        )(weights, mine, theirs, *after)
        return own, [
            lax.ppermute(block, "layer", [(l, (l + k) % layer_size) for l in range(layer_size)])
            for k, block in enumerate(away, 1)
        ]

    def summed(which, offset, own, others, after):
        return pl.pallas_call(
            functools.partial(layers_kernel, layer_size, which),
            out_shape=jax.ShapeDtypeStruct((rows, count), BF16 if offset else F32),
            in_specs=[vmem] * layer_size + [anywhere] * len(after),
            out_specs=vmem,
            compiler_params=params,
            name="layers",
        )(own, *others, *after)

    def kept(block, after):
        return pl.pallas_call(
            keep_kernel,
            out_shape=jax.ShapeDtypeStruct(block.shape, F32),
            in_specs=[vmem] + [anywhere] * len(after),
            out_specs=vmem,
            compiler_params=params,
            name="keep",
        )(block, *after)

    own, others = scored((0,), (0,), feats[None], over_cores(feats[None]), [])
    order = (1, *range(train_size - 1, 1, -1))
    mine = pl.pallas_call(
        functools.partial(pack_kernel, len(order)),
        out_shape=jax.ShapeDtypeStruct((len(order), 2 * rank, half), BF16),
        in_specs=[vmem] * len(order) + [anywhere],
        out_specs=vmem,
        compiler_params=params,
        name="pack",
    )(*[gathered[offset] for offset in order], own)
    theirs = over_cores(mine)

    size = -(-(train_size - 1) // 3)
    groups = [tuple(range(last, max(last - size, 0), -1)) for last in range(train_size - 1, 0, -size)]
    terms, after = {}, []
    for offsets in groups:
        places = [order.index(offset) for offset in offsets]
        mine_terms, their_terms = scored(offsets, places, mine, theirs, after)
        terms.update({offset: (which, offset, mine_terms, their_terms) for which, offset in enumerate(offsets)})
        after = [mine_terms]
    home = summed(0, 0, own, others, after)
    arrived, after = {}, [home]
    for offset in range(train_size - 1, 0, -1):
        block = summed(*terms[offset], after)
        after = [block]
        arrived[offset] = exchange(block, offset)
    blocks, after = [home], []
    for offset in range(train_size - 1, 1, -1):
        blocks.append(kept(arrived[offset], after))
        after = blocks[-1:]
    blocks.append(arrived[1])

    total = pl.pallas_call(
        functools.partial(place_kernel, train_size),
        out_shape=jax.ShapeDtypeStruct((rows * train_size, count), F32),
        in_specs=[vmem] * train_size,
        out_specs=vmem,
        compiler_params=params,
        name="place",
    )(*blocks)
    return total.reshape(rows, train_size, 1, count)


def solution(mesh):
    placed = (
        P("layer", ("parts", "train"), None),
        P("layer", ("parts", "train"), None),
        P("layer", None, None),
        P("layer", None, None),
        P("layer", None, None),
        P("layer", None, None),
        P("layer", None, None),
        P("layer", ("parts", "train", "sub"), None),
    )
    return jax.shard_map(
        body,
        mesh=mesh,
        in_specs=placed,
        out_specs=P(("parts", "train", "layer"), None, "sub", None),
        check_vma=False,
    )
```

```python
import functools

import jax
import jax.numpy as jnp
from jax import lax
from jax.experimental import pallas as pl
from jax.experimental.pallas import tpu as pltpu
from jax.sharding import PartitionSpec as P

F32 = jnp.float32
BF16 = jnp.bfloat16
PACK = 4


def nt(left, right):
    return lax.dot_general(left, right, (((1,), (1,)), ((), ())), preferred_element_type=F32)


def two_terms(matrix):
    high = matrix.astype(BF16)
    return jnp.concatenate([high, (matrix - high.astype(F32)).astype(BF16)], axis=1)


def block_diagonal(matrix):
    rank = matrix.shape[0]
    wide = jnp.concatenate([matrix] * PACK, axis=1)
    tall = jnp.concatenate([wide] * PACK, axis=0)
    rows = lax.broadcasted_iota(jnp.int32, tall.shape, 0) // rank
    columns = lax.broadcasted_iota(jnp.int32, tall.shape, 1) // rank
    return jnp.where(rows == columns, tall, 0.0)


def features_kernel(chunks, *refs):
    sides, (queries_hbm, eigen_hbm) = (refs[0:3], refs[3:6]), refs[6:8]
    feats, queries, eigen, basis_in, basis_out, rows, proj, sems = refs[8:]
    core = lax.axis_index("sub")
    step = rows.shape[1] // chunks

    def part(chunk):
        return pl.ds(chunk * step, step)

    for side, (rows_hbm, proj_hbm, _) in enumerate(sides):
        @pl.when(core == side)
        def _():
            for chunk in range(chunks):
                for number, (source, target) in enumerate(((proj_hbm, proj), (rows_hbm, rows))):
                    pltpu.make_async_copy(
                        source.at[0, :, part(chunk)], target.at[:, part(chunk)], sems.at[number, chunk]
                    ).start()

    others = [
        pltpu.make_async_copy(source.at[0], target, sems.at[2 + number, 0])
        for number, (source, target) in enumerate((
            (sides[0][2], basis_in), (sides[1][2], basis_out), (eigen_hbm, eigen), (queries_hbm, queries)
        ))
    ]
    for copy in others:
        copy.start()
    total = None
    for chunk in range(chunks):
        for number, (source, target) in enumerate(((sides[0][1], proj), (sides[0][0], rows))):
            pltpu.make_async_copy(
                source.at[0, :, part(chunk)], target.at[:, part(chunk)], sems.at[number, chunk]
            ).wait()
        columns = slice(chunk * step, (chunk + 1) * step)
        term = nt(proj[:, columns], rows[:, columns])
        total = term if total is None else total + term
    for copy in others:
        copy.wait()
    basis = jnp.where(core == 0, basis_in[...], basis_out[...])
    feats[...] = jnp.dot(
        two_terms(basis.T),
        jnp.concatenate([total.astype(BF16)] * 2, axis=0),
        preferred_element_type=F32,
    ).astype(BF16)


def pack_kernel(count, *refs):
    for i, ref in enumerate(refs[:count]):
        refs[-1][i] = ref[...]


def score_block(side_in, side_out, weights):
    rank, tokens = side_in.shape
    side_in = side_in.astype(F32)
    side_out = side_out.reshape(rank // 16, 16, tokens)
    total = None
    for part in range(rank // PACK):
        products = []
        for b in range(part * PACK, (part + 1) * PACK):
            row = jnp.broadcast_to(side_in[b:b + 1, :], (16, tokens)).astype(BF16)
            products.append((side_out * row[None]).reshape(rank, tokens))
        width = PACK * rank
        term = jnp.dot(
            weights[:, part * width:(part + 1) * width],
            jnp.concatenate(products, axis=0),
            preferred_element_type=F32,
        )
        total = term if total is None else total + term
    return total.T


def queries_kernel(queries, basis_in, basis_out, eigen, *refs):
    weights, half = refs[-2:]
    rank = basis_in.shape[0]
    width = PACK * rank
    groups = rank // PACK
    right = block_diagonal(basis_in[...].T).astype(BF16)
    for part in range(groups):
        half[part * width:(part + 1) * width, :] = nt(
            right, queries[:, part * width:(part + 1) * width]
        )
    left = block_diagonal(basis_out[...]).astype(BF16)
    spectrum = eigen[...]
    inverse = (1.0 / (spectrum + 0.1 * jnp.mean(spectrum))).T
    for part in range(groups):
        columns = range(part * PACK, (part + 1) * PACK)
        matrix = jnp.concatenate(
            [half[pl.ds(b, rank, stride=rank), :] for b in columns], axis=0
        )
        turned = jnp.dot(matrix.T.astype(BF16), left, preferred_element_type=F32)
        scale = jnp.concatenate([inverse[b:b + 1, :] for b in columns], axis=1)
        weights[:, part * width:(part + 1) * width] = (turned * scale).astype(BF16)


def scores_kernel(layer_size, offsets, places, weights, mine, theirs, *refs):
    own, away, scores = refs[-layer_size - 1], refs[-layer_size:-1], refs[-1]
    layer, core = lax.axis_index("layer"), lax.axis_index("sub")
    rows = own.shape[1]
    for i, (offset, place) in enumerate(zip(offsets, places)):
        here, there = mine[place], theirs[place]
        mine_in = (core == 0) == (offset == 0)
        scores[...] = score_block(
            jnp.where(mine_in, here, there), jnp.where(mine_in, there, here), weights
        )
        for k, block in enumerate((own, *away)):
            first = pl.multiple_of(lax.rem(layer + k, layer_size) * rows, rows)
            block[i] = scores[pl.ds(first, rows), :].astype(block.dtype)


def layers_kernel(layer_size, which, own, *refs):
    total = own[which]
    for other in refs[:layer_size - 1]:
        total = total + other[which].astype(F32)
    refs[-1][...] = total.astype(refs[-1].dtype)


def place_kernel(train_size, *refs):
    arrived, out = refs[:-1], refs[-1]
    here = lax.axis_index("train")
    for offset, block in enumerate(reversed(arrived)):
        out[pl.ds(here ^ offset, block.shape[0], stride=train_size), :] = block[...].astype(F32)


def body(inputs, out_grads, proj_in, proj_out, basis_in, basis_out, eigen, queries):
    train_size, layer_size = lax.axis_size("train"), lax.axis_size("layer")
    tokens, width = inputs.shape[1:]
    count, entries = queries.shape[1:]
    rank = proj_in.shape[1]
    chunks = 2
    vmem, hbm = pl.BlockSpec(memory_space=pltpu.VMEM), pl.BlockSpec(memory_space=pltpu.HBM)
    anywhere = pl.BlockSpec(memory_space=pl.ANY)
    params = pltpu.CompilerParams(vmem_limit_bytes=32 << 20)

    sources = (inputs, proj_in, basis_in, out_grads, proj_out, basis_out, queries, eigen)
    feats, queries, eigen, basis_in, basis_out = pl.pallas_call(
        functools.partial(features_kernel, chunks),
        out_shape=[
            jax.ShapeDtypeStruct((rank, tokens), BF16),
            jax.ShapeDtypeStruct((count, entries), BF16),
            *[jax.ShapeDtypeStruct((rank, rank), F32)] * 3,
        ],
        in_specs=[hbm] * len(sources),
        out_specs=[vmem] * 5,
        scratch_shapes=[
            pltpu.VMEM((tokens, width), BF16),
            pltpu.VMEM((rank, width), BF16),
            pltpu.SemaphoreType.DMA((6, chunks)),
        ],
        compiler_params=params,
        cost_estimate=pl.CostEstimate(
            flops=2 * tokens * rank * width, bytes_accessed=2 * width * (tokens + rank), transcendentals=0
        ),
        name="features",
    )(*[pltpu.with_memory_space_constraint(value, pltpu.HBM) for value in sources])

    def exchange(value, offset):
        return lax.ppermute(value, "train", [(j, j ^ offset) for j in range(train_size)])

    def exchange_across(value, offset):
        pairs = [(2 * j + s, 2 * (j ^ offset) + 1 - s) for j in range(train_size) for s in range(2)]
        return lax.ppermute(value, ("train", "sub"), pairs)

    middle = train_size // 2
    far, near = tuple(range(train_size - 1, middle - 1, -1)), tuple(range(middle))
    gathered = {offset: exchange_across(feats, offset) for offset in range(train_size - 1, 0, -1)}
    gathered[0] = feats

    weights = pl.pallas_call(
        queries_kernel,
        out_shape=jax.ShapeDtypeStruct((count, entries), BF16),
        in_specs=[vmem] * 4,
        out_specs=vmem,
        scratch_shapes=[pltpu.VMEM((entries, count), F32)],
        compiler_params=params,
        cost_estimate=pl.CostEstimate(
            flops=4 * PACK * count * entries * rank, bytes_accessed=4 * count * entries, transcendentals=0
        ),
        name="queries",
    )(queries, basis_in, basis_out, eigen)

    order = (*near, *far)
    mine = pl.pallas_call(
        functools.partial(pack_kernel, len(order)),
        out_shape=jax.ShapeDtypeStruct((len(order), rank, tokens), BF16),
        in_specs=[vmem] * len(order) + [anywhere],
        out_specs=vmem,
        compiler_params=params,
        name="pack",
    )(*[gathered[offset] for offset in order], weights)
    theirs = lax.ppermute(mine, "sub", [(0, 1), (1, 0)])

    rows = tokens // layer_size

    def scored(offsets, after):
        places = [order.index(offset) for offset in offsets]
        own, *away = pl.pallas_call(
            functools.partial(scores_kernel, layer_size, offsets, places),
            out_shape=[
                jax.ShapeDtypeStruct((len(offsets), rows, count), BF16 if k else F32)
                for k in range(layer_size)
            ],
            in_specs=[vmem] * 3 + [anywhere] * len(after),
            out_specs=[vmem] * layer_size,
            scratch_shapes=[pltpu.VMEM((tokens, count), F32)],
            compiler_params=params,
            cost_estimate=pl.CostEstimate(
                flops=2 * len(offsets) * tokens * entries * count,
                bytes_accessed=2 * count * entries,
                transcendentals=0,
            ),
            name="scores",
        )(weights, mine, theirs, *after)
        return own, [
            lax.ppermute(block, "layer", [(l, (l + k) % layer_size) for l in range(layer_size)])
            for k, block in enumerate(away, 1)
        ]

    def summed(which, offset, own, others, after):
        return pl.pallas_call(
            functools.partial(layers_kernel, layer_size, which),
            out_shape=jax.ShapeDtypeStruct((rows, count), BF16 if offset else F32),
            in_specs=[vmem] * layer_size + [anywhere] * len(after),
            out_specs=vmem,
            compiler_params=params,
            name="layers",
        )(own, *others, *after)

    terms, after = {}, []
    for offsets in (far, near):
        own, others = scored(offsets, after)
        terms.update({offset: (which, offset, own, others) for which, offset in enumerate(offsets)})
        after = [own]
    arrived, after = {}, []
    for offset in (*far, *near):
        block = summed(*terms[offset], after)
        after = [block]
        arrived[offset] = exchange(block, offset) if offset else block

    total = pl.pallas_call(
        functools.partial(place_kernel, train_size),
        out_shape=jax.ShapeDtypeStruct((rows * train_size, count), F32),
        in_specs=[vmem] * train_size,
        out_specs=vmem,
        compiler_params=params,
        name="place",
    )(*[arrived[offset] for offset in reversed(range(train_size))])
    return total.reshape(rows, train_size, 1, count)


def solution(mesh):
    placed = (
        P("layer", ("parts", "train"), None),
        P("layer", ("parts", "train"), None),
        P("layer", None, None),
        P("layer", None, None),
        P("layer", None, None),
        P("layer", None, None),
        P("layer", None, None),
        P("layer", ("parts", "train", "sub"), None),
    )
    return jax.shard_map(
        body,
        mesh=mesh,
        in_specs=placed,
        out_specs=P(("parts", "train", "layer"), None, "sub", None),
        check_vma=False,
    )
```

```python
import functools

import jax
import jax.numpy as jnp
from jax import lax
from jax.experimental import pallas as pl
from jax.experimental.pallas import tpu as pltpu
from jax.sharding import PartitionSpec as P

F32 = jnp.float32
BF16 = jnp.bfloat16
PACK = 4


def plan(train_size):
    if train_size == 4:
        return FEATURE_ROUNDS, SCORE_ROUNDS, FIRST
    rounds = [
        tuple((j, j ^ offset) for j in range(train_size)) for offset in range(train_size - 1, 0, -1)
    ]
    return rounds, rounds, train_size // 2


FEATURE_ROUNDS = [((3, 1), (2, 0)), ((1, 0),), ((3, 0), (0, 2), (1, 3), (2, 1)), ((0, 3), (3, 2)), ((0, 1), (2, 3), (1, 2))]
SCORE_ROUNDS = [((3, 0), (1, 2)), ((2, 0), (0, 2), (3, 1)), ((2, 1), (1, 0), (0, 3)), ((1, 3), (0, 1), (3, 2)), ((2, 3),)]
FIRST = 3


def lookup(index, values):
    found = jnp.int32(values[0])
    for place, value in enumerate(values[1:], 1):
        found = jnp.where(index == place, jnp.int32(value), found)
    return found


def sources_of(pairs, train_size):
    return [next((s for s, d in pairs if d == j), -1) for j in range(train_size)]


def nt(left, right):
    return lax.dot_general(left, right, (((1,), (1,)), ((), ())), preferred_element_type=F32)


def two_terms(matrix):
    high = matrix.astype(BF16)
    return jnp.concatenate([high, (matrix - high.astype(F32)).astype(BF16)], axis=1)


def block_diagonal(matrix):
    rank = matrix.shape[0]
    wide = jnp.concatenate([matrix] * PACK, axis=1)
    tall = jnp.concatenate([wide] * PACK, axis=0)
    rows = lax.broadcasted_iota(jnp.int32, tall.shape, 0) // rank
    columns = lax.broadcasted_iota(jnp.int32, tall.shape, 1) // rank
    return jnp.where(rows == columns, tall, 0.0)


def features_kernel(chunks, *refs):
    sides, (queries_hbm, eigen_hbm) = (refs[0:3], refs[3:6]), refs[6:8]
    feats, queries, eigen, basis_in, basis_out, rows, proj, sems = refs[8:]
    core = lax.axis_index("sub")
    step = rows.shape[1] // chunks

    def part(chunk):
        return pl.ds(chunk * step, step)

    for side, (rows_hbm, proj_hbm, _) in enumerate(sides):
        @pl.when(core == side)
        def _():
            for chunk in range(chunks):
                for number, (source, target) in enumerate(((proj_hbm, proj), (rows_hbm, rows))):
                    pltpu.make_async_copy(
                        source.at[0, :, part(chunk)], target.at[:, part(chunk)], sems.at[number, chunk]
                    ).start()

    others = [
        pltpu.make_async_copy(source.at[0], target, sems.at[2 + number, 0])
        for number, (source, target) in enumerate((
            (sides[0][2], basis_in), (sides[1][2], basis_out), (eigen_hbm, eigen), (queries_hbm, queries)
        ))
    ]
    for copy in others:
        copy.start()
    total = None
    for chunk in range(chunks):
        for number, (source, target) in enumerate(((sides[0][1], proj), (sides[0][0], rows))):
            pltpu.make_async_copy(
                source.at[0, :, part(chunk)], target.at[:, part(chunk)], sems.at[number, chunk]
            ).wait()
        columns = slice(chunk * step, (chunk + 1) * step)
        term = nt(proj[:, columns], rows[:, columns])
        total = term if total is None else total + term
    for copy in others:
        copy.wait()
    basis = jnp.where(core == 0, basis_in[...], basis_out[...])
    feats[...] = jnp.dot(
        two_terms(basis.T),
        jnp.concatenate([total.astype(BF16)] * 2, axis=0),
        preferred_element_type=F32,
    ).astype(BF16)


def pack_kernel(rounds, *refs):
    own, arrivals, out = refs[0], refs[1:1 + len(rounds)], refs[-1]
    train_size = out.shape[0]
    here = lax.axis_index("train")
    out[here] = own[...]
    for pairs, arrival in zip(rounds, arrivals):
        sources = sources_of(pairs, train_size)
        source = lookup(here, sources)
        if min(sources) >= 0:
            out[source] = arrival[...]
        else:
            @pl.when(source >= 0)
            def _():
                out[source] = arrival[...]


def score_block(side_in, side_out, weights):
    rank, tokens = side_in.shape
    side_in = side_in.astype(F32)
    side_out = side_out.reshape(rank // 16, 16, tokens)
    total = None
    for part in range(rank // PACK):
        products = []
        for b in range(part * PACK, (part + 1) * PACK):
            row = jnp.broadcast_to(side_in[b:b + 1, :], (16, tokens)).astype(BF16)
            products.append((side_out * row[None]).reshape(rank, tokens))
        width = PACK * rank
        term = jnp.dot(
            weights[:, part * width:(part + 1) * width],
            jnp.concatenate(products, axis=0),
            preferred_element_type=F32,
        )
        total = term if total is None else total + term
    return total.T


def queries_kernel(queries, basis_in, basis_out, eigen, *refs):
    weights, half = refs[-2:]
    rank = basis_in.shape[0]
    width = PACK * rank
    groups = rank // PACK
    right = block_diagonal(basis_in[...].T).astype(BF16)
    for part in range(groups):
        half[part * width:(part + 1) * width, :] = nt(
            right, queries[:, part * width:(part + 1) * width]
        )
    left = block_diagonal(basis_out[...]).astype(BF16)
    spectrum = eigen[...]
    inverse = (1.0 / (spectrum + 0.1 * jnp.mean(spectrum))).T
    for part in range(groups):
        columns = range(part * PACK, (part + 1) * PACK)
        matrix = jnp.concatenate(
            [half[pl.ds(b, rank, stride=rank), :] for b in columns], axis=0
        )
        turned = jnp.dot(matrix.T.astype(BF16), left, preferred_element_type=F32)
        scale = jnp.concatenate([inverse[b:b + 1, :] for b in columns], axis=1)
        weights[:, part * width:(part + 1) * width] = (turned * scale).astype(BF16)


def scores_kernel(layer_size, targets, weights, mine, theirs, *refs):
    own, away, scores = refs[-layer_size - 1], refs[-layer_size:-1], refs[-1]
    place, layer, core = (lax.axis_index(name) for name in ("train", "layer", "sub"))
    rows = own.shape[1]
    for i, target in enumerate(targets):
        slot = lookup(place, target)
        here, there = mine[slot], theirs[slot]
        mine_in = (core == 0) == (slot == place)
        scores[...] = score_block(
            jnp.where(mine_in, here, there), jnp.where(mine_in, there, here), weights
        )
        for k, block in enumerate((own, *away)):
            first = pl.multiple_of(lax.rem(layer + k, layer_size) * rows, rows)
            block[i] = scores[pl.ds(first, rows), :].astype(block.dtype)


def layers_kernel(layer_size, places, own, *refs):
    which = places[0] if len(set(places)) == 1 else lookup(lax.axis_index("train"), places)
    total = own[which]
    for other in refs[:layer_size - 1]:
        total = total + other[which].astype(F32)
    refs[-1][...] = total.astype(refs[-1].dtype)


def keep_kernel(block, *refs):
    refs[-1][...] = block[...]


def place_kernel(train_size, rounds, own, *refs):
    arrivals, out = refs[:-1], refs[-1]
    here = lax.axis_index("train")
    rows = own.shape[0]
    out[pl.ds(here, rows, stride=train_size), :] = own[...]
    for pairs, arrival in zip(rounds, arrivals):
        sources = sources_of(pairs, train_size)
        source = lookup(here, sources)
        if min(sources) >= 0:
            out[pl.ds(source, rows, stride=train_size), :] = arrival[...].astype(F32)
        else:
            @pl.when(source >= 0)
            def _():
                out[pl.ds(source, rows, stride=train_size), :] = arrival[...].astype(F32)


def body(inputs, out_grads, proj_in, proj_out, basis_in, basis_out, eigen, queries):
    train_size, layer_size = lax.axis_size("train"), lax.axis_size("layer")
    tokens, width = inputs.shape[1:]
    count, entries = queries.shape[1:]
    rank = proj_in.shape[1]
    chunks = 2
    vmem, hbm = pl.BlockSpec(memory_space=pltpu.VMEM), pl.BlockSpec(memory_space=pltpu.HBM)
    anywhere = pl.BlockSpec(memory_space=pl.ANY)
    params = pltpu.CompilerParams(vmem_limit_bytes=32 << 20)

    sources = (inputs, proj_in, basis_in, out_grads, proj_out, basis_out, queries, eigen)
    feats, queries, eigen, basis_in, basis_out = pl.pallas_call(
        functools.partial(features_kernel, chunks),
        out_shape=[
            jax.ShapeDtypeStruct((rank, tokens), BF16),
            jax.ShapeDtypeStruct((count, entries), BF16),
            *[jax.ShapeDtypeStruct((rank, rank), F32)] * 3,
        ],
        in_specs=[hbm] * len(sources),
        out_specs=[vmem] * 5,
        scratch_shapes=[
            pltpu.VMEM((tokens, width), BF16),
            pltpu.VMEM((rank, width), BF16),
            pltpu.SemaphoreType.DMA((6, chunks)),
        ],
        compiler_params=params,
        cost_estimate=pl.CostEstimate(
            flops=2 * tokens * rank * width, bytes_accessed=2 * width * (tokens + rank), transcendentals=0
        ),
        name="features",
    )(*[pltpu.with_memory_space_constraint(value, pltpu.HBM) for value in sources])

    feature_rounds, score_rounds, first = plan(train_size)

    def kept(block, after):
        return pl.pallas_call(
            keep_kernel,
            out_shape=jax.ShapeDtypeStruct(block.shape, block.dtype),
            in_specs=[vmem] + [anywhere] * len(after),
            out_specs=vmem,
            compiler_params=params,
            name="keep",
        )(block, *after)

    def in_order(blocks):
        ordered = []
        for block in blocks[:-1]:
            ordered.append(kept(block, ordered[-1:]))
        return ordered + blocks[-1:]

    def across(pairs):
        cores = [(2 * s + c, 2 * d + 1 - c) for s, d in pairs for c in range(2)]
        return lax.ppermute(feats, ("train", "sub"), cores)

    gathered = [across(pairs) for pairs in feature_rounds]

    weights = pl.pallas_call(
        queries_kernel,
        out_shape=jax.ShapeDtypeStruct((count, entries), BF16),
        in_specs=[vmem] * 4,
        out_specs=vmem,
        scratch_shapes=[pltpu.VMEM((entries, count), F32)],
        compiler_params=params,
        cost_estimate=pl.CostEstimate(
            flops=4 * PACK * count * entries * rank, bytes_accessed=4 * count * entries, transcendentals=0
        ),
        name="queries",
    )(queries, basis_in, basis_out, eigen)

    mine = pl.pallas_call(
        functools.partial(pack_kernel, feature_rounds[::-1]),
        out_shape=jax.ShapeDtypeStruct((train_size, rank, tokens), BF16),
        in_specs=[vmem] * (1 + len(gathered)) + [anywhere],
        out_specs=vmem,
        compiler_params=params,
        name="pack",
    )(feats, *gathered[::-1], weights)
    theirs = lax.ppermute(mine, "sub", [(0, 1), (1, 0)])

    rows = tokens // layer_size

    def scored(targets, after):
        own, *away = pl.pallas_call(
            functools.partial(scores_kernel, layer_size, targets),
            out_shape=[
                jax.ShapeDtypeStruct((len(targets), rows, count), BF16 if k else F32)
                for k in range(layer_size)
            ],
            in_specs=[vmem] * 3 + [anywhere] * len(after),
            out_specs=[vmem] * layer_size,
            scratch_shapes=[pltpu.VMEM((tokens, count), F32)],
            compiler_params=params,
            cost_estimate=pl.CostEstimate(
                flops=2 * len(targets) * tokens * entries * count,
                bytes_accessed=2 * count * entries,
                transcendentals=0,
            ),
            name="scores",
        )(weights, mine, theirs, *after)
        return own, [
            lax.ppermute(block, "layer", [(l, (l + k) % layer_size) for l in range(layer_size)])
            for k, block in enumerate(away, 1)
        ]

    def summed(places, dtype, own, others, after):
        return pl.pallas_call(
            functools.partial(layers_kernel, layer_size, places),
            out_shape=jax.ShapeDtypeStruct((rows, count), dtype),
            in_specs=[vmem] * layer_size + [anywhere] * len(after),
            out_specs=vmem,
            compiler_params=params,
            name="layers",
        )(own, *others, *after)

    def table(rounds, lead):
        lists = [lead(j) + [d for pairs in rounds for s, d in pairs if s == j] for j in range(train_size)]
        length = max(len(targets) for targets in lists)
        return lists, [
            [targets[i] if i < len(targets) else j for j, targets in enumerate(lists)] for i in range(length)
        ]

    first_lists, first_targets = table(score_rounds[:first], lambda j: [])
    last_lists, last_targets = table(score_rounds[first:], lambda j: [j])
    first_terms = scored(first_targets, [])
    last_terms = scored(last_targets, first_terms[:1])
    arrivals, after = [], []
    for number, pairs in enumerate(score_rounds):
        lists, terms = (first_lists, first_terms) if number < first else (last_lists, last_terms)
        if number == first:
            home = summed([0] * train_size, F32, *last_terms, after)
            after = [home]
        targets = dict(pairs)
        places = [lists[j].index(targets[j]) if j in targets else 0 for j in range(train_size)]
        block = summed(places, BF16, *terms, after)
        after = [block]
        arrivals.append(lax.ppermute(block, "train", pairs))
    if first >= len(score_rounds):
        home = summed([0] * train_size, F32, *last_terms, after)

    total = pl.pallas_call(
        functools.partial(place_kernel, train_size, score_rounds),
        out_shape=jax.ShapeDtypeStruct((rows * train_size, count), F32),
        in_specs=[vmem] * (1 + len(arrivals)),
        out_specs=vmem,
        compiler_params=params,
        name="place",
    )(home, *in_order(arrivals))
    return total.reshape(rows, train_size, 1, count)


def solution(mesh):
    placed = (
        P("layer", ("parts", "train"), None),
        P("layer", ("parts", "train"), None),
        P("layer", None, None),
        P("layer", None, None),
        P("layer", None, None),
        P("layer", None, None),
        P("layer", None, None),
        P("layer", ("parts", "train", "sub"), None),
    )
    return jax.shard_map(
        body,
        mesh=mesh,
        in_specs=placed,
        out_specs=P(("parts", "train", "layer"), None, "sub", None),
        check_vma=False,
    )
```

```python
import functools

import jax
import jax.numpy as jnp
from jax import lax
from jax.experimental import pallas as pl
from jax.experimental.pallas import tpu as pltpu
from jax.sharding import PartitionSpec as P

F32 = jnp.float32
BF16 = jnp.bfloat16
PACK = 4


def nt(left, right):
    return lax.dot_general(left, right, (((1,), (1,)), ((), ())), preferred_element_type=F32)


def two_terms(matrix):
    high = matrix.astype(BF16)
    return jnp.concatenate([high, (matrix - high.astype(F32)).astype(BF16)], axis=1)


def block_diagonal(matrix):
    rank = matrix.shape[0]
    wide = jnp.concatenate([matrix] * PACK, axis=1)
    tall = jnp.concatenate([wide] * PACK, axis=0)
    rows = lax.broadcasted_iota(jnp.int32, tall.shape, 0) // rank
    columns = lax.broadcasted_iota(jnp.int32, tall.shape, 1) // rank
    return jnp.where(rows == columns, tall, 0.0)


def features_kernel(chunks, *refs):
    sides, (queries_hbm, eigen_hbm) = (refs[0:3], refs[3:6]), refs[6:8]
    feats, queries, eigen, basis_in, basis_out, rows, proj, sems = refs[8:]
    core = lax.axis_index("sub")
    step = rows.shape[1] // chunks

    def part(chunk):
        return pl.ds(chunk * step, step)

    for side, (rows_hbm, proj_hbm, _) in enumerate(sides):
        @pl.when(core == side)
        def _():
            for chunk in range(chunks):
                for number, (source, target) in enumerate(((proj_hbm, proj), (rows_hbm, rows))):
                    pltpu.make_async_copy(
                        source.at[0, :, part(chunk)], target.at[:, part(chunk)], sems.at[number, chunk]
                    ).start()

    others = [
        pltpu.make_async_copy(source.at[0], target, sems.at[2 + number, 0])
        for number, (source, target) in enumerate((
            (sides[0][2], basis_in), (sides[1][2], basis_out), (eigen_hbm, eigen), (queries_hbm, queries)
        ))
    ]
    for copy in others:
        copy.start()
    total = None
    for chunk in range(chunks):
        for number, (source, target) in enumerate(((sides[0][1], proj), (sides[0][0], rows))):
            pltpu.make_async_copy(
                source.at[0, :, part(chunk)], target.at[:, part(chunk)], sems.at[number, chunk]
            ).wait()
        columns = slice(chunk * step, (chunk + 1) * step)
        term = nt(proj[:, columns], rows[:, columns])
        total = term if total is None else total + term
    for copy in others[:2]:
        copy.wait()
    basis = jnp.where(core == 0, basis_in[...], basis_out[...])
    feats[...] = jnp.dot(
        two_terms(basis.T),
        jnp.concatenate([total.astype(BF16)] * 2, axis=0),
        preferred_element_type=F32,
    ).astype(BF16)
    for copy in others[2:]:
        copy.wait()


def pack_kernel(count, *refs):
    for i, ref in enumerate(refs[:count]):
        refs[-1][i] = ref[...]


def score_block(side_in, side_out, weights):
    rank, tokens = side_in.shape
    side_in = side_in.astype(F32)
    side_out = side_out.reshape(rank // 16, 16, tokens)
    total = None
    for part in range(rank // PACK):
        products = []
        for b in range(part * PACK, (part + 1) * PACK):
            row = jnp.broadcast_to(side_in[b:b + 1, :], (16, tokens)).astype(BF16)
            products.append((side_out * row[None]).reshape(rank, tokens))
        width = PACK * rank
        term = jnp.dot(
            weights[:, part * width:(part + 1) * width],
            jnp.concatenate(products, axis=0),
            preferred_element_type=F32,
        )
        total = term if total is None else total + term
    return total.T


def queries_kernel(queries, basis_in, basis_out, eigen, *refs):
    weights, half = refs[-2:]
    rank = basis_in.shape[0]
    width = PACK * rank
    groups = rank // PACK
    right = block_diagonal(basis_in[...].T).astype(BF16)
    for part in range(groups):
        half[part * width:(part + 1) * width, :] = nt(
            right, queries[:, part * width:(part + 1) * width]
        )
    left = block_diagonal(basis_out[...]).astype(BF16)
    spectrum = eigen[...]
    inverse = (1.0 / (spectrum + 0.1 * jnp.mean(spectrum))).T
    for part in range(groups):
        columns = range(part * PACK, (part + 1) * PACK)
        matrix = jnp.concatenate(
            [half[pl.ds(b, rank, stride=rank), :] for b in columns], axis=0
        )
        turned = jnp.dot(matrix.T.astype(BF16), left, preferred_element_type=F32)
        scale = jnp.concatenate([inverse[b:b + 1, :] for b in columns], axis=1)
        weights[:, part * width:(part + 1) * width] = (turned * scale).astype(BF16)


def scores_kernel(layer_size, offsets, places, weights, mine, theirs, *refs):
    own, away, scores = refs[-layer_size - 1], refs[-layer_size:-1], refs[-1]
    layer, core = lax.axis_index("layer"), lax.axis_index("sub")
    rows = own.shape[1]
    for i, (offset, place) in enumerate(zip(offsets, places)):
        here, there = mine[place], theirs[place]
        mine_in = (core == 0) == (offset == 0)
        scores[...] = score_block(
            jnp.where(mine_in, here, there), jnp.where(mine_in, there, here), weights
        )
        for k, block in enumerate((own, *away)):
            first = pl.multiple_of(lax.rem(layer + k, layer_size) * rows, rows)
            block[i] = scores[pl.ds(first, rows), :].astype(block.dtype)


def layers_kernel(layer_size, which, own, *refs):
    total = own[which]
    for other in refs[:layer_size - 1]:
        total = total + other[which].astype(F32)
    refs[-1][...] = total.astype(refs[-1].dtype)


def place_kernel(train_size, pieces, *refs):
    arrived, out, staged, sems = refs[:train_size], *refs[train_size:]
    here = lax.axis_index("train")
    step = arrived[0].shape[0] // pieces
    copies = []
    for piece in range(pieces):
        rows = pl.ds(piece * step * train_size, step * train_size)
        for offset, block in enumerate(reversed(arrived)):
            first = piece * step * train_size + (here ^ offset)
            staged[pl.ds(first, step, stride=train_size), :] = block[piece * step:(piece + 1) * step, :].astype(F32)
        copies.append(pltpu.make_async_copy(staged.at[rows, :], out.at[rows, :], sems.at[piece]))
        copies[-1].start()
    for copy in copies:
        copy.wait()


def body(inputs, out_grads, proj_in, proj_out, basis_in, basis_out, eigen, queries):
    train_size, layer_size = lax.axis_size("train"), lax.axis_size("layer")
    tokens, width = inputs.shape[1:]
    count, entries = queries.shape[1:]
    rank = proj_in.shape[1]
    chunks = 4
    vmem, hbm = pl.BlockSpec(memory_space=pltpu.VMEM), pl.BlockSpec(memory_space=pltpu.HBM)
    anywhere = pl.BlockSpec(memory_space=pl.ANY)
    params = pltpu.CompilerParams(vmem_limit_bytes=32 << 20)

    sources = (inputs, proj_in, basis_in, out_grads, proj_out, basis_out, queries, eigen)
    feats, queries, eigen, basis_in, basis_out = pl.pallas_call(
        functools.partial(features_kernel, chunks),
        out_shape=[
            jax.ShapeDtypeStruct((rank, tokens), BF16),
            jax.ShapeDtypeStruct((count, entries), BF16),
            *[jax.ShapeDtypeStruct((rank, rank), F32)] * 3,
        ],
        in_specs=[hbm] * len(sources),
        out_specs=[vmem] * 5,
        scratch_shapes=[
            pltpu.VMEM((tokens, width), BF16),
            pltpu.VMEM((rank, width), BF16),
            pltpu.SemaphoreType.DMA((6, chunks)),
        ],
        compiler_params=params,
        cost_estimate=pl.CostEstimate(
            flops=2 * tokens * rank * width, bytes_accessed=2 * width * (tokens + rank), transcendentals=0
        ),
        name="features",
    )(*[pltpu.with_memory_space_constraint(value, pltpu.HBM) for value in sources])

    def exchange(value, offset):
        return lax.ppermute(value, "train", [(j, j ^ offset) for j in range(train_size)])

    def exchange_across(value, offset):
        pairs = [(2 * j + s, 2 * (j ^ offset) + 1 - s) for j in range(train_size) for s in range(2)]
        return lax.ppermute(value, ("train", "sub"), pairs)

    middle = train_size // 2
    far, near = tuple(range(train_size - 1, middle - 1, -1)), tuple(range(middle))
    gathered = {offset: exchange_across(feats, offset) for offset in range(train_size - 1, 0, -1)}
    gathered[0] = feats

    weights = pl.pallas_call(
        queries_kernel,
        out_shape=jax.ShapeDtypeStruct((count, entries), BF16),
        in_specs=[vmem] * 4,
        out_specs=vmem,
        scratch_shapes=[pltpu.VMEM((entries, count), F32)],
        compiler_params=params,
        cost_estimate=pl.CostEstimate(
            flops=4 * PACK * count * entries * rank, bytes_accessed=4 * count * entries, transcendentals=0
        ),
        name="queries",
    )(queries, basis_in, basis_out, eigen)

    order = (*near, *far)
    mine = pl.pallas_call(
        functools.partial(pack_kernel, len(order)),
        out_shape=jax.ShapeDtypeStruct((len(order), rank, tokens), BF16),
        in_specs=[vmem] * len(order) + [anywhere],
        out_specs=vmem,
        compiler_params=params,
        name="pack",
    )(*[gathered[offset] for offset in order], weights)
    theirs = lax.ppermute(mine, "sub", [(0, 1), (1, 0)])

    rows = tokens // layer_size

    def scored(offsets, after):
        places = [order.index(offset) for offset in offsets]
        own, *away = pl.pallas_call(
            functools.partial(scores_kernel, layer_size, offsets, places),
            out_shape=[
                jax.ShapeDtypeStruct((len(offsets), rows, count), BF16 if k else F32)
                for k in range(layer_size)
            ],
            in_specs=[vmem] * 3 + [anywhere] * len(after),
            out_specs=[vmem] * layer_size,
            scratch_shapes=[pltpu.VMEM((tokens, count), F32)],
            compiler_params=params,
            cost_estimate=pl.CostEstimate(
                flops=2 * len(offsets) * tokens * entries * count,
                bytes_accessed=2 * count * entries,
                transcendentals=0,
            ),
            name="scores",
        )(weights, mine, theirs, *after)
        return own, [
            lax.ppermute(block, "layer", [(l, (l + k) % layer_size) for l in range(layer_size)])
            for k, block in enumerate(away, 1)
        ]

    def summed(which, offset, own, others, after):
        return pl.pallas_call(
            functools.partial(layers_kernel, layer_size, which),
            out_shape=jax.ShapeDtypeStruct((rows, count), BF16 if offset else F32),
            in_specs=[vmem] * layer_size + [anywhere] * len(after),
            out_specs=vmem,
            compiler_params=params,
            name="layers",
        )(own, *others, *after)

    terms, after = {}, []
    for offsets in (far, near):
        own, others = scored(offsets, after)
        terms.update({offset: (which, offset, own, others) for which, offset in enumerate(offsets)})
        after = [own]
    arrived, after = {}, []
    for offset in (*far, *near):
        block = summed(*terms[offset], after)
        after = [block]
        arrived[offset] = exchange(block, offset) if offset else block

    pieces = 2
    total = pl.pallas_call(
        functools.partial(place_kernel, train_size, pieces),
        out_shape=jax.ShapeDtypeStruct((rows * train_size, count), F32),
        in_specs=[vmem] * train_size,
        out_specs=hbm,
        scratch_shapes=[pltpu.VMEM((rows * train_size, count), F32), pltpu.SemaphoreType.DMA((pieces,))],
        compiler_params=params,
        name="place",
    )(*[arrived[offset] for offset in reversed(range(train_size))])
    return total.reshape(rows, train_size, 1, count)


def solution(mesh):
    placed = (
        P("layer", ("parts", "train"), None),
        P("layer", ("parts", "train"), None),
        P("layer", None, None),
        P("layer", None, None),
        P("layer", None, None),
        P("layer", None, None),
        P("layer", None, None),
        P("layer", ("parts", "train", "sub"), None),
    )
    return jax.shard_map(
        body,
        mesh=mesh,
        in_specs=placed,
        out_specs=P(("parts", "train", "layer"), None, "sub", None),
        check_vma=False,
    )
```

```python
import functools

import jax
import jax.numpy as jnp
from jax import lax
from jax.experimental import pallas as pl
from jax.experimental.pallas import tpu as pltpu
from jax.sharding import PartitionSpec as P

F32 = jnp.float32
BF16 = jnp.bfloat16
PACK = 4


def nt(left, right):
    return lax.dot_general(left, right, (((1,), (1,)), ((), ())), preferred_element_type=F32)


def two_terms(matrix):
    high = matrix.astype(BF16)
    return jnp.concatenate([high, (matrix - high.astype(F32)).astype(BF16)], axis=1)


def block_diagonal(matrix):
    rank = matrix.shape[0]
    wide = jnp.concatenate([matrix] * PACK, axis=1)
    tall = jnp.concatenate([wide] * PACK, axis=0)
    rows = lax.broadcasted_iota(jnp.int32, tall.shape, 0) // rank
    columns = lax.broadcasted_iota(jnp.int32, tall.shape, 1) // rank
    return jnp.where(rows == columns, tall, 0.0)


def features_kernel(chunks, *refs):
    sides, (feats, rows, proj, basis, sems) = (refs[0:3], refs[3:6]), refs[6:]
    core = lax.axis_index("sub")
    step = rows.shape[1] // chunks

    def copies(side):
        rows_hbm, proj_hbm, basis_hbm = side
        pairs = [(proj_hbm.at[0], proj)]
        for chunk in range(chunks):
            part = pl.ds(chunk * step, step)
            pairs.append((rows_hbm.at[0, :, part], rows.at[:, part]))
        pairs.append((basis_hbm.at[0], basis))
        return [pltpu.make_async_copy(*pair, sems.at[i]) for i, pair in enumerate(pairs)]

    for number, side in enumerate(sides):
        @pl.when(core == number)
        def _():
            for copy in copies(side):
                copy.start()

    waits = copies(sides[0])
    waits[0].wait()
    total = None
    for chunk in range(chunks):
        waits[1 + chunk].wait()
        columns = slice(chunk * step, (chunk + 1) * step)
        term = nt(proj[:, columns], rows[:, columns])
        total = term if total is None else total + term
    waits[-1].wait()
    feats[...] = jnp.dot(
        two_terms(basis[...].T),
        jnp.concatenate([total.astype(BF16)] * 2, axis=0),
        preferred_element_type=F32,
    ).astype(BF16)


def pack_kernel(count, *refs):
    for i, ref in enumerate(refs[:count]):
        refs[-1][i] = ref[...]


def score_block(side_in, side_out, weights):
    rank, tokens = side_in.shape
    side_in = side_in.astype(F32)
    side_out = side_out.reshape(rank // 16, 16, tokens)
    total = None
    for part in range(rank // PACK):
        products = []
        for b in range(part * PACK, (part + 1) * PACK):
            row = jnp.broadcast_to(side_in[b:b + 1, :], (16, tokens)).astype(BF16)
            products.append((side_out * row[None]).reshape(rank, tokens))
        width = PACK * rank
        term = jnp.dot(
            weights[:, part * width:(part + 1) * width],
            jnp.concatenate(products, axis=0),
            preferred_element_type=F32,
        )
        total = term if total is None else total + term
    return total.T


def queries_kernel(queries, basis_in, basis_out, eigen, *refs):
    weights, half = refs[-2:]
    rank = basis_in.shape[0]
    width = PACK * rank
    groups = rank // PACK
    right = block_diagonal(basis_in[...].T).astype(BF16)
    for part in range(groups):
        half[part * width:(part + 1) * width, :] = nt(
            right, queries[:, part * width:(part + 1) * width]
        )
    left = block_diagonal(basis_out[...]).astype(BF16)
    spectrum = eigen[...]
    inverse = (1.0 / (spectrum + 0.1 * jnp.mean(spectrum))).T
    for part in range(groups):
        columns = range(part * PACK, (part + 1) * PACK)
        matrix = jnp.concatenate(
            [half[pl.ds(b, rank, stride=rank), :] for b in columns], axis=0
        )
        turned = jnp.dot(matrix.T.astype(BF16), left, preferred_element_type=F32)
        scale = jnp.concatenate([inverse[b:b + 1, :] for b in columns], axis=1)
        weights[:, part * width:(part + 1) * width] = (turned * scale).astype(BF16)


def scores_kernel(layer_size, offsets, places, weights, mine, theirs, *refs):
    own, away, scores = refs[-layer_size - 1], refs[-layer_size:-1], refs[-1]
    layer, core = lax.axis_index("layer"), lax.axis_index("sub")
    rows = own.shape[1]
    for i, (offset, place) in enumerate(zip(offsets, places)):
        here, there = mine[place], theirs[place]
        mine_in = (core == 0) == (offset == 0)
        scores[...] = score_block(
            jnp.where(mine_in, here, there), jnp.where(mine_in, there, here), weights
        )
        for k, block in enumerate((own, *away)):
            first = pl.multiple_of(lax.rem(layer + k, layer_size) * rows, rows)
            block[i] = scores[pl.ds(first, rows), :].astype(block.dtype)


def layers_kernel(layer_size, which, own, *refs):
    total = own[which]
    for other in refs[:layer_size - 1]:
        total = total + other[which].astype(F32)
    refs[-1][...] = total.astype(refs[-1].dtype)


def place_kernel(train_size, *refs):
    arrived, out = refs[:-1], refs[-1]
    here = lax.axis_index("train")
    for offset, block in enumerate(reversed(arrived)):
        out[pl.ds(here ^ offset, block.shape[0], stride=train_size), :] = block[...].astype(F32)


def body(inputs, out_grads, proj_in, proj_out, basis_in, basis_out, eigen, queries):
    train_size, layer_size = lax.axis_size("train"), lax.axis_size("layer")
    tokens, width = inputs.shape[1:]
    count, entries = queries.shape[1:]
    rank = proj_in.shape[1]
    chunks = 2
    vmem, hbm = pl.BlockSpec(memory_space=pltpu.VMEM), pl.BlockSpec(memory_space=pltpu.HBM)
    anywhere = pl.BlockSpec(memory_space=pl.ANY)
    params = pltpu.CompilerParams(vmem_limit_bytes=32 << 20)

    sources = (inputs, proj_in, basis_in, out_grads, proj_out, basis_out)
    feats = pl.pallas_call(
        functools.partial(features_kernel, chunks),
        out_shape=jax.ShapeDtypeStruct((rank, tokens), BF16),
        in_specs=[hbm] * len(sources),
        out_specs=vmem,
        scratch_shapes=[
            pltpu.VMEM((tokens, width), BF16),
            pltpu.VMEM((rank, width), BF16),
            pltpu.VMEM((rank, rank), F32),
            pltpu.SemaphoreType.DMA((chunks + 2,)),
        ],
        compiler_params=params,
        cost_estimate=pl.CostEstimate(
            flops=2 * tokens * rank * width, bytes_accessed=2 * width * (tokens + rank), transcendentals=0
        ),
        name="features",
    )(*[pltpu.with_memory_space_constraint(value, pltpu.HBM) for value in sources])

    def exchange(value, offset):
        return lax.ppermute(value, "train", [(j, j ^ offset) for j in range(train_size)])

    def exchange_across(value, offset):
        pairs = [(2 * j + s, 2 * (j ^ offset) + 1 - s) for j in range(train_size) for s in range(2)]
        return lax.ppermute(value, ("train", "sub"), pairs)

    middle = train_size // 2
    far, near = tuple(range(train_size - 1, middle - 1, -1)), tuple(range(middle))
    gathered = {offset: exchange_across(feats, offset) for offset in range(train_size - 1, 0, -1)}
    gathered[0] = feats

    weights = pl.pallas_call(
        queries_kernel,
        out_shape=jax.ShapeDtypeStruct((count, entries), BF16),
        in_specs=[vmem] * 4,
        out_specs=vmem,
        scratch_shapes=[pltpu.VMEM((entries, count), F32)],
        compiler_params=params,
        cost_estimate=pl.CostEstimate(
            flops=4 * PACK * count * entries * rank, bytes_accessed=4 * count * entries, transcendentals=0
        ),
        name="queries",
    )(queries[0], basis_in[0], basis_out[0], eigen[0])

    order = (*near, *far)
    mine = pl.pallas_call(
        functools.partial(pack_kernel, len(order)),
        out_shape=jax.ShapeDtypeStruct((len(order), rank, tokens), BF16),
        in_specs=[vmem] * len(order) + [anywhere],
        out_specs=vmem,
        compiler_params=params,
        name="pack",
    )(*[gathered[offset] for offset in order], weights)
    theirs = lax.ppermute(mine, "sub", [(0, 1), (1, 0)])

    rows = tokens // layer_size

    def scored(offsets, after):
        places = [order.index(offset) for offset in offsets]
        own, *away = pl.pallas_call(
            functools.partial(scores_kernel, layer_size, offsets, places),
            out_shape=[
                jax.ShapeDtypeStruct((len(offsets), rows, count), BF16 if k else F32)
                for k in range(layer_size)
            ],
            in_specs=[vmem] * 3 + [anywhere] * len(after),
            out_specs=[vmem] * layer_size,
            scratch_shapes=[pltpu.VMEM((tokens, count), F32)],
            compiler_params=params,
            cost_estimate=pl.CostEstimate(
                flops=2 * len(offsets) * tokens * entries * count,
                bytes_accessed=2 * count * entries,
                transcendentals=0,
            ),
            name="scores",
        )(weights, mine, theirs, *after)
        return own, [
            lax.ppermute(block, "layer", [(l, (l + k) % layer_size) for l in range(layer_size)])
            for k, block in enumerate(away, 1)
        ]

    def summed(which, offset, own, others, after):
        return pl.pallas_call(
            functools.partial(layers_kernel, layer_size, which),
            out_shape=jax.ShapeDtypeStruct((rows, count), BF16 if offset else F32),
            in_specs=[vmem] * layer_size + [anywhere] * len(after),
            out_specs=vmem,
            compiler_params=params,
            name="layers",
        )(own, *others, *after)

    terms, after = {}, []
    for offsets in (far, near):
        own, others = scored(offsets, after)
        terms.update({offset: (which, offset, own, others) for which, offset in enumerate(offsets)})
        after = [own]
    arrived, after = {}, []
    for offset in (*far, *near):
        block = summed(*terms[offset], after)
        after = [block]
        arrived[offset] = exchange(block, offset) if offset else block

    total = pl.pallas_call(
        functools.partial(place_kernel, train_size),
        out_shape=jax.ShapeDtypeStruct((rows * train_size, count), F32),
        in_specs=[vmem] * train_size,
        out_specs=vmem,
        compiler_params=params,
        name="place",
    )(*[arrived[offset] for offset in reversed(range(train_size))])
    return total.reshape(rows, train_size, 1, count)


def solution(mesh):
    placed = (
        P("layer", ("parts", "train"), None),
        P("layer", ("parts", "train"), None),
        P("layer", None, None),
        P("layer", None, None),
        P("layer", None, None),
        P("layer", None, None),
        P("layer", None, None),
        P("layer", ("parts", "train", "sub"), None),
    )
    return jax.shard_map(
        body,
        mesh=mesh,
        in_specs=placed,
        out_specs=P(("parts", "train", "layer"), None, "sub", None),
        check_vma=False,
    )
```

```python
import functools

import jax
import jax.numpy as jnp
from jax import lax
from jax.experimental import pallas as pl
from jax.experimental.pallas import tpu as pltpu
from jax.sharding import PartitionSpec as P

F32 = jnp.float32
BF16 = jnp.bfloat16
PACK = 4


def nt(left, right):
    return lax.dot_general(left, right, (((1,), (1,)), ((), ())), preferred_element_type=F32)


def two_terms(matrix):
    high = matrix.astype(BF16)
    return jnp.concatenate([high, (matrix - high.astype(F32)).astype(BF16)], axis=1)


def block_diagonal(matrix):
    rank = matrix.shape[0]
    wide = jnp.concatenate([matrix] * PACK, axis=1)
    tall = jnp.concatenate([wide] * PACK, axis=0)
    rows = lax.broadcasted_iota(jnp.int32, tall.shape, 0) // rank
    columns = lax.broadcasted_iota(jnp.int32, tall.shape, 1) // rank
    return jnp.where(rows == columns, tall, 0.0)


def features_kernel(chunks, *refs):
    sides, (feats, rows, proj, basis, sems) = (refs[0:3], refs[3:6]), refs[6:]
    core = lax.axis_index("sub")
    step = rows.shape[0] // chunks

    def copies(side):
        rows_hbm, proj_hbm, basis_hbm = side
        pairs = [(proj_hbm.at[0], proj)]
        for chunk in range(chunks):
            part = pl.ds(chunk * step, step)
            pairs.append((rows_hbm.at[0, part], rows.at[part]))
        pairs.append((basis_hbm.at[0], basis))
        return [pltpu.make_async_copy(*pair, sems.at[i]) for i, pair in enumerate(pairs)]

    for number, side in enumerate(sides):
        @pl.when(core == number)
        def _():
            for copy in copies(side):
                copy.start()

    waits = copies(sides[0])
    waits[0].wait()
    totals = []
    for chunk in range(chunks):
        waits[1 + chunk].wait()
        totals.append(nt(proj[...], rows[chunk * step:(chunk + 1) * step, :]).astype(BF16))
    total = jnp.concatenate(totals, axis=1)
    waits[-1].wait()
    feats[...] = jnp.dot(
        two_terms(basis[...].T),
        jnp.concatenate([total] * 2, axis=0),
        preferred_element_type=F32,
    ).astype(BF16)


def pack_kernel(count, *refs):
    for i, ref in enumerate(refs[:count]):
        refs[-1][i] = ref[...]


def score_block(side_in, side_out, weights):
    rank, tokens = side_in.shape
    side_in = side_in.astype(F32)
    side_out = side_out.reshape(rank // 16, 16, tokens)
    total = None
    for part in range(rank // PACK):
        products = []
        for b in range(part * PACK, (part + 1) * PACK):
            row = jnp.broadcast_to(side_in[b:b + 1, :], (16, tokens)).astype(BF16)
            products.append((side_out * row[None]).reshape(rank, tokens))
        width = PACK * rank
        term = jnp.dot(
            weights[:, part * width:(part + 1) * width],
            jnp.concatenate(products, axis=0),
            preferred_element_type=F32,
        )
        total = term if total is None else total + term
    return total.T


def queries_kernel(queries, basis_in, basis_out, eigen, *refs):
    weights, half = refs[-2:]
    rank = basis_in.shape[0]
    width = PACK * rank
    groups = rank // PACK
    right = block_diagonal(basis_in[...].T).astype(BF16)
    for part in range(groups):
        half[part * width:(part + 1) * width, :] = nt(
            right, queries[:, part * width:(part + 1) * width]
        )
    left = block_diagonal(basis_out[...]).astype(BF16)
    spectrum = eigen[...]
    inverse = (1.0 / (spectrum + 0.1 * jnp.mean(spectrum))).T
    for part in range(groups):
        columns = range(part * PACK, (part + 1) * PACK)
        matrix = jnp.concatenate(
            [half[pl.ds(b, rank, stride=rank), :] for b in columns], axis=0
        )
        turned = jnp.dot(matrix.T.astype(BF16), left, preferred_element_type=F32)
        scale = jnp.concatenate([inverse[b:b + 1, :] for b in columns], axis=1)
        weights[:, part * width:(part + 1) * width] = (turned * scale).astype(BF16)


def scores_kernel(layer_size, offsets, places, weights, mine, theirs, *refs):
    own, away, scores = refs[-layer_size - 1], refs[-layer_size:-1], refs[-1]
    layer, core = lax.axis_index("layer"), lax.axis_index("sub")
    rows = own.shape[1]
    for i, (offset, place) in enumerate(zip(offsets, places)):
        here, there = mine[place], theirs[place]
        mine_in = (core == 0) == (offset == 0)
        scores[...] = score_block(
            jnp.where(mine_in, here, there), jnp.where(mine_in, there, here), weights
        )
        for k, block in enumerate((own, *away)):
            first = pl.multiple_of(lax.rem(layer + k, layer_size) * rows, rows)
            block[i] = scores[pl.ds(first, rows), :].astype(block.dtype)


def layers_kernel(layer_size, which, own, *refs):
    total = own[which]
    for other in refs[:layer_size - 1]:
        total = total + other[which].astype(F32)
    refs[-1][...] = total.astype(refs[-1].dtype)


def place_kernel(train_size, *refs):
    arrived, out = refs[:-1], refs[-1]
    here = lax.axis_index("train")
    for offset, block in enumerate(reversed(arrived)):
        out[pl.ds(here ^ offset, block.shape[0], stride=train_size), :] = block[...].astype(F32)


def body(inputs, out_grads, proj_in, proj_out, basis_in, basis_out, eigen, queries):
    train_size, layer_size = lax.axis_size("train"), lax.axis_size("layer")
    tokens, width = inputs.shape[1:]
    count, entries = queries.shape[1:]
    rank = proj_in.shape[1]
    chunks = 2
    vmem, hbm = pl.BlockSpec(memory_space=pltpu.VMEM), pl.BlockSpec(memory_space=pltpu.HBM)
    anywhere = pl.BlockSpec(memory_space=pl.ANY)
    params = pltpu.CompilerParams(vmem_limit_bytes=32 << 20)

    sources = (inputs, proj_in, basis_in, out_grads, proj_out, basis_out)
    feats = pl.pallas_call(
        functools.partial(features_kernel, chunks),
        out_shape=jax.ShapeDtypeStruct((rank, tokens), BF16),
        in_specs=[hbm] * len(sources),
        out_specs=vmem,
        scratch_shapes=[
            pltpu.VMEM((tokens, width), BF16),
            pltpu.VMEM((rank, width), BF16),
            pltpu.VMEM((rank, rank), F32),
            pltpu.SemaphoreType.DMA((chunks + 2,)),
        ],
        compiler_params=params,
        cost_estimate=pl.CostEstimate(
            flops=2 * tokens * rank * width, bytes_accessed=2 * width * (tokens + rank), transcendentals=0
        ),
        name="features",
    )(*[pltpu.with_memory_space_constraint(value, pltpu.HBM) for value in sources])

    def exchange(value, offset):
        return lax.ppermute(value, "train", [(j, j ^ offset) for j in range(train_size)])

    def exchange_across(value, offset):
        pairs = [(2 * j + s, 2 * (j ^ offset) + 1 - s) for j in range(train_size) for s in range(2)]
        return lax.ppermute(value, ("train", "sub"), pairs)

    middle = train_size // 2
    far, near = tuple(range(train_size - 1, middle - 1, -1)), tuple(range(middle))
    gathered = {offset: exchange_across(feats, offset) for offset in range(train_size - 1, 0, -1)}
    gathered[0] = feats

    weights = pl.pallas_call(
        queries_kernel,
        out_shape=jax.ShapeDtypeStruct((count, entries), BF16),
        in_specs=[vmem] * 4,
        out_specs=vmem,
        scratch_shapes=[pltpu.VMEM((entries, count), F32)],
        compiler_params=params,
        cost_estimate=pl.CostEstimate(
            flops=4 * PACK * count * entries * rank, bytes_accessed=4 * count * entries, transcendentals=0
        ),
        name="queries",
    )(queries[0], basis_in[0], basis_out[0], eigen[0])

    order = (*near, *far)
    mine = pl.pallas_call(
        functools.partial(pack_kernel, len(order)),
        out_shape=jax.ShapeDtypeStruct((len(order), rank, tokens), BF16),
        in_specs=[vmem] * len(order) + [anywhere],
        out_specs=vmem,
        compiler_params=params,
        name="pack",
    )(*[gathered[offset] for offset in order], weights)
    theirs = lax.ppermute(mine, "sub", [(0, 1), (1, 0)])

    rows = tokens // layer_size

    def scored(offsets, after):
        places = [order.index(offset) for offset in offsets]
        own, *away = pl.pallas_call(
            functools.partial(scores_kernel, layer_size, offsets, places),
            out_shape=[
                jax.ShapeDtypeStruct((len(offsets), rows, count), BF16 if k else F32)
                for k in range(layer_size)
            ],
            in_specs=[vmem] * 3 + [anywhere] * len(after),
            out_specs=[vmem] * layer_size,
            scratch_shapes=[pltpu.VMEM((tokens, count), F32)],
            compiler_params=params,
            cost_estimate=pl.CostEstimate(
                flops=2 * len(offsets) * tokens * entries * count,
                bytes_accessed=2 * count * entries,
                transcendentals=0,
            ),
            name="scores",
        )(weights, mine, theirs, *after)
        return own, [
            lax.ppermute(block, "layer", [(l, (l + k) % layer_size) for l in range(layer_size)])
            for k, block in enumerate(away, 1)
        ]

    def summed(which, offset, own, others, after):
        return pl.pallas_call(
            functools.partial(layers_kernel, layer_size, which),
            out_shape=jax.ShapeDtypeStruct((rows, count), BF16 if offset else F32),
            in_specs=[vmem] * layer_size + [anywhere] * len(after),
            out_specs=vmem,
            compiler_params=params,
            name="layers",
        )(own, *others, *after)

    terms, after = {}, []
    for offsets in (far, near):
        own, others = scored(offsets, after)
        terms.update({offset: (which, offset, own, others) for which, offset in enumerate(offsets)})
        after = [own]
    arrived, after = {}, []
    for offset in (*far, *near):
        block = summed(*terms[offset], after)
        after = [block]
        arrived[offset] = exchange(block, offset) if offset else block

    total = pl.pallas_call(
        functools.partial(place_kernel, train_size),
        out_shape=jax.ShapeDtypeStruct((rows * train_size, count), F32),
        in_specs=[vmem] * train_size,
        out_specs=vmem,
        compiler_params=params,
        name="place",
    )(*[arrived[offset] for offset in reversed(range(train_size))])
    return total.reshape(rows, train_size, 1, count)


def solution(mesh):
    placed = (
        P("layer", ("parts", "train"), None),
        P("layer", ("parts", "train"), None),
        P("layer", None, None),
        P("layer", None, None),
        P("layer", None, None),
        P("layer", None, None),
        P("layer", None, None),
        P("layer", ("parts", "train", "sub"), None),
    )
    return jax.shard_map(
        body,
        mesh=mesh,
        in_specs=placed,
        out_specs=P(("parts", "train", "layer"), None, "sub", None),
        check_vma=False,
    )
```

```python
import functools

import jax
import jax.numpy as jnp
from jax import lax
from jax.experimental import pallas as pl
from jax.experimental.pallas import tpu as pltpu
from jax.sharding import PartitionSpec as P

F32 = jnp.float32
BF16 = jnp.bfloat16
PACK = 4


def nt(left, right):
    return lax.dot_general(left, right, (((1,), (1,)), ((), ())), preferred_element_type=F32)


def two_terms(matrix):
    high = matrix.astype(BF16)
    return jnp.concatenate([high, (matrix - high.astype(F32)).astype(BF16)], axis=1)


def block_diagonal(matrix):
    rank = matrix.shape[0]
    wide = jnp.concatenate([matrix] * PACK, axis=1)
    tall = jnp.concatenate([wide] * PACK, axis=0)
    rows = lax.broadcasted_iota(jnp.int32, tall.shape, 0) // rank
    columns = lax.broadcasted_iota(jnp.int32, tall.shape, 1) // rank
    return jnp.where(rows == columns, tall, 0.0)


def features_kernel(chunks, *refs):
    sides, (feats, rows, proj, basis, sems) = (refs[0:3], refs[3:6]), refs[6:]
    core = lax.axis_index("sub")
    step = rows.shape[1] // chunks

    def copies(side):
        rows_hbm, proj_hbm, basis_hbm = side
        pairs = [(proj_hbm.at[0], proj)]
        for chunk in range(chunks):
            part = pl.ds(chunk * step, step)
            pairs.append((rows_hbm.at[0, :, part], rows.at[:, part]))
        pairs.append((basis_hbm.at[0], basis))
        return [pltpu.make_async_copy(*pair, sems.at[i]) for i, pair in enumerate(pairs)]

    for number, side in enumerate(sides):
        @pl.when(core == number)
        def _():
            for copy in copies(side):
                copy.start()

    waits = copies(sides[0])
    waits[0].wait()
    total = None
    for chunk in range(chunks):
        waits[1 + chunk].wait()
        columns = slice(chunk * step, (chunk + 1) * step)
        term = nt(rows[:, columns], proj[:, columns])
        total = term if total is None else total + term
    waits[-1].wait()
    feats[...] = nt(
        two_terms(basis[...].T), jnp.concatenate([total.astype(BF16)] * 2, axis=1)
    ).astype(BF16)


def pack_kernel(count, *refs):
    for i, ref in enumerate(refs[:count]):
        refs[-1][i] = ref[...]


def score_block(side_in, side_out, weights):
    rank, tokens = side_in.shape
    side_in = side_in.astype(F32)
    side_out = side_out.reshape(rank // 16, 16, tokens)
    total = None
    for part in range(rank // PACK):
        products = []
        for b in range(part * PACK, (part + 1) * PACK):
            row = jnp.broadcast_to(side_in[b:b + 1, :], (16, tokens)).astype(BF16)
            products.append((side_out * row[None]).reshape(rank, tokens))
        width = PACK * rank
        term = jnp.dot(
            weights[:, part * width:(part + 1) * width],
            jnp.concatenate(products, axis=0),
            preferred_element_type=F32,
        )
        total = term if total is None else total + term
    return total.T


def queries_kernel(queries, basis_in, basis_out, eigen, *refs):
    weights, half = refs[-2:]
    rank = basis_in.shape[0]
    width = PACK * rank
    groups = rank // PACK
    right = block_diagonal(basis_in[...].T).astype(BF16)
    for part in range(groups):
        half[part * width:(part + 1) * width, :] = nt(
            right, queries[:, part * width:(part + 1) * width]
        )
    left = block_diagonal(basis_out[...]).astype(BF16)
    spectrum = eigen[...]
    inverse = (1.0 / (spectrum + 0.1 * jnp.mean(spectrum))).T
    for part in range(groups):
        columns = range(part * PACK, (part + 1) * PACK)
        matrix = jnp.concatenate(
            [half[pl.ds(b, rank, stride=rank), :] for b in columns], axis=0
        )
        turned = jnp.dot(matrix.T.astype(BF16), left, preferred_element_type=F32)
        scale = jnp.concatenate([inverse[b:b + 1, :] for b in columns], axis=1)
        weights[:, part * width:(part + 1) * width] = (turned * scale).astype(BF16)


def scores_kernel(layer_size, offsets, places, weights, mine, theirs, *refs):
    own, away, scores = refs[-layer_size - 1], refs[-layer_size:-1], refs[-1]
    layer, core = lax.axis_index("layer"), lax.axis_index("sub")
    rows = own.shape[1]
    for i, (offset, place) in enumerate(zip(offsets, places)):
        here, there = mine[place], theirs[place]
        mine_in = (core == 0) == (offset == 0)
        scores[...] = score_block(
            jnp.where(mine_in, here, there), jnp.where(mine_in, there, here), weights
        )
        for k, block in enumerate((own, *away)):
            first = pl.multiple_of(lax.rem(layer + k, layer_size) * rows, rows)
            block[i] = scores[pl.ds(first, rows), :].astype(block.dtype)


def layers_kernel(layer_size, which, own, *refs):
    total = own[which]
    for other in refs[:layer_size - 1]:
        total = total + other[which].astype(F32)
    refs[-1][...] = total.astype(refs[-1].dtype)


def place_kernel(train_size, *refs):
    arrived, out = refs[:-1], refs[-1]
    here = lax.axis_index("train")
    for offset, block in enumerate(reversed(arrived)):
        out[pl.ds(here ^ offset, block.shape[0], stride=train_size), :] = block[...].astype(F32)


def body(inputs, out_grads, proj_in, proj_out, basis_in, basis_out, eigen, queries):
    train_size, layer_size = lax.axis_size("train"), lax.axis_size("layer")
    tokens, width = inputs.shape[1:]
    count, entries = queries.shape[1:]
    rank = proj_in.shape[1]
    chunks = 2
    vmem, hbm = pl.BlockSpec(memory_space=pltpu.VMEM), pl.BlockSpec(memory_space=pltpu.HBM)
    anywhere = pl.BlockSpec(memory_space=pl.ANY)
    params = pltpu.CompilerParams(vmem_limit_bytes=32 << 20)

    sources = (inputs, proj_in, basis_in, out_grads, proj_out, basis_out)
    feats = pl.pallas_call(
        functools.partial(features_kernel, chunks),
        out_shape=jax.ShapeDtypeStruct((rank, tokens), BF16),
        in_specs=[hbm] * len(sources),
        out_specs=vmem,
        scratch_shapes=[
            pltpu.VMEM((tokens, width), BF16),
            pltpu.VMEM((rank, width), BF16),
            pltpu.VMEM((rank, rank), F32),
            pltpu.SemaphoreType.DMA((chunks + 2,)),
        ],
        compiler_params=params,
        cost_estimate=pl.CostEstimate(
            flops=2 * tokens * rank * width, bytes_accessed=2 * width * (tokens + rank), transcendentals=0
        ),
        name="features",
    )(*[pltpu.with_memory_space_constraint(value, pltpu.HBM) for value in sources])

    def exchange(value, offset):
        return lax.ppermute(value, "train", [(j, j ^ offset) for j in range(train_size)])

    def exchange_across(value, offset):
        pairs = [(2 * j + s, 2 * (j ^ offset) + 1 - s) for j in range(train_size) for s in range(2)]
        return lax.ppermute(value, ("train", "sub"), pairs)

    middle = train_size // 2
    far, near = tuple(range(train_size - 1, middle - 1, -1)), tuple(range(middle))
    gathered = {offset: exchange_across(feats, offset) for offset in range(train_size - 1, 0, -1)}
    gathered[0] = feats

    weights = pl.pallas_call(
        queries_kernel,
        out_shape=jax.ShapeDtypeStruct((count, entries), BF16),
        in_specs=[vmem] * 4,
        out_specs=vmem,
        scratch_shapes=[pltpu.VMEM((entries, count), F32)],
        compiler_params=params,
        cost_estimate=pl.CostEstimate(
            flops=4 * PACK * count * entries * rank, bytes_accessed=4 * count * entries, transcendentals=0
        ),
        name="queries",
    )(queries[0], basis_in[0], basis_out[0], eigen[0])

    order = (*near, *far)
    mine = pl.pallas_call(
        functools.partial(pack_kernel, len(order)),
        out_shape=jax.ShapeDtypeStruct((len(order), rank, tokens), BF16),
        in_specs=[vmem] * len(order) + [anywhere],
        out_specs=vmem,
        compiler_params=params,
        name="pack",
    )(*[gathered[offset] for offset in order], weights)
    theirs = lax.ppermute(mine, "sub", [(0, 1), (1, 0)])

    rows = tokens // layer_size

    def scored(offsets, after):
        places = [order.index(offset) for offset in offsets]
        own, *away = pl.pallas_call(
            functools.partial(scores_kernel, layer_size, offsets, places),
            out_shape=[
                jax.ShapeDtypeStruct((len(offsets), rows, count), BF16 if k else F32)
                for k in range(layer_size)
            ],
            in_specs=[vmem] * 3 + [anywhere] * len(after),
            out_specs=[vmem] * layer_size,
            scratch_shapes=[pltpu.VMEM((tokens, count), F32)],
            compiler_params=params,
            cost_estimate=pl.CostEstimate(
                flops=2 * len(offsets) * tokens * entries * count,
                bytes_accessed=2 * count * entries,
                transcendentals=0,
            ),
            name="scores",
        )(weights, mine, theirs, *after)
        return own, [
            lax.ppermute(block, "layer", [(l, (l + k) % layer_size) for l in range(layer_size)])
            for k, block in enumerate(away, 1)
        ]

    def summed(which, offset, own, others, after):
        return pl.pallas_call(
            functools.partial(layers_kernel, layer_size, which),
            out_shape=jax.ShapeDtypeStruct((rows, count), BF16 if offset else F32),
            in_specs=[vmem] * layer_size + [anywhere] * len(after),
            out_specs=vmem,
            compiler_params=params,
            name="layers",
        )(own, *others, *after)

    terms, after = {}, []
    for offsets in (far, near):
        own, others = scored(offsets, after)
        terms.update({offset: (which, offset, own, others) for which, offset in enumerate(offsets)})
        after = [own]
    arrived, after = {}, []
    for offset in (*far, *near):
        block = summed(*terms[offset], after)
        after = [block]
        arrived[offset] = exchange(block, offset) if offset else block

    total = pl.pallas_call(
        functools.partial(place_kernel, train_size),
        out_shape=jax.ShapeDtypeStruct((rows * train_size, count), F32),
        in_specs=[vmem] * train_size,
        out_specs=vmem,
        compiler_params=params,
        name="place",
    )(*[arrived[offset] for offset in reversed(range(train_size))])
    return total.reshape(rows, train_size, 1, count)


def solution(mesh):
    placed = (
        P("layer", ("parts", "train"), None),
        P("layer", ("parts", "train"), None),
        P("layer", None, None),
        P("layer", None, None),
        P("layer", None, None),
        P("layer", None, None),
        P("layer", None, None),
        P("layer", ("parts", "train", "sub"), None),
    )
    return jax.shard_map(
        body,
        mesh=mesh,
        in_specs=placed,
        out_specs=P(("parts", "train", "layer"), None, "sub", None),
        check_vma=False,
    )
```

```python
import functools

import jax
import jax.numpy as jnp
from jax import lax
from jax.experimental import pallas as pl
from jax.experimental.pallas import tpu as pltpu
from jax.sharding import PartitionSpec as P

F32 = jnp.float32
BF16 = jnp.bfloat16
PACK = 4


def plan(train_size):
    if train_size == 4:
        return FEATURE_ROUNDS, SCORE_ROUNDS, FIRST
    rounds = [
        tuple((j, j ^ offset) for j in range(train_size)) for offset in range(train_size - 1, 0, -1)
    ]
    return rounds, rounds, train_size // 2


FEATURE_ROUNDS = [((0, 2), (1, 3), (2, 0), (3, 1)), ((0, 3), (1, 2), (2, 1), (3, 0)), ((0, 1), (1, 0), (2, 3), (3, 2))]
SCORE_ROUNDS = [((0, 1), (1, 2), (2, 3), (3, 0)), ((0, 2), (1, 3), (2, 0), (3, 1)), ((0, 3), (1, 0), (2, 1), (3, 2))]
FIRST = 2


def lookup(index, values):
    found = jnp.int32(values[0])
    for place, value in enumerate(values[1:], 1):
        found = jnp.where(index == place, jnp.int32(value), found)
    return found


def sources_of(pairs, train_size):
    return [next((s for s, d in pairs if d == j), -1) for j in range(train_size)]


def nt(left, right):
    return lax.dot_general(left, right, (((1,), (1,)), ((), ())), preferred_element_type=F32)


def two_terms(matrix):
    high = matrix.astype(BF16)
    return jnp.concatenate([high, (matrix - high.astype(F32)).astype(BF16)], axis=1)


def block_diagonal(matrix):
    rank = matrix.shape[0]
    wide = jnp.concatenate([matrix] * PACK, axis=1)
    tall = jnp.concatenate([wide] * PACK, axis=0)
    rows = lax.broadcasted_iota(jnp.int32, tall.shape, 0) // rank
    columns = lax.broadcasted_iota(jnp.int32, tall.shape, 1) // rank
    return jnp.where(rows == columns, tall, 0.0)


def features_kernel(chunks, *refs):
    sides, (queries_hbm, eigen_hbm) = (refs[0:3], refs[3:6]), refs[6:8]
    feats, queries, eigen, basis_in, basis_out, rows, proj, sems = refs[8:]
    core = lax.axis_index("sub")
    step = rows.shape[1] // chunks

    def part(chunk):
        return pl.ds(chunk * step, step)

    for side, (rows_hbm, proj_hbm, _) in enumerate(sides):
        @pl.when(core == side)
        def _():
            for chunk in range(chunks):
                for number, (source, target) in enumerate(((proj_hbm, proj), (rows_hbm, rows))):
                    pltpu.make_async_copy(
                        source.at[0, :, part(chunk)], target.at[:, part(chunk)], sems.at[number, chunk]
                    ).start()

    others = [
        pltpu.make_async_copy(source.at[0], target, sems.at[2 + number, 0])
        for number, (source, target) in enumerate((
            (sides[0][2], basis_in), (sides[1][2], basis_out), (eigen_hbm, eigen), (queries_hbm, queries)
        ))
    ]
    for copy in others:
        copy.start()
    total = None
    for chunk in range(chunks):
        for number, (source, target) in enumerate(((sides[0][1], proj), (sides[0][0], rows))):
            pltpu.make_async_copy(
                source.at[0, :, part(chunk)], target.at[:, part(chunk)], sems.at[number, chunk]
            ).wait()
        columns = slice(chunk * step, (chunk + 1) * step)
        term = nt(proj[:, columns], rows[:, columns])
        total = term if total is None else total + term
    for copy in others:
        copy.wait()
    basis = jnp.where(core == 0, basis_in[...], basis_out[...])
    feats[...] = jnp.dot(
        two_terms(basis.T),
        jnp.concatenate([total.astype(BF16)] * 2, axis=0),
        preferred_element_type=F32,
    ).astype(BF16)


def pack_kernel(rounds, *refs):
    own, arrivals, out = refs[0], refs[1:1 + len(rounds)], refs[-1]
    train_size = out.shape[0]
    here = lax.axis_index("train")
    out[here] = own[...]
    for pairs, arrival in zip(rounds, arrivals):
        sources = sources_of(pairs, train_size)
        source = lookup(here, sources)
        if min(sources) >= 0:
            out[source] = arrival[...]
        else:
            @pl.when(source >= 0)
            def _():
                out[source] = arrival[...]


def score_block(side_in, side_out, weights):
    rank, tokens = side_in.shape
    side_in = side_in.astype(F32)
    side_out = side_out.reshape(rank // 16, 16, tokens)
    total = None
    for part in range(rank // PACK):
        products = []
        for b in range(part * PACK, (part + 1) * PACK):
            row = jnp.broadcast_to(side_in[b:b + 1, :], (16, tokens)).astype(BF16)
            products.append((side_out * row[None]).reshape(rank, tokens))
        width = PACK * rank
        term = jnp.dot(
            weights[:, part * width:(part + 1) * width],
            jnp.concatenate(products, axis=0),
            preferred_element_type=F32,
        )
        total = term if total is None else total + term
    return total.T


def queries_kernel(queries, basis_in, basis_out, eigen, *refs):
    weights, half = refs[-2:]
    rank = basis_in.shape[0]
    width = PACK * rank
    groups = rank // PACK
    right = block_diagonal(basis_in[...].T).astype(BF16)
    for part in range(groups):
        half[part * width:(part + 1) * width, :] = nt(
            right, queries[:, part * width:(part + 1) * width]
        )
    left = block_diagonal(basis_out[...]).astype(BF16)
    spectrum = eigen[...]
    inverse = (1.0 / (spectrum + 0.1 * jnp.mean(spectrum))).T
    for part in range(groups):
        columns = range(part * PACK, (part + 1) * PACK)
        matrix = jnp.concatenate(
            [half[pl.ds(b, rank, stride=rank), :] for b in columns], axis=0
        )
        turned = jnp.dot(matrix.T.astype(BF16), left, preferred_element_type=F32)
        scale = jnp.concatenate([inverse[b:b + 1, :] for b in columns], axis=1)
        weights[:, part * width:(part + 1) * width] = (turned * scale).astype(BF16)


def scores_kernel(layer_size, targets, weights, mine, theirs, *refs):
    own, away, scores = refs[-layer_size - 1], refs[-layer_size:-1], refs[-1]
    place, layer, core = (lax.axis_index(name) for name in ("train", "layer", "sub"))
    rows = own.shape[1]
    for i, target in enumerate(targets):
        slot = lookup(place, target)
        here, there = mine[slot], theirs[slot]
        mine_in = (core == 0) == (slot == place)
        scores[...] = score_block(
            jnp.where(mine_in, here, there), jnp.where(mine_in, there, here), weights
        )
        for k, block in enumerate((own, *away)):
            first = pl.multiple_of(lax.rem(layer + k, layer_size) * rows, rows)
            block[i] = scores[pl.ds(first, rows), :].astype(block.dtype)


def layers_kernel(layer_size, places, own, *refs):
    which = places[0] if len(set(places)) == 1 else lookup(lax.axis_index("train"), places)
    total = own[which]
    for other in refs[:layer_size - 1]:
        total = total + other[which].astype(F32)
    refs[-1][...] = total.astype(refs[-1].dtype)


def keep_kernel(block, *refs):
    refs[-1][...] = block[...]


def place_kernel(train_size, rounds, own, *refs):
    arrivals, out = refs[:-1], refs[-1]
    here = lax.axis_index("train")
    rows = own.shape[0]
    out[pl.ds(here, rows, stride=train_size), :] = own[...]
    for pairs, arrival in zip(rounds, arrivals):
        sources = sources_of(pairs, train_size)
        source = lookup(here, sources)
        if min(sources) >= 0:
            out[pl.ds(source, rows, stride=train_size), :] = arrival[...].astype(F32)
        else:
            @pl.when(source >= 0)
            def _():
                out[pl.ds(source, rows, stride=train_size), :] = arrival[...].astype(F32)


def body(inputs, out_grads, proj_in, proj_out, basis_in, basis_out, eigen, queries):
    train_size, layer_size = lax.axis_size("train"), lax.axis_size("layer")
    tokens, width = inputs.shape[1:]
    count, entries = queries.shape[1:]
    rank = proj_in.shape[1]
    chunks = 1
    vmem, hbm = pl.BlockSpec(memory_space=pltpu.VMEM), pl.BlockSpec(memory_space=pltpu.HBM)
    anywhere = pl.BlockSpec(memory_space=pl.ANY)
    params = pltpu.CompilerParams(vmem_limit_bytes=32 << 20)

    sources = (inputs, proj_in, basis_in, out_grads, proj_out, basis_out, queries, eigen)
    feats, queries, eigen, basis_in, basis_out = pl.pallas_call(
        functools.partial(features_kernel, chunks),
        out_shape=[
            jax.ShapeDtypeStruct((rank, tokens), BF16),
            jax.ShapeDtypeStruct((count, entries), BF16),
            *[jax.ShapeDtypeStruct((rank, rank), F32)] * 3,
        ],
        in_specs=[hbm] * len(sources),
        out_specs=[vmem] * 5,
        scratch_shapes=[
            pltpu.VMEM((tokens, width), BF16),
            pltpu.VMEM((rank, width), BF16),
            pltpu.SemaphoreType.DMA((6, chunks)),
        ],
        compiler_params=params,
        cost_estimate=pl.CostEstimate(
            flops=2 * tokens * rank * width, bytes_accessed=2 * width * (tokens + rank), transcendentals=0
        ),
        name="features",
    )(*[pltpu.with_memory_space_constraint(value, pltpu.HBM) for value in sources])

    feature_rounds, score_rounds, first = plan(train_size)

    def kept(block, after):
        return pl.pallas_call(
            keep_kernel,
            out_shape=jax.ShapeDtypeStruct(block.shape, block.dtype),
            in_specs=[vmem] + [anywhere] * len(after),
            out_specs=vmem,
            compiler_params=params,
            name="keep",
        )(block, *after)

    def in_order(blocks):
        ordered = []
        for block in blocks[:-1]:
            ordered.append(kept(block, ordered[-1:]))
        return ordered + blocks[-1:]

    def across(pairs):
        cores = [(2 * s + c, 2 * d + 1 - c) for s, d in pairs for c in range(2)]
        return lax.ppermute(feats, ("train", "sub"), cores)

    gathered = [across(pairs) for pairs in feature_rounds]

    weights = pl.pallas_call(
        queries_kernel,
        out_shape=jax.ShapeDtypeStruct((count, entries), BF16),
        in_specs=[vmem] * 4,
        out_specs=vmem,
        scratch_shapes=[pltpu.VMEM((entries, count), F32)],
        compiler_params=params,
        cost_estimate=pl.CostEstimate(
            flops=4 * PACK * count * entries * rank, bytes_accessed=4 * count * entries, transcendentals=0
        ),
        name="queries",
    )(queries, basis_in, basis_out, eigen)

    mine = pl.pallas_call(
        functools.partial(pack_kernel, feature_rounds[::-1]),
        out_shape=jax.ShapeDtypeStruct((train_size, rank, tokens), BF16),
        in_specs=[vmem] * (1 + len(gathered)) + [anywhere],
        out_specs=vmem,
        compiler_params=params,
        name="pack",
    )(feats, *gathered[::-1], weights)
    theirs = lax.ppermute(mine, "sub", [(0, 1), (1, 0)])

    rows = tokens // layer_size

    def scored(targets, after):
        own, *away = pl.pallas_call(
            functools.partial(scores_kernel, layer_size, targets),
            out_shape=[
                jax.ShapeDtypeStruct((len(targets), rows, count), BF16 if k else F32)
                for k in range(layer_size)
            ],
            in_specs=[vmem] * 3 + [anywhere] * len(after),
            out_specs=[vmem] * layer_size,
            scratch_shapes=[pltpu.VMEM((tokens, count), F32)],
            compiler_params=params,
            cost_estimate=pl.CostEstimate(
                flops=2 * len(targets) * tokens * entries * count,
                bytes_accessed=2 * count * entries,
                transcendentals=0,
            ),
            name="scores",
        )(weights, mine, theirs, *after)
        return own, [
            lax.ppermute(block, "layer", [(l, (l + k) % layer_size) for l in range(layer_size)])
            for k, block in enumerate(away, 1)
        ]

    def summed(places, dtype, own, others, after):
        return pl.pallas_call(
            functools.partial(layers_kernel, layer_size, places),
            out_shape=jax.ShapeDtypeStruct((rows, count), dtype),
            in_specs=[vmem] * layer_size + [anywhere] * len(after),
            out_specs=vmem,
            compiler_params=params,
            name="layers",
        )(own, *others, *after)

    def table(rounds, lead):
        lists = [lead(j) + [d for pairs in rounds for s, d in pairs if s == j] for j in range(train_size)]
        length = max(len(targets) for targets in lists)
        return lists, [
            [targets[i] if i < len(targets) else j for j, targets in enumerate(lists)] for i in range(length)
        ]

    first_lists, first_targets = table(score_rounds[:first], lambda j: [])
    last_lists, last_targets = table(score_rounds[first:], lambda j: [j])
    first_terms = scored(first_targets, [])
    last_terms = scored(last_targets, first_terms[:1])
    arrivals, after = [], []
    for number, pairs in enumerate(score_rounds):
        lists, terms = (first_lists, first_terms) if number < first else (last_lists, last_terms)
        if number == first:
            home = summed([0] * train_size, F32, *last_terms, after)
            after = [home]
        targets = dict(pairs)
        places = [lists[j].index(targets[j]) if j in targets else 0 for j in range(train_size)]
        block = summed(places, BF16, *terms, after)
        after = [block]
        arrivals.append(lax.ppermute(block, "train", pairs))
    if first >= len(score_rounds):
        home = summed([0] * train_size, F32, *last_terms, after)

    total = pl.pallas_call(
        functools.partial(place_kernel, train_size, score_rounds),
        out_shape=jax.ShapeDtypeStruct((rows * train_size, count), F32),
        in_specs=[vmem] * (1 + len(arrivals)),
        out_specs=vmem,
        compiler_params=params,
        name="place",
    )(home, *in_order(arrivals))
    return total.reshape(rows, train_size, 1, count)


def solution(mesh):
    placed = (
        P("layer", ("parts", "train"), None),
        P("layer", ("parts", "train"), None),
        P("layer", None, None),
        P("layer", None, None),
        P("layer", None, None),
        P("layer", None, None),
        P("layer", None, None),
        P("layer", ("parts", "train", "sub"), None),
    )
    return jax.shard_map(
        body,
        mesh=mesh,
        in_specs=placed,
        out_specs=P(("parts", "train", "layer"), None, "sub", None),
        check_vma=False,
    )
```

```python
import functools

import jax
import jax.numpy as jnp
from jax import lax
from jax.experimental import pallas as pl
from jax.experimental.pallas import tpu as pltpu
from jax.sharding import PartitionSpec as P

F32 = jnp.float32
BF16 = jnp.bfloat16
PACK = 4


def plan(train_size):
    if train_size == 4:
        return FEATURE_ROUNDS, SCORE_ROUNDS, FIRST
    rounds = [
        tuple((j, j ^ offset) for j in range(train_size)) for offset in range(train_size - 1, 0, -1)
    ]
    return rounds, rounds, train_size // 2


FEATURE_ROUNDS = [((0, 2), (1, 3), (2, 0), (3, 1)), ((0, 3), (1, 2), (2, 1), (3, 0)), ((0, 1), (1, 0), (2, 3), (3, 2))]
SCORE_ROUNDS = [((0, 1), (1, 2), (2, 3), (3, 0)), ((0, 2), (1, 3), (2, 0), (3, 1)), ((0, 3), (1, 0), (2, 1), (3, 2))]
FIRST = 2


def lookup(index, values):
    found = jnp.int32(values[0])
    for place, value in enumerate(values[1:], 1):
        found = jnp.where(index == place, jnp.int32(value), found)
    return found


def sources_of(pairs, train_size):
    return [next((s for s, d in pairs if d == j), -1) for j in range(train_size)]


def nt(left, right):
    return lax.dot_general(left, right, (((1,), (1,)), ((), ())), preferred_element_type=F32)


def two_terms(matrix):
    high = matrix.astype(BF16)
    return jnp.concatenate([high, (matrix - high.astype(F32)).astype(BF16)], axis=1)


def block_diagonal(matrix):
    rank = matrix.shape[0]
    wide = jnp.concatenate([matrix] * PACK, axis=1)
    tall = jnp.concatenate([wide] * PACK, axis=0)
    rows = lax.broadcasted_iota(jnp.int32, tall.shape, 0) // rank
    columns = lax.broadcasted_iota(jnp.int32, tall.shape, 1) // rank
    return jnp.where(rows == columns, tall, 0.0)


def features_kernel(chunks, *refs):
    sides, eigen_hbm = (refs[0:3], refs[3:6]), refs[6]
    feats, eigen, basis_in, basis_out, rows, proj, sems = refs[7:]
    core = lax.axis_index("sub")
    step = rows.shape[1] // chunks

    def part(chunk):
        return pl.ds(chunk * step, step)

    for side, (rows_hbm, proj_hbm, _) in enumerate(sides):
        @pl.when(core == side)
        def _():
            for chunk in range(chunks):
                for number, (source, target) in enumerate(((proj_hbm, proj), (rows_hbm, rows))):
                    pltpu.make_async_copy(
                        source.at[0, :, part(chunk)], target.at[:, part(chunk)], sems.at[number, chunk]
                    ).start()

    others = [
        pltpu.make_async_copy(source.at[0], target, sems.at[2 + number, 0])
        for number, (source, target) in enumerate((
            (sides[0][2], basis_in), (sides[1][2], basis_out), (eigen_hbm, eigen)
        ))
    ]
    for copy in others:
        copy.start()
    total = None
    for chunk in range(chunks):
        for number, (source, target) in enumerate(((sides[0][1], proj), (sides[0][0], rows))):
            pltpu.make_async_copy(
                source.at[0, :, part(chunk)], target.at[:, part(chunk)], sems.at[number, chunk]
            ).wait()
        columns = slice(chunk * step, (chunk + 1) * step)
        term = nt(proj[:, columns], rows[:, columns])
        total = term if total is None else total + term
    for copy in others:
        copy.wait()
    basis = jnp.where(core == 0, basis_in[...], basis_out[...])
    feats[...] = jnp.dot(
        two_terms(basis.T),
        jnp.concatenate([total.astype(BF16)] * 2, axis=0),
        preferred_element_type=F32,
    ).astype(BF16)


def pack_kernel(rounds, *refs):
    own, arrivals, out = refs[0], refs[1:1 + len(rounds)], refs[-1]
    train_size = out.shape[0]
    here = lax.axis_index("train")
    out[here] = own[...]
    for pairs, arrival in zip(rounds, arrivals):
        sources = sources_of(pairs, train_size)
        source = lookup(here, sources)
        if min(sources) >= 0:
            out[source] = arrival[...]
        else:
            @pl.when(source >= 0)
            def _():
                out[source] = arrival[...]


def score_block(side_in, side_out, weights):
    rank, tokens = side_in.shape
    side_in = side_in.astype(F32)
    side_out = side_out.reshape(rank // 16, 16, tokens)
    total = None
    for part in range(rank // PACK):
        products = []
        for b in range(part * PACK, (part + 1) * PACK):
            row = jnp.broadcast_to(side_in[b:b + 1, :], (16, tokens)).astype(BF16)
            products.append((side_out * row[None]).reshape(rank, tokens))
        width = PACK * rank
        term = jnp.dot(
            weights[:, part * width:(part + 1) * width],
            jnp.concatenate(products, axis=0),
            preferred_element_type=F32,
        )
        total = term if total is None else total + term
    return total.T


def queries_kernel(pieces, queries_hbm, basis_in, basis_out, eigen, weights, queries, half, sems):
    rank = basis_in.shape[0]
    width = PACK * rank
    groups = rank // PACK
    step = queries.shape[1] // pieces
    copies = []
    for piece in range(pieces):
        columns = pl.ds(piece * step, step)
        copies.append(
            pltpu.make_async_copy(queries_hbm.at[0, :, columns], queries.at[:, columns], sems.at[piece])
        )
        copies[-1].start()
    right = block_diagonal(basis_in[...].T).astype(BF16)
    for part in range(groups):
        if part * width % step == 0:
            copies[part * width // step].wait()
        half[part * width:(part + 1) * width, :] = nt(
            right, queries[:, part * width:(part + 1) * width]
        )
    left = block_diagonal(basis_out[...]).astype(BF16)
    spectrum = eigen[...]
    inverse = (1.0 / (spectrum + 0.1 * jnp.mean(spectrum))).T
    for part in range(groups):
        columns = range(part * PACK, (part + 1) * PACK)
        matrix = jnp.concatenate(
            [half[pl.ds(b, rank, stride=rank), :] for b in columns], axis=0
        )
        turned = jnp.dot(matrix.T.astype(BF16), left, preferred_element_type=F32)
        scale = jnp.concatenate([inverse[b:b + 1, :] for b in columns], axis=1)
        weights[:, part * width:(part + 1) * width] = (turned * scale).astype(BF16)


def scores_kernel(layer_size, targets, weights, mine, theirs, *refs):
    own, away, scores = refs[-layer_size - 1], refs[-layer_size:-1], refs[-1]
    place, layer, core = (lax.axis_index(name) for name in ("train", "layer", "sub"))
    rows = own.shape[1]
    for i, target in enumerate(targets):
        slot = lookup(place, target)
        here, there = mine[slot], theirs[slot]
        mine_in = (core == 0) == (slot == place)
        scores[...] = score_block(
            jnp.where(mine_in, here, there), jnp.where(mine_in, there, here), weights
        )
        for k, block in enumerate((own, *away)):
            first = pl.multiple_of(lax.rem(layer + k, layer_size) * rows, rows)
            block[i] = scores[pl.ds(first, rows), :].astype(block.dtype)


def layers_kernel(layer_size, places, own, *refs):
    which = places[0] if len(set(places)) == 1 else lookup(lax.axis_index("train"), places)
    total = own[which]
    for other in refs[:layer_size - 1]:
        total = total + other[which].astype(F32)
    refs[-1][...] = total.astype(refs[-1].dtype)


def keep_kernel(block, *refs):
    refs[-1][...] = block[...]


def place_kernel(train_size, rounds, own, *refs):
    arrivals, out = refs[:-1], refs[-1]
    here = lax.axis_index("train")
    rows = own.shape[0]
    out[pl.ds(here, rows, stride=train_size), :] = own[...]
    for pairs, arrival in zip(rounds, arrivals):
        sources = sources_of(pairs, train_size)
        source = lookup(here, sources)
        if min(sources) >= 0:
            out[pl.ds(source, rows, stride=train_size), :] = arrival[...].astype(F32)
        else:
            @pl.when(source >= 0)
            def _():
                out[pl.ds(source, rows, stride=train_size), :] = arrival[...].astype(F32)


def body(inputs, out_grads, proj_in, proj_out, basis_in, basis_out, eigen, queries):
    train_size, layer_size = lax.axis_size("train"), lax.axis_size("layer")
    tokens, width = inputs.shape[1:]
    count, entries = queries.shape[1:]
    rank = proj_in.shape[1]
    chunks = 1
    vmem, hbm = pl.BlockSpec(memory_space=pltpu.VMEM), pl.BlockSpec(memory_space=pltpu.HBM)
    anywhere = pl.BlockSpec(memory_space=pl.ANY)
    params = pltpu.CompilerParams(vmem_limit_bytes=32 << 20)

    sources = (inputs, proj_in, basis_in, out_grads, proj_out, basis_out, eigen)
    feats, eigen, basis_in, basis_out = pl.pallas_call(
        functools.partial(features_kernel, chunks),
        out_shape=[
            jax.ShapeDtypeStruct((rank, tokens), BF16),
            *[jax.ShapeDtypeStruct((rank, rank), F32)] * 3,
        ],
        in_specs=[hbm] * len(sources),
        out_specs=[vmem] * 4,
        scratch_shapes=[
            pltpu.VMEM((tokens, width), BF16),
            pltpu.VMEM((rank, width), BF16),
            pltpu.SemaphoreType.DMA((5, chunks)),
        ],
        compiler_params=params,
        cost_estimate=pl.CostEstimate(
            flops=2 * tokens * rank * width, bytes_accessed=2 * width * (tokens + rank), transcendentals=0
        ),
        name="features",
    )(*[pltpu.with_memory_space_constraint(value, pltpu.HBM) for value in sources])

    feature_rounds, score_rounds, first = plan(train_size)

    def kept(block, after):
        return pl.pallas_call(
            keep_kernel,
            out_shape=jax.ShapeDtypeStruct(block.shape, block.dtype),
            in_specs=[vmem] + [anywhere] * len(after),
            out_specs=vmem,
            compiler_params=params,
            name="keep",
        )(block, *after)

    def in_order(blocks):
        ordered = []
        for block in blocks[:-1]:
            ordered.append(kept(block, ordered[-1:]))
        return ordered + blocks[-1:]

    def across(pairs):
        cores = [(2 * s + c, 2 * d + 1 - c) for s, d in pairs for c in range(2)]
        return lax.ppermute(feats, ("train", "sub"), cores)

    gathered = [across(pairs) for pairs in feature_rounds]

    pieces = 4
    weights = pl.pallas_call(
        functools.partial(queries_kernel, pieces),
        out_shape=jax.ShapeDtypeStruct((count, entries), BF16),
        in_specs=[hbm] + [vmem] * 3,
        out_specs=vmem,
        scratch_shapes=[
            pltpu.VMEM((count, entries), BF16),
            pltpu.VMEM((entries, count), F32),
            pltpu.SemaphoreType.DMA((pieces,)),
        ],
        compiler_params=params,
        cost_estimate=pl.CostEstimate(
            flops=4 * PACK * count * entries * rank, bytes_accessed=4 * count * entries, transcendentals=0
        ),
        name="queries",
    )(pltpu.with_memory_space_constraint(queries, pltpu.HBM), basis_in, basis_out, eigen)

    mine = pl.pallas_call(
        functools.partial(pack_kernel, feature_rounds),
        out_shape=jax.ShapeDtypeStruct((train_size, rank, tokens), BF16),
        in_specs=[vmem] * (1 + len(gathered)) + [anywhere],
        out_specs=vmem,
        compiler_params=params,
        name="pack",
    )(feats, *gathered, weights)
    theirs = lax.ppermute(mine, "sub", [(0, 1), (1, 0)])

    rows = tokens // layer_size

    def scored(targets, after):
        own, *away = pl.pallas_call(
            functools.partial(scores_kernel, layer_size, targets),
            out_shape=[
                jax.ShapeDtypeStruct((len(targets), rows, count), BF16 if k else F32)
                for k in range(layer_size)
            ],
            in_specs=[vmem] * 3 + [anywhere] * len(after),
            out_specs=[vmem] * layer_size,
            scratch_shapes=[pltpu.VMEM((tokens, count), F32)],
            compiler_params=params,
            cost_estimate=pl.CostEstimate(
                flops=2 * len(targets) * tokens * entries * count,
                bytes_accessed=2 * count * entries,
                transcendentals=0,
            ),
            name="scores",
        )(weights, mine, theirs, *after)
        return own, [
            lax.ppermute(block, "layer", [(l, (l + k) % layer_size) for l in range(layer_size)])
            for k, block in enumerate(away, 1)
        ]

    def summed(places, dtype, own, others, after):
        return pl.pallas_call(
            functools.partial(layers_kernel, layer_size, places),
            out_shape=jax.ShapeDtypeStruct((rows, count), dtype),
            in_specs=[vmem] * layer_size + [anywhere] * len(after),
            out_specs=vmem,
            compiler_params=params,
            name="layers",
        )(own, *others, *after)

    def table(rounds, lead):
        lists = [lead(j) + [d for pairs in rounds for s, d in pairs if s == j] for j in range(train_size)]
        length = max(len(targets) for targets in lists)
        return lists, [
            [targets[i] if i < len(targets) else j for j, targets in enumerate(lists)] for i in range(length)
        ]

    first_lists, first_targets = table(score_rounds[:first], lambda j: [])
    last_lists, last_targets = table(score_rounds[first:], lambda j: [j])
    first_terms = scored(first_targets, [])
    last_terms = scored(last_targets, first_terms[:1])
    arrivals, after = [], []
    for number, pairs in enumerate(score_rounds):
        lists, terms = (first_lists, first_terms) if number < first else (last_lists, last_terms)
        if number == first:
            home = summed([0] * train_size, F32, *last_terms, after)
            after = [home]
        targets = dict(pairs)
        places = [lists[j].index(targets[j]) if j in targets else 0 for j in range(train_size)]
        block = summed(places, BF16, *terms, after)
        after = [block]
        arrivals.append(lax.ppermute(block, "train", pairs))
    if first >= len(score_rounds):
        home = summed([0] * train_size, F32, *last_terms, after)

    total = pl.pallas_call(
        functools.partial(place_kernel, train_size, score_rounds),
        out_shape=jax.ShapeDtypeStruct((rows * train_size, count), F32),
        in_specs=[vmem] * (1 + len(arrivals)),
        out_specs=vmem,
        compiler_params=params,
        name="place",
    )(home, *in_order(arrivals))
    return total.reshape(rows, train_size, 1, count)


def solution(mesh):
    placed = (
        P("layer", ("parts", "train"), None),
        P("layer", ("parts", "train"), None),
        P("layer", None, None),
        P("layer", None, None),
        P("layer", None, None),
        P("layer", None, None),
        P("layer", None, None),
        P("layer", ("parts", "train", "sub"), None),
    )
    return jax.shard_map(
        body,
        mesh=mesh,
        in_specs=placed,
        out_specs=P(("parts", "train", "layer"), None, "sub", None),
        check_vma=False,
    )
```

```python
import functools

import jax
import jax.numpy as jnp
from jax import lax
from jax.experimental import pallas as pl
from jax.experimental.pallas import tpu as pltpu
from jax.sharding import PartitionSpec as P

F32 = jnp.float32
BF16 = jnp.bfloat16
PACK = 4


def plan(train_size):
    if train_size == 4:
        return FEATURE_ROUNDS, SCORE_ROUNDS, FIRST
    rounds = [
        tuple((j, j ^ offset) for j in range(train_size)) for offset in range(train_size - 1, 0, -1)
    ]
    return rounds, rounds, train_size // 2


FEATURE_ROUNDS = [((0, 2), (1, 3), (2, 0), (3, 1)), ((0, 3), (1, 2), (2, 1), (3, 0)), ((0, 1), (1, 0), (2, 3), (3, 2))]
SCORE_ROUNDS = [((0, 1), (1, 2), (2, 3), (3, 0)), ((0, 2), (1, 3), (2, 0), (3, 1)), ((0, 3), (1, 0), (2, 1), (3, 2))]
FIRST = 2


def lookup(index, values):
    found = jnp.int32(values[0])
    for place, value in enumerate(values[1:], 1):
        found = jnp.where(index == place, jnp.int32(value), found)
    return found


def sources_of(pairs, train_size):
    return [next((s for s, d in pairs if d == j), -1) for j in range(train_size)]


def nt(left, right):
    return lax.dot_general(left, right, (((1,), (1,)), ((), ())), preferred_element_type=F32)


def two_terms(matrix):
    high = matrix.astype(BF16)
    return jnp.concatenate([high, (matrix - high.astype(F32)).astype(BF16)], axis=1)


def block_diagonal(matrix):
    rank = matrix.shape[0]
    wide = jnp.concatenate([matrix] * PACK, axis=1)
    tall = jnp.concatenate([wide] * PACK, axis=0)
    rows = lax.broadcasted_iota(jnp.int32, tall.shape, 0) // rank
    columns = lax.broadcasted_iota(jnp.int32, tall.shape, 1) // rank
    return jnp.where(rows == columns, tall, 0.0)


def features_kernel(chunks, *refs):
    sides, (queries_hbm, eigen_hbm) = (refs[0:3], refs[3:6]), refs[6:8]
    feats, queries, eigen, basis_in, basis_out, rows, proj, sems = refs[8:]
    core = lax.axis_index("sub")
    step = rows.shape[0] // chunks

    def copies(rows_hbm, proj_hbm):
        pieces = [pl.ds(chunk * step, step) for chunk in range(chunks)]
        pairs = [(rows_hbm.at[0, piece], rows.at[piece]) for piece in pieces]
        pairs.append((proj_hbm.at[0], proj))
        return [pltpu.make_async_copy(*pair, sems.at[0, i]) for i, pair in enumerate(pairs)]

    for side, (rows_hbm, proj_hbm, _) in enumerate(sides):
        @pl.when(core == side)
        def _():
            for copy in copies(rows_hbm, proj_hbm):
                copy.start()

    others = [
        pltpu.make_async_copy(source.at[0], target, sems.at[1, number])
        for number, (source, target) in enumerate((
            (sides[0][2], basis_in), (sides[1][2], basis_out), (eigen_hbm, eigen), (queries_hbm, queries)
        ))
    ]
    for copy in others:
        copy.start()
    for copy in copies(*sides[0][:2]):
        copy.wait()
    total = nt(proj[...], rows[...])
    for copy in others[:2]:
        copy.wait()
    basis = jnp.where(core == 0, basis_in[...], basis_out[...])
    feats[...] = jnp.dot(
        two_terms(basis.T),
        jnp.concatenate([total.astype(BF16)] * 2, axis=0),
        preferred_element_type=F32,
    ).astype(BF16)
    for copy in others[2:]:
        copy.wait()


def pack_kernel(rounds, *refs):
    own, arrivals, out = refs[0], refs[1:1 + len(rounds)], refs[-1]
    train_size = out.shape[0]
    here = lax.axis_index("train")
    out[here] = own[...]
    for pairs, arrival in zip(rounds, arrivals):
        sources = sources_of(pairs, train_size)
        source = lookup(here, sources)
        if min(sources) >= 0:
            out[source] = arrival[...]
        else:
            @pl.when(source >= 0)
            def _():
                out[source] = arrival[...]


def score_block(side_in, side_out, weights):
    rank, tokens = side_in.shape
    side_in = side_in.astype(F32)
    side_out = side_out.reshape(rank // 16, 16, tokens)
    total = None
    for part in range(rank // PACK):
        products = []
        for b in range(part * PACK, (part + 1) * PACK):
            row = jnp.broadcast_to(side_in[b:b + 1, :], (16, tokens)).astype(BF16)
            products.append((side_out * row[None]).reshape(rank, tokens))
        width = PACK * rank
        term = jnp.dot(
            weights[:, part * width:(part + 1) * width],
            jnp.concatenate(products, axis=0),
            preferred_element_type=F32,
        )
        total = term if total is None else total + term
    return total.T


def queries_kernel(queries, basis_in, basis_out, eigen, *refs):
    weights, half = refs[-2:]
    rank = basis_in.shape[0]
    width = PACK * rank
    groups = rank // PACK
    right = block_diagonal(basis_in[...].T).astype(BF16)
    for part in range(groups):
        half[part * width:(part + 1) * width, :] = nt(
            right, queries[:, part * width:(part + 1) * width]
        )
    left = block_diagonal(basis_out[...]).astype(BF16)
    spectrum = eigen[...]
    inverse = (1.0 / (spectrum + 0.1 * jnp.mean(spectrum))).T
    for part in range(groups):
        columns = range(part * PACK, (part + 1) * PACK)
        matrix = jnp.concatenate(
            [half[pl.ds(b, rank, stride=rank), :] for b in columns], axis=0
        )
        turned = jnp.dot(matrix.T.astype(BF16), left, preferred_element_type=F32)
        scale = jnp.concatenate([inverse[b:b + 1, :] for b in columns], axis=1)
        weights[:, part * width:(part + 1) * width] = (turned * scale).astype(BF16)


def scores_kernel(layer_size, targets, weights, mine, theirs, *refs):
    own, away, scores = refs[-layer_size - 1], refs[-layer_size:-1], refs[-1]
    place, layer, core = (lax.axis_index(name) for name in ("train", "layer", "sub"))
    rows = own.shape[1]
    for i, target in enumerate(targets):
        slot = lookup(place, target)
        here, there = mine[slot], theirs[slot]
        mine_in = (core == 0) == (slot == place)
        scores[...] = score_block(
            jnp.where(mine_in, here, there), jnp.where(mine_in, there, here), weights
        )
        for k, block in enumerate((own, *away)):
            first = pl.multiple_of(lax.rem(layer + k, layer_size) * rows, rows)
            block[i] = scores[pl.ds(first, rows), :].astype(block.dtype)


def layers_kernel(layer_size, places, own, *refs):
    which = places[0] if len(set(places)) == 1 else lookup(lax.axis_index("train"), places)
    total = own[which]
    for other in refs[:layer_size - 1]:
        total = total + other[which].astype(F32)
    refs[-1][...] = total.astype(refs[-1].dtype)


def keep_kernel(block, *refs):
    refs[-1][...] = block[...]


def place_kernel(train_size, rounds, own, *refs):
    arrivals, out = refs[:-1], refs[-1]
    here = lax.axis_index("train")
    rows = own.shape[0]
    out[pl.ds(here, rows, stride=train_size), :] = own[...]
    for pairs, arrival in zip(rounds, arrivals):
        sources = sources_of(pairs, train_size)
        source = lookup(here, sources)
        if min(sources) >= 0:
            out[pl.ds(source, rows, stride=train_size), :] = arrival[...].astype(F32)
        else:
            @pl.when(source >= 0)
            def _():
                out[pl.ds(source, rows, stride=train_size), :] = arrival[...].astype(F32)


def body(inputs, out_grads, proj_in, proj_out, basis_in, basis_out, eigen, queries):
    train_size, layer_size = lax.axis_size("train"), lax.axis_size("layer")
    tokens, width = inputs.shape[1:]
    count, entries = queries.shape[1:]
    rank = proj_in.shape[1]
    chunks = 4
    vmem, hbm = pl.BlockSpec(memory_space=pltpu.VMEM), pl.BlockSpec(memory_space=pltpu.HBM)
    anywhere = pl.BlockSpec(memory_space=pl.ANY)
    params = pltpu.CompilerParams(vmem_limit_bytes=32 << 20)

    sources = (inputs, proj_in, basis_in, out_grads, proj_out, basis_out, queries, eigen)
    feats, queries, eigen, basis_in, basis_out = pl.pallas_call(
        functools.partial(features_kernel, chunks),
        out_shape=[
            jax.ShapeDtypeStruct((rank, tokens), BF16),
            jax.ShapeDtypeStruct((count, entries), BF16),
            *[jax.ShapeDtypeStruct((rank, rank), F32)] * 3,
        ],
        in_specs=[hbm] * len(sources),
        out_specs=[vmem] * 5,
        scratch_shapes=[
            pltpu.VMEM((tokens, width), BF16),
            pltpu.VMEM((rank, width), BF16),
            pltpu.SemaphoreType.DMA((2, chunks + 1)),
        ],
        compiler_params=params,
        cost_estimate=pl.CostEstimate(
            flops=2 * tokens * rank * width, bytes_accessed=2 * width * (tokens + rank), transcendentals=0
        ),
        name="features",
    )(*[pltpu.with_memory_space_constraint(value, pltpu.HBM) for value in sources])

    feature_rounds, score_rounds, first = plan(train_size)

    def kept(block, after):
        return pl.pallas_call(
            keep_kernel,
            out_shape=jax.ShapeDtypeStruct(block.shape, block.dtype),
            in_specs=[vmem] + [anywhere] * len(after),
            out_specs=vmem,
            compiler_params=params,
            name="keep",
        )(block, *after)

    def in_order(blocks):
        ordered = []
        for block in blocks[:-1]:
            ordered.append(kept(block, ordered[-1:]))
        return ordered + blocks[-1:]

    def across(pairs):
        cores = [(2 * s + c, 2 * d + 1 - c) for s, d in pairs for c in range(2)]
        return lax.ppermute(feats, ("train", "sub"), cores)

    gathered = [across(pairs) for pairs in feature_rounds]

    weights = pl.pallas_call(
        queries_kernel,
        out_shape=jax.ShapeDtypeStruct((count, entries), BF16),
        in_specs=[vmem] * 4,
        out_specs=vmem,
        scratch_shapes=[pltpu.VMEM((entries, count), F32)],
        compiler_params=params,
        cost_estimate=pl.CostEstimate(
            flops=4 * PACK * count * entries * rank, bytes_accessed=4 * count * entries, transcendentals=0
        ),
        name="queries",
    )(queries, basis_in, basis_out, eigen)

    mine = pl.pallas_call(
        functools.partial(pack_kernel, feature_rounds[::-1]),
        out_shape=jax.ShapeDtypeStruct((train_size, rank, tokens), BF16),
        in_specs=[vmem] * (1 + len(gathered)) + [anywhere],
        out_specs=vmem,
        compiler_params=params,
        name="pack",
    )(feats, *gathered[::-1], weights)
    theirs = lax.ppermute(mine, "sub", [(0, 1), (1, 0)])

    rows = tokens // layer_size

    def scored(targets, after):
        own, *away = pl.pallas_call(
            functools.partial(scores_kernel, layer_size, targets),
            out_shape=[
                jax.ShapeDtypeStruct((len(targets), rows, count), BF16 if k else F32)
                for k in range(layer_size)
            ],
            in_specs=[vmem] * 3 + [anywhere] * len(after),
            out_specs=[vmem] * layer_size,
            scratch_shapes=[pltpu.VMEM((tokens, count), F32)],
            compiler_params=params,
            cost_estimate=pl.CostEstimate(
                flops=2 * len(targets) * tokens * entries * count,
                bytes_accessed=2 * count * entries,
                transcendentals=0,
            ),
            name="scores",
        )(weights, mine, theirs, *after)
        return own, [
            lax.ppermute(block, "layer", [(l, (l + k) % layer_size) for l in range(layer_size)])
            for k, block in enumerate(away, 1)
        ]

    def summed(places, dtype, own, others, after):
        return pl.pallas_call(
            functools.partial(layers_kernel, layer_size, places),
            out_shape=jax.ShapeDtypeStruct((rows, count), dtype),
            in_specs=[vmem] * layer_size + [anywhere] * len(after),
            out_specs=vmem,
            compiler_params=params,
            name="layers",
        )(own, *others, *after)

    def table(rounds, lead):
        lists = [lead(j) + [d for pairs in rounds for s, d in pairs if s == j] for j in range(train_size)]
        length = max(len(targets) for targets in lists)
        return lists, [
            [targets[i] if i < len(targets) else j for j, targets in enumerate(lists)] for i in range(length)
        ]

    first_lists, first_targets = table(score_rounds[:first], lambda j: [])
    last_lists, last_targets = table(score_rounds[first:], lambda j: [j])
    first_terms = scored(first_targets, [])
    last_terms = scored(last_targets, first_terms[:1])
    arrivals, after = [], []
    for number, pairs in enumerate(score_rounds):
        lists, terms = (first_lists, first_terms) if number < first else (last_lists, last_terms)
        if number == first:
            home = summed([0] * train_size, F32, *last_terms, after)
            after = [home]
        targets = dict(pairs)
        places = [lists[j].index(targets[j]) if j in targets else 0 for j in range(train_size)]
        block = summed(places, BF16, *terms, after)
        after = [block]
        arrivals.append(lax.ppermute(block, "train", pairs))
    if first >= len(score_rounds):
        home = summed([0] * train_size, F32, *last_terms, after)

    total = pl.pallas_call(
        functools.partial(place_kernel, train_size, score_rounds),
        out_shape=jax.ShapeDtypeStruct((rows * train_size, count), F32),
        in_specs=[vmem] * (1 + len(arrivals)),
        out_specs=vmem,
        compiler_params=params,
        name="place",
    )(home, *in_order(arrivals))
    return total.reshape(rows, train_size, 1, count)


def solution(mesh):
    placed = (
        P("layer", ("parts", "train"), None),
        P("layer", ("parts", "train"), None),
        P("layer", None, None),
        P("layer", None, None),
        P("layer", None, None),
        P("layer", None, None),
        P("layer", None, None),
        P("layer", ("parts", "train", "sub"), None),
    )
    return jax.shard_map(
        body,
        mesh=mesh,
        in_specs=placed,
        out_specs=P(("parts", "train", "layer"), None, "sub", None),
        check_vma=False,
    )
```

```python
import functools

import jax
import jax.numpy as jnp
from jax import lax
from jax.experimental import pallas as pl
from jax.experimental.pallas import tpu as pltpu
from jax.sharding import PartitionSpec as P

F32 = jnp.float32
BF16 = jnp.bfloat16
PACK = 4


def plan(train_size):
    if train_size == 4:
        return FEATURE_ROUNDS, SCORE_ROUNDS, FIRST
    rounds = [
        tuple((j, j ^ offset) for j in range(train_size)) for offset in range(train_size - 1, 0, -1)
    ]
    return rounds, rounds, train_size // 2


FEATURE_ROUNDS = [((0, 2), (1, 3), (2, 0), (3, 1)), ((0, 3), (1, 2), (2, 1), (3, 0)), ((0, 1), (1, 0), (2, 3), (3, 2))]
SCORE_ROUNDS = [((0, 1), (1, 2), (2, 3), (3, 0)), ((0, 2), (1, 3), (2, 0), (3, 1)), ((0, 3), (1, 0), (2, 1), (3, 2))]
FIRST = 2


def lookup(index, values):
    found = jnp.int32(values[0])
    for place, value in enumerate(values[1:], 1):
        found = jnp.where(index == place, jnp.int32(value), found)
    return found


def sources_of(pairs, train_size):
    return [next((s for s, d in pairs if d == j), -1) for j in range(train_size)]


def nt(left, right):
    return lax.dot_general(left, right, (((1,), (1,)), ((), ())), preferred_element_type=F32)


def two_terms(matrix):
    high = matrix.astype(BF16)
    return jnp.concatenate([high, (matrix - high.astype(F32)).astype(BF16)], axis=1)


def block_diagonal(matrix):
    rank = matrix.shape[0]
    wide = jnp.concatenate([matrix] * PACK, axis=1)
    tall = jnp.concatenate([wide] * PACK, axis=0)
    rows = lax.broadcasted_iota(jnp.int32, tall.shape, 0) // rank
    columns = lax.broadcasted_iota(jnp.int32, tall.shape, 1) // rank
    return jnp.where(rows == columns, tall, 0.0)


def features_kernel(chunks, *refs):
    sides, (queries_hbm, eigen_hbm) = (refs[0:3], refs[3:6]), refs[6:8]
    feats, queries, eigen, basis_in, basis_out, rows, proj, sems = refs[8:]
    core = lax.axis_index("sub")
    step = rows.shape[0] // chunks

    def copies(rows_hbm, proj_hbm):
        pieces = [pl.ds(chunk * step, step) for chunk in range(chunks)]
        pairs = [(rows_hbm.at[0, piece], rows.at[piece]) for piece in pieces]
        pairs.append((proj_hbm.at[0], proj))
        return [pltpu.make_async_copy(*pair, sems.at[0, i]) for i, pair in enumerate(pairs)]

    for side, (rows_hbm, proj_hbm, _) in enumerate(sides):
        @pl.when(core == side)
        def _():
            for copy in copies(rows_hbm, proj_hbm):
                copy.start()

    others = [
        pltpu.make_async_copy(source.at[0], target, sems.at[1, number])
        for number, (source, target) in enumerate((
            (sides[0][2], basis_in), (sides[1][2], basis_out), (eigen_hbm, eigen), (queries_hbm, queries)
        ))
    ]
    for copy in others:
        copy.start()
    for copy in copies(*sides[0][:2]):
        copy.wait()
    total = nt(proj[...], rows[...])
    for copy in others[:2]:
        copy.wait()
    basis = jnp.where(core == 0, basis_in[...], basis_out[...])
    feats[...] = jnp.dot(
        two_terms(basis.T),
        jnp.concatenate([total.astype(BF16)] * 2, axis=0),
        preferred_element_type=F32,
    ).astype(BF16)
    for copy in others[2:]:
        copy.wait()


def pack_kernel(rounds, *refs):
    own, arrivals, out = refs[0], refs[1:1 + len(rounds)], refs[-1]
    train_size = out.shape[0]
    here = lax.axis_index("train")
    out[here] = own[...]
    for pairs, arrival in zip(rounds, arrivals):
        sources = sources_of(pairs, train_size)
        source = lookup(here, sources)
        if min(sources) >= 0:
            out[source] = arrival[...]
        else:
            @pl.when(source >= 0)
            def _():
                out[source] = arrival[...]


def score_block(side_in, side_out, weights):
    rank, tokens = side_in.shape
    side_in = side_in.astype(F32)
    side_out = side_out.reshape(rank // 16, 16, tokens)
    total = None
    span = rank // 4
    for part in range(4):
        products = []
        for b in range(part * span, (part + 1) * span):
            row = jnp.broadcast_to(side_in[b:b + 1, :], (16, tokens)).astype(BF16)
            products.append((side_out * row[None]).reshape(rank, tokens))
        width = span * rank
        term = jnp.dot(
            weights[:, part * width:(part + 1) * width],
            jnp.concatenate(products, axis=0),
            preferred_element_type=F32,
        )
        total = term if total is None else total + term
    return total.T


def queries_kernel(queries, basis_in, basis_out, eigen, *refs):
    weights, half = refs[-2:]
    rank = basis_in.shape[0]
    width = PACK * rank
    groups = rank // PACK
    right = block_diagonal(basis_in[...].T).astype(BF16)
    for part in range(groups):
        half[part * width:(part + 1) * width, :] = nt(
            right, queries[:, part * width:(part + 1) * width]
        )
    left = block_diagonal(basis_out[...]).astype(BF16)
    spectrum = eigen[...]
    inverse = (1.0 / (spectrum + 0.1 * jnp.mean(spectrum))).T
    for part in range(groups):
        columns = range(part * PACK, (part + 1) * PACK)
        matrix = jnp.concatenate(
            [half[pl.ds(b, rank, stride=rank), :] for b in columns], axis=0
        )
        turned = jnp.dot(matrix.T.astype(BF16), left, preferred_element_type=F32)
        scale = jnp.concatenate([inverse[b:b + 1, :] for b in columns], axis=1)
        weights[:, part * width:(part + 1) * width] = (turned * scale).astype(BF16)


def scores_kernel(layer_size, targets, weights, mine, theirs, *refs):
    own, away, scores = refs[-layer_size - 1], refs[-layer_size:-1], refs[-1]
    place, layer, core = (lax.axis_index(name) for name in ("train", "layer", "sub"))
    rows = own.shape[1]
    for i, target in enumerate(targets):
        slot = lookup(place, target)
        here, there = mine[slot], theirs[slot]
        mine_in = (core == 0) == (slot == place)
        scores[...] = score_block(
            jnp.where(mine_in, here, there), jnp.where(mine_in, there, here), weights
        )
        for k, block in enumerate((own, *away)):
            first = pl.multiple_of(lax.rem(layer + k, layer_size) * rows, rows)
            block[i] = scores[pl.ds(first, rows), :].astype(block.dtype)


def layers_kernel(layer_size, places, own, *refs):
    which = places[0] if len(set(places)) == 1 else lookup(lax.axis_index("train"), places)
    total = own[which]
    for other in refs[:layer_size - 1]:
        total = total + other[which].astype(F32)
    refs[-1][...] = total.astype(refs[-1].dtype)


def keep_kernel(block, *refs):
    refs[-1][...] = block[...]


def place_kernel(train_size, rounds, own, *refs):
    arrivals, out = refs[:-1], refs[-1]
    here = lax.axis_index("train")
    rows = own.shape[0]
    out[pl.ds(here, rows, stride=train_size), :] = own[...]
    for pairs, arrival in zip(rounds, arrivals):
        sources = sources_of(pairs, train_size)
        source = lookup(here, sources)
        if min(sources) >= 0:
            out[pl.ds(source, rows, stride=train_size), :] = arrival[...].astype(F32)
        else:
            @pl.when(source >= 0)
            def _():
                out[pl.ds(source, rows, stride=train_size), :] = arrival[...].astype(F32)


def body(inputs, out_grads, proj_in, proj_out, basis_in, basis_out, eigen, queries):
    train_size, layer_size = lax.axis_size("train"), lax.axis_size("layer")
    tokens, width = inputs.shape[1:]
    count, entries = queries.shape[1:]
    rank = proj_in.shape[1]
    chunks = 4
    vmem, hbm = pl.BlockSpec(memory_space=pltpu.VMEM), pl.BlockSpec(memory_space=pltpu.HBM)
    anywhere = pl.BlockSpec(memory_space=pl.ANY)
    params = pltpu.CompilerParams(vmem_limit_bytes=32 << 20)

    sources = (inputs, proj_in, basis_in, out_grads, proj_out, basis_out, queries, eigen)
    feats, queries, eigen, basis_in, basis_out = pl.pallas_call(
        functools.partial(features_kernel, chunks),
        out_shape=[
            jax.ShapeDtypeStruct((rank, tokens), BF16),
            jax.ShapeDtypeStruct((count, entries), BF16),
            *[jax.ShapeDtypeStruct((rank, rank), F32)] * 3,
        ],
        in_specs=[hbm] * len(sources),
        out_specs=[vmem] * 5,
        scratch_shapes=[
            pltpu.VMEM((tokens, width), BF16),
            pltpu.VMEM((rank, width), BF16),
            pltpu.SemaphoreType.DMA((2, chunks + 1)),
        ],
        compiler_params=params,
        cost_estimate=pl.CostEstimate(
            flops=2 * tokens * rank * width, bytes_accessed=2 * width * (tokens + rank), transcendentals=0
        ),
        name="features",
    )(*[pltpu.with_memory_space_constraint(value, pltpu.HBM) for value in sources])

    feature_rounds, score_rounds, first = plan(train_size)

    def kept(block, after):
        return pl.pallas_call(
            keep_kernel,
            out_shape=jax.ShapeDtypeStruct(block.shape, block.dtype),
            in_specs=[vmem] + [anywhere] * len(after),
            out_specs=vmem,
            compiler_params=params,
            name="keep",
        )(block, *after)

    def in_order(blocks):
        ordered = []
        for block in blocks[:-1]:
            ordered.append(kept(block, ordered[-1:]))
        return ordered + blocks[-1:]

    def across(pairs):
        cores = [(2 * s + c, 2 * d + 1 - c) for s, d in pairs for c in range(2)]
        return lax.ppermute(feats, ("train", "sub"), cores)

    gathered = [across(pairs) for pairs in feature_rounds]

    weights = pl.pallas_call(
        queries_kernel,
        out_shape=jax.ShapeDtypeStruct((count, entries), BF16),
        in_specs=[vmem] * 4,
        out_specs=vmem,
        scratch_shapes=[pltpu.VMEM((entries, count), F32)],
        compiler_params=params,
        cost_estimate=pl.CostEstimate(
            flops=4 * PACK * count * entries * rank, bytes_accessed=4 * count * entries, transcendentals=0
        ),
        name="queries",
    )(queries, basis_in, basis_out, eigen)

    mine = pl.pallas_call(
        functools.partial(pack_kernel, feature_rounds[::-1]),
        out_shape=jax.ShapeDtypeStruct((train_size, rank, tokens), BF16),
        in_specs=[vmem] * (1 + len(gathered)) + [anywhere],
        out_specs=vmem,
        compiler_params=params,
        name="pack",
    )(feats, *gathered[::-1], weights)
    theirs = lax.ppermute(mine, "sub", [(0, 1), (1, 0)])

    rows = tokens // layer_size

    def scored(targets, after):
        own, *away = pl.pallas_call(
            functools.partial(scores_kernel, layer_size, targets),
            out_shape=[
                jax.ShapeDtypeStruct((len(targets), rows, count), BF16 if k else F32)
                for k in range(layer_size)
            ],
            in_specs=[vmem] * 3 + [anywhere] * len(after),
            out_specs=[vmem] * layer_size,
            scratch_shapes=[pltpu.VMEM((tokens, count), F32)],
            compiler_params=params,
            cost_estimate=pl.CostEstimate(
                flops=2 * len(targets) * tokens * entries * count,
                bytes_accessed=2 * count * entries,
                transcendentals=0,
            ),
            name="scores",
        )(weights, mine, theirs, *after)
        return own, [
            lax.ppermute(block, "layer", [(l, (l + k) % layer_size) for l in range(layer_size)])
            for k, block in enumerate(away, 1)
        ]

    def summed(places, dtype, own, others, after):
        return pl.pallas_call(
            functools.partial(layers_kernel, layer_size, places),
            out_shape=jax.ShapeDtypeStruct((rows, count), dtype),
            in_specs=[vmem] * layer_size + [anywhere] * len(after),
            out_specs=vmem,
            compiler_params=params,
            name="layers",
        )(own, *others, *after)

    def table(rounds, lead):
        lists = [lead(j) + [d for pairs in rounds for s, d in pairs if s == j] for j in range(train_size)]
        length = max(len(targets) for targets in lists)
        return lists, [
            [targets[i] if i < len(targets) else j for j, targets in enumerate(lists)] for i in range(length)
        ]

    first_lists, first_targets = table(score_rounds[:first], lambda j: [])
    last_lists, last_targets = table(score_rounds[first:], lambda j: [j])
    first_terms = scored(first_targets, [])
    last_terms = scored(last_targets, first_terms[:1])
    arrivals, after = [], []
    for number, pairs in enumerate(score_rounds):
        lists, terms = (first_lists, first_terms) if number < first else (last_lists, last_terms)
        if number == first:
            home = summed([0] * train_size, F32, *last_terms, after)
            after = [home]
        targets = dict(pairs)
        places = [lists[j].index(targets[j]) if j in targets else 0 for j in range(train_size)]
        block = summed(places, BF16, *terms, after)
        after = [block]
        arrivals.append(lax.ppermute(block, "train", pairs))
    if first >= len(score_rounds):
        home = summed([0] * train_size, F32, *last_terms, after)

    total = pl.pallas_call(
        functools.partial(place_kernel, train_size, score_rounds),
        out_shape=jax.ShapeDtypeStruct((rows * train_size, count), F32),
        in_specs=[vmem] * (1 + len(arrivals)),
        out_specs=vmem,
        compiler_params=params,
        name="place",
    )(home, *in_order(arrivals))
    return total.reshape(rows, train_size, 1, count)


def solution(mesh):
    placed = (
        P("layer", ("parts", "train"), None),
        P("layer", ("parts", "train"), None),
        P("layer", None, None),
        P("layer", None, None),
        P("layer", None, None),
        P("layer", None, None),
        P("layer", None, None),
        P("layer", ("parts", "train", "sub"), None),
    )
    return jax.shard_map(
        body,
        mesh=mesh,
        in_specs=placed,
        out_specs=P(("parts", "train", "layer"), None, "sub", None),
        check_vma=False,
    )
```

```python
import functools

import jax
import jax.numpy as jnp
from jax import lax
from jax.experimental import pallas as pl
from jax.experimental.pallas import tpu as pltpu
from jax.sharding import PartitionSpec as P

F32 = jnp.float32
BF16 = jnp.bfloat16
PACK = 4


def plan(train_size):
    if train_size == 4:
        return FEATURE_ROUNDS, SCORE_ROUNDS, FIRST
    rounds = [
        tuple((j, j ^ offset) for j in range(train_size)) for offset in range(train_size - 1, 0, -1)
    ]
    return rounds, rounds, train_size // 2


FEATURE_ROUNDS = [
    ((0, 2), (2, 3), (3, 0), (1, 1)),
    ((0, 3), (1, 2), (2, 0), (3, 1)),
    ((1, 3), (2, 1), (3, 2), (0, 0)),
    ((0, 1), (1, 0), (2, 2), (3, 3)),
]
SCORE_ROUNDS = [((0, 1), (1, 2), (2, 3), (3, 0)), ((0, 2), (1, 3), (2, 0), (3, 1)), ((0, 3), (1, 0), (2, 1), (3, 2))]
FIRST = 2


def lookup(index, values):
    found = jnp.int32(values[0])
    for place, value in enumerate(values[1:], 1):
        found = jnp.where(index == place, jnp.int32(value), found)
    return found


def sources_of(pairs, train_size):
    return [next((s for s, d in pairs if d == j), -1) for j in range(train_size)]


def nt(left, right):
    return lax.dot_general(left, right, (((1,), (1,)), ((), ())), preferred_element_type=F32)


def two_terms(matrix):
    high = matrix.astype(BF16)
    return jnp.concatenate([high, (matrix - high.astype(F32)).astype(BF16)], axis=1)


def block_diagonal(matrix):
    rank = matrix.shape[0]
    wide = jnp.concatenate([matrix] * PACK, axis=1)
    tall = jnp.concatenate([wide] * PACK, axis=0)
    rows = lax.broadcasted_iota(jnp.int32, tall.shape, 0) // rank
    columns = lax.broadcasted_iota(jnp.int32, tall.shape, 1) // rank
    return jnp.where(rows == columns, tall, 0.0)


def features_kernel(chunks, *refs):
    sides, (queries_hbm, eigen_hbm) = (refs[0:3], refs[3:6]), refs[6:8]
    feats, queries, eigen, basis_in, basis_out, rows, proj, sems = refs[8:]
    core = lax.axis_index("sub")
    step = rows.shape[0] // chunks

    def copies(rows_hbm, proj_hbm):
        pieces = [pl.ds(chunk * step, step) for chunk in range(chunks)]
        pairs = [(rows_hbm.at[0, piece], rows.at[piece]) for piece in pieces]
        pairs.append((proj_hbm.at[0], proj))
        return [pltpu.make_async_copy(*pair, sems.at[0, i]) for i, pair in enumerate(pairs)]

    for side, (rows_hbm, proj_hbm, _) in enumerate(sides):
        @pl.when(core == side)
        def _():
            for copy in copies(rows_hbm, proj_hbm):
                copy.start()

    others = [
        pltpu.make_async_copy(source.at[0], target, sems.at[1, number])
        for number, (source, target) in enumerate((
            (sides[0][2], basis_in), (sides[1][2], basis_out), (eigen_hbm, eigen), (queries_hbm, queries)
        ))
    ]
    for copy in others:
        copy.start()
    for copy in copies(*sides[0][:2]):
        copy.wait()
    total = nt(proj[...], rows[...])
    for copy in others[:2]:
        copy.wait()
    basis = jnp.where(core == 0, basis_in[...], basis_out[...])
    feats[...] = jnp.dot(
        two_terms(basis.T),
        jnp.concatenate([total.astype(BF16)] * 2, axis=0),
        preferred_element_type=F32,
    ).astype(BF16)
    for copy in others[2:]:
        copy.wait()


def pack_kernel(rounds, *refs):
    own, arrivals, out = refs[0], refs[1:1 + len(rounds)], refs[-1]
    train_size = out.shape[0]
    here = lax.axis_index("train")
    out[here] = own[...]
    for pairs, arrival in zip(rounds, arrivals):
        sources = sources_of(pairs, train_size)
        source = lookup(here, sources)
        if min(sources) >= 0:
            out[source] = arrival[...]
        else:
            @pl.when(source >= 0)
            def _():
                out[source] = arrival[...]


def score_block(side_in, side_out, weights):
    rank, tokens = side_in.shape
    side_in = side_in.astype(F32)
    side_out = side_out.reshape(rank // 16, 16, tokens)
    total = None
    span = rank // 4
    for part in range(4):
        products = []
        for b in range(part * span, (part + 1) * span):
            row = jnp.broadcast_to(side_in[b:b + 1, :], (16, tokens)).astype(BF16)
            products.append((side_out * row[None]).reshape(rank, tokens))
        width = span * rank
        term = jnp.dot(
            weights[:, part * width:(part + 1) * width],
            jnp.concatenate(products, axis=0),
            preferred_element_type=F32,
        )
        total = term if total is None else total + term
    return total.T


def queries_kernel(queries, basis_in, basis_out, eigen, *refs):
    weights, half = refs[-2:]
    rank = basis_in.shape[0]
    width = PACK * rank
    groups = rank // PACK
    right = block_diagonal(basis_in[...].T).astype(BF16)
    for part in range(groups):
        half[part * width:(part + 1) * width, :] = nt(
            right, queries[:, part * width:(part + 1) * width]
        )
    left = block_diagonal(basis_out[...]).astype(BF16)
    spectrum = eigen[...]
    inverse = (1.0 / (spectrum + 0.1 * jnp.mean(spectrum))).T
    for part in range(groups):
        columns = range(part * PACK, (part + 1) * PACK)
        matrix = jnp.concatenate(
            [half[pl.ds(b, rank, stride=rank), :] for b in columns], axis=0
        )
        turned = jnp.dot(matrix.T.astype(BF16), left, preferred_element_type=F32)
        scale = jnp.concatenate([inverse[b:b + 1, :] for b in columns], axis=1)
        weights[:, part * width:(part + 1) * width] = (turned * scale).astype(BF16)


def scores_kernel(layer_size, targets, weights, mine, theirs, *refs):
    own, away, scores = refs[-layer_size - 1], refs[-layer_size:-1], refs[-1]
    place, layer, core = (lax.axis_index(name) for name in ("train", "layer", "sub"))
    rows = own.shape[1]
    for i, target in enumerate(targets):
        slot = lookup(place, target)
        here, there = mine[slot], theirs[slot]
        mine_in = (core == 0) == (slot == place)
        scores[...] = score_block(
            jnp.where(mine_in, here, there), jnp.where(mine_in, there, here), weights
        )
        for k, block in enumerate((own, *away)):
            first = pl.multiple_of(lax.rem(layer + k, layer_size) * rows, rows)
            block[i] = scores[pl.ds(first, rows), :].astype(block.dtype)


def layers_kernel(layer_size, places, own, *refs):
    which = places[0] if len(set(places)) == 1 else lookup(lax.axis_index("train"), places)
    total = own[which]
    for other in refs[:layer_size - 1]:
        total = total + other[which].astype(F32)
    refs[-1][...] = total.astype(refs[-1].dtype)


def keep_kernel(block, *refs):
    refs[-1][...] = block[...]


def place_kernel(train_size, rounds, own, *refs):
    arrivals, out = refs[:-1], refs[-1]
    here = lax.axis_index("train")
    rows = own.shape[0]
    out[pl.ds(here, rows, stride=train_size), :] = own[...]
    for pairs, arrival in zip(rounds, arrivals):
        sources = sources_of(pairs, train_size)
        source = lookup(here, sources)
        if min(sources) >= 0:
            out[pl.ds(source, rows, stride=train_size), :] = arrival[...].astype(F32)
        else:
            @pl.when(source >= 0)
            def _():
                out[pl.ds(source, rows, stride=train_size), :] = arrival[...].astype(F32)


def body(inputs, out_grads, proj_in, proj_out, basis_in, basis_out, eigen, queries):
    train_size, layer_size = lax.axis_size("train"), lax.axis_size("layer")
    tokens, width = inputs.shape[1:]
    count, entries = queries.shape[1:]
    rank = proj_in.shape[1]
    chunks = 4
    vmem, hbm = pl.BlockSpec(memory_space=pltpu.VMEM), pl.BlockSpec(memory_space=pltpu.HBM)
    anywhere = pl.BlockSpec(memory_space=pl.ANY)
    params = pltpu.CompilerParams(vmem_limit_bytes=32 << 20)

    sources = (inputs, proj_in, basis_in, out_grads, proj_out, basis_out, queries, eigen)
    feats, queries, eigen, basis_in, basis_out = pl.pallas_call(
        functools.partial(features_kernel, chunks),
        out_shape=[
            jax.ShapeDtypeStruct((rank, tokens), BF16),
            jax.ShapeDtypeStruct((count, entries), BF16),
            *[jax.ShapeDtypeStruct((rank, rank), F32)] * 3,
        ],
        in_specs=[hbm] * len(sources),
        out_specs=[vmem] * 5,
        scratch_shapes=[
            pltpu.VMEM((tokens, width), BF16),
            pltpu.VMEM((rank, width), BF16),
            pltpu.SemaphoreType.DMA((2, chunks + 1)),
        ],
        compiler_params=params,
        cost_estimate=pl.CostEstimate(
            flops=2 * tokens * rank * width, bytes_accessed=2 * width * (tokens + rank), transcendentals=0
        ),
        name="features",
    )(*[pltpu.with_memory_space_constraint(value, pltpu.HBM) for value in sources])

    feature_rounds, score_rounds, first = plan(train_size)

    def kept(block, after):
        return pl.pallas_call(
            keep_kernel,
            out_shape=jax.ShapeDtypeStruct(block.shape, block.dtype),
            in_specs=[vmem] + [anywhere] * len(after),
            out_specs=vmem,
            compiler_params=params,
            name="keep",
        )(block, *after)

    def in_order(blocks):
        ordered = []
        for block in blocks[:-1]:
            ordered.append(kept(block, ordered[-1:]))
        return ordered + blocks[-1:]

    def across(pairs):
        cores = [(2 * s + c, 2 * d + (c if s == d else 1 - c)) for s, d in pairs for c in range(2)]
        return lax.ppermute(feats, ("train", "sub"), cores)

    gathered = [across(pairs) for pairs in feature_rounds]

    weights = pl.pallas_call(
        queries_kernel,
        out_shape=jax.ShapeDtypeStruct((count, entries), BF16),
        in_specs=[vmem] * 4,
        out_specs=vmem,
        scratch_shapes=[pltpu.VMEM((entries, count), F32)],
        compiler_params=params,
        cost_estimate=pl.CostEstimate(
            flops=4 * PACK * count * entries * rank, bytes_accessed=4 * count * entries, transcendentals=0
        ),
        name="queries",
    )(queries, basis_in, basis_out, eigen)

    mine = pl.pallas_call(
        functools.partial(pack_kernel, feature_rounds[::-1]),
        out_shape=jax.ShapeDtypeStruct((train_size, rank, tokens), BF16),
        in_specs=[vmem] * (1 + len(gathered)) + [anywhere],
        out_specs=vmem,
        compiler_params=params,
        name="pack",
    )(feats, *gathered[::-1], weights)
    theirs = lax.ppermute(mine, "sub", [(0, 1), (1, 0)])

    rows = tokens // layer_size

    def scored(targets, after):
        own, *away = pl.pallas_call(
            functools.partial(scores_kernel, layer_size, targets),
            out_shape=[
                jax.ShapeDtypeStruct((len(targets), rows, count), BF16 if k else F32)
                for k in range(layer_size)
            ],
            in_specs=[vmem] * 3 + [anywhere] * len(after),
            out_specs=[vmem] * layer_size,
            scratch_shapes=[pltpu.VMEM((tokens, count), F32)],
            compiler_params=params,
            cost_estimate=pl.CostEstimate(
                flops=2 * len(targets) * tokens * entries * count,
                bytes_accessed=2 * count * entries,
                transcendentals=0,
            ),
            name="scores",
        )(weights, mine, theirs, *after)
        return own, [
            lax.ppermute(block, "layer", [(l, (l + k) % layer_size) for l in range(layer_size)])
            for k, block in enumerate(away, 1)
        ]

    def summed(places, dtype, own, others, after):
        return pl.pallas_call(
            functools.partial(layers_kernel, layer_size, places),
            out_shape=jax.ShapeDtypeStruct((rows, count), dtype),
            in_specs=[vmem] * layer_size + [anywhere] * len(after),
            out_specs=vmem,
            compiler_params=params,
            name="layers",
        )(own, *others, *after)

    def table(rounds, lead):
        lists = [lead(j) + [d for pairs in rounds for s, d in pairs if s == j] for j in range(train_size)]
        length = max(len(targets) for targets in lists)
        return lists, [
            [targets[i] if i < len(targets) else j for j, targets in enumerate(lists)] for i in range(length)
        ]

    first_lists, first_targets = table(score_rounds[:first], lambda j: [])
    last_lists, last_targets = table(score_rounds[first:], lambda j: [j])
    first_terms = scored(first_targets, [])
    last_terms = scored(last_targets, first_terms[:1])
    arrivals, after = [], []
    for number, pairs in enumerate(score_rounds):
        lists, terms = (first_lists, first_terms) if number < first else (last_lists, last_terms)
        if number == first:
            home = summed([0] * train_size, F32, *last_terms, after)
            after = [home]
        targets = dict(pairs)
        places = [lists[j].index(targets[j]) if j in targets else 0 for j in range(train_size)]
        block = summed(places, BF16, *terms, after)
        after = [block]
        arrivals.append(lax.ppermute(block, "train", pairs))
    if first >= len(score_rounds):
        home = summed([0] * train_size, F32, *last_terms, after)

    total = pl.pallas_call(
        functools.partial(place_kernel, train_size, score_rounds),
        out_shape=jax.ShapeDtypeStruct((rows * train_size, count), F32),
        in_specs=[vmem] * (1 + len(arrivals)),
        out_specs=vmem,
        compiler_params=params,
        name="place",
    )(home, *in_order(arrivals))
    return total.reshape(rows, train_size, 1, count)


def solution(mesh):
    placed = (
        P("layer", ("parts", "train"), None),
        P("layer", ("parts", "train"), None),
        P("layer", None, None),
        P("layer", None, None),
        P("layer", None, None),
        P("layer", None, None),
        P("layer", None, None),
        P("layer", ("parts", "train", "sub"), None),
    )
    return jax.shard_map(
        body,
        mesh=mesh,
        in_specs=placed,
        out_specs=P(("parts", "train", "layer"), None, "sub", None),
        check_vma=False,
    )
```

```python
import functools

import jax
import jax.numpy as jnp
from jax import lax
from jax.experimental import pallas as pl
from jax.experimental.pallas import tpu as pltpu
from jax.sharding import PartitionSpec as P

F32 = jnp.float32
BF16 = jnp.bfloat16
PACK = 4


def plan(train_size):
    if train_size == 4:
        return FEATURE_ROUNDS, SCORE_ROUNDS, FIRST
    rounds = [
        tuple((j, j ^ offset) for j in range(train_size)) for offset in range(train_size - 1, 0, -1)
    ]
    return rounds, rounds, train_size // 2


FEATURE_ROUNDS = [((0, 2), (1, 3), (2, 0), (3, 1)), ((0, 3), (1, 2), (2, 1), (3, 0)), ((0, 1), (1, 0), (2, 3), (3, 2))]
SCORE_ROUNDS = [((0, 1), (1, 2), (2, 3), (3, 0)), ((0, 2), (1, 3), (2, 0), (3, 1)), ((0, 3), (1, 0), (2, 1), (3, 2))]
FIRST = 2


def lookup(index, values):
    found = jnp.int32(values[0])
    for place, value in enumerate(values[1:], 1):
        found = jnp.where(index == place, jnp.int32(value), found)
    return found


def sources_of(pairs, train_size):
    return [next((s for s, d in pairs if d == j), -1) for j in range(train_size)]


def nt(left, right):
    return lax.dot_general(left, right, (((1,), (1,)), ((), ())), preferred_element_type=F32)


def two_terms(matrix):
    high = matrix.astype(BF16)
    return jnp.concatenate([high, (matrix - high.astype(F32)).astype(BF16)], axis=1)


def block_diagonal(matrix):
    rank = matrix.shape[0]
    wide = jnp.concatenate([matrix] * PACK, axis=1)
    tall = jnp.concatenate([wide] * PACK, axis=0)
    rows = lax.broadcasted_iota(jnp.int32, tall.shape, 0) // rank
    columns = lax.broadcasted_iota(jnp.int32, tall.shape, 1) // rank
    return jnp.where(rows == columns, tall, 0.0)


def features_kernel(chunks, *refs):
    sides, (queries_hbm, eigen_hbm) = (refs[0:3], refs[3:6]), refs[6:8]
    feats, queries, eigen, basis_in, basis_out, rows, proj, sems = refs[8:]
    core = lax.axis_index("sub")
    step = rows.shape[0] // chunks

    def copies(rows_hbm, proj_hbm):
        pieces = [pl.ds(chunk * step, step) for chunk in range(chunks)]
        pairs = [(rows_hbm.at[0, piece], rows.at[piece]) for piece in pieces]
        pairs.append((proj_hbm.at[0], proj))
        return [pltpu.make_async_copy(*pair, sems.at[0, i]) for i, pair in enumerate(pairs)]

    for side, (rows_hbm, proj_hbm, _) in enumerate(sides):
        @pl.when(core == side)
        def _():
            for copy in copies(rows_hbm, proj_hbm):
                copy.start()

    others = [
        pltpu.make_async_copy(source.at[0], target, sems.at[1, number])
        for number, (source, target) in enumerate((
            (sides[0][2], basis_in), (sides[1][2], basis_out), (eigen_hbm, eigen), (queries_hbm, queries)
        ))
    ]
    for copy in others:
        copy.start()
    for copy in copies(*sides[0][:2]):
        copy.wait()
    total = nt(proj[...], rows[...])
    for copy in others[:2]:
        copy.wait()
    basis = jnp.where(core == 0, basis_in[...], basis_out[...])
    feats[...] = jnp.dot(
        two_terms(basis.T),
        jnp.concatenate([total.astype(BF16)] * 2, axis=0),
        preferred_element_type=F32,
    ).astype(BF16)
    for copy in others[2:]:
        copy.wait()


def pack_kernel(rounds, *refs):
    own, arrivals, out = refs[0], refs[1:1 + len(rounds)], refs[-1]
    train_size = out.shape[0]
    here = lax.axis_index("train")
    out[here] = own[...]
    for pairs, arrival in zip(rounds, arrivals):
        sources = sources_of(pairs, train_size)
        source = lookup(here, sources)
        if min(sources) >= 0:
            out[source] = arrival[...]
        else:
            @pl.when(source >= 0)
            def _():
                out[source] = arrival[...]


def score_block(side_in, side_out, weights):
    rank, tokens = side_in.shape
    side_in = side_in.astype(F32)
    side_out = side_out.reshape(rank // 16, 16, tokens)
    total = None
    span = rank // 4
    for part in range(4):
        products = []
        for b in range(part * span, (part + 1) * span):
            row = jnp.broadcast_to(side_in[b:b + 1, :], (16, tokens)).astype(BF16)
            products.append((side_out * row[None]).reshape(rank, tokens))
        width = span * rank
        term = jnp.dot(
            weights[:, part * width:(part + 1) * width],
            jnp.concatenate(products, axis=0),
            preferred_element_type=F32,
        )
        total = term if total is None else total + term
    return total.T


def queries_kernel(queries, basis_in, basis_out, eigen, *refs):
    weights, half = refs[-2:]
    rank = basis_in.shape[0]
    width = PACK * rank
    groups = rank // PACK
    right = block_diagonal(basis_in[...].T).astype(BF16)
    for part in range(groups):
        half[part * width:(part + 1) * width, :] = nt(
            right, queries[:, part * width:(part + 1) * width]
        )
    left = block_diagonal(basis_out[...]).astype(BF16)
    spectrum = eigen[...]
    inverse = (1.0 / (spectrum + 0.1 * jnp.mean(spectrum))).T
    for part in range(groups):
        columns = range(part * PACK, (part + 1) * PACK)
        matrix = jnp.concatenate(
            [half[pl.ds(b, rank, stride=rank), :] for b in columns], axis=0
        )
        turned = jnp.dot(matrix.T.astype(BF16), left, preferred_element_type=F32)
        scale = jnp.concatenate([inverse[b:b + 1, :] for b in columns], axis=1)
        weights[:, part * width:(part + 1) * width] = (turned * scale).astype(BF16)


def scores_kernel(layer_size, targets, weights, mine, theirs, *refs):
    own, away, scores = refs[-layer_size - 1], refs[-layer_size:-1], refs[-1]
    place, layer, core = (lax.axis_index(name) for name in ("train", "layer", "sub"))
    rows = own.shape[1]
    for i, target in enumerate(targets):
        slot = lookup(place, target)
        here, there = mine[slot], theirs[slot]
        mine_in = (core == 0) == (slot == place)
        scores[...] = score_block(
            jnp.where(mine_in, here, there), jnp.where(mine_in, there, here), weights
        )
        for k, block in enumerate((own, *away)):
            first = pl.multiple_of(lax.rem(layer + k, layer_size) * rows, rows)
            block[i] = scores[pl.ds(first, rows), :].astype(block.dtype)


def layers_kernel(layer_size, places, own, *refs):
    which = places[0] if len(set(places)) == 1 else lookup(lax.axis_index("train"), places)
    total = own[which]
    for other in refs[:layer_size - 1]:
        total = total + other[which].astype(F32)
    refs[-1][...] = total.astype(refs[-1].dtype)


def keep_kernel(block, *refs):
    refs[-1][...] = block[...]


def place_kernel(train_size, rounds, own, *refs):
    arrivals, out = refs[:-1], refs[-1]
    here = lax.axis_index("train")
    rows = own.shape[0]
    out[pl.ds(here, rows, stride=train_size), :] = own[...]
    for pairs, arrival in zip(rounds, arrivals):
        sources = sources_of(pairs, train_size)
        source = lookup(here, sources)
        if min(sources) >= 0:
            out[pl.ds(source, rows, stride=train_size), :] = arrival[...].astype(F32)
        else:
            @pl.when(source >= 0)
            def _():
                out[pl.ds(source, rows, stride=train_size), :] = arrival[...].astype(F32)


def body(inputs, out_grads, proj_in, proj_out, basis_in, basis_out, eigen, queries):
    train_size, layer_size = lax.axis_size("train"), lax.axis_size("layer")
    tokens, width = inputs.shape[1:]
    count, entries = queries.shape[1:]
    rank = proj_in.shape[1]
    chunks = 8
    vmem, hbm = pl.BlockSpec(memory_space=pltpu.VMEM), pl.BlockSpec(memory_space=pltpu.HBM)
    anywhere = pl.BlockSpec(memory_space=pl.ANY)
    params = pltpu.CompilerParams(vmem_limit_bytes=32 << 20)

    sources = (inputs, proj_in, basis_in, out_grads, proj_out, basis_out, queries, eigen)
    feats, queries, eigen, basis_in, basis_out = pl.pallas_call(
        functools.partial(features_kernel, chunks),
        out_shape=[
            jax.ShapeDtypeStruct((rank, tokens), BF16),
            jax.ShapeDtypeStruct((count, entries), BF16),
            *[jax.ShapeDtypeStruct((rank, rank), F32)] * 3,
        ],
        in_specs=[hbm] * len(sources),
        out_specs=[vmem] * 5,
        scratch_shapes=[
            pltpu.VMEM((tokens, width), BF16),
            pltpu.VMEM((rank, width), BF16),
            pltpu.SemaphoreType.DMA((2, chunks + 1)),
        ],
        compiler_params=params,
        cost_estimate=pl.CostEstimate(
            flops=2 * tokens * rank * width, bytes_accessed=2 * width * (tokens + rank), transcendentals=0
        ),
        name="features",
    )(*[pltpu.with_memory_space_constraint(value, pltpu.HBM) for value in sources])

    feature_rounds, score_rounds, first = plan(train_size)

    def kept(block, after):
        return pl.pallas_call(
            keep_kernel,
            out_shape=jax.ShapeDtypeStruct(block.shape, block.dtype),
            in_specs=[vmem] + [anywhere] * len(after),
            out_specs=vmem,
            compiler_params=params,
            name="keep",
        )(block, *after)

    def in_order(blocks):
        ordered = []
        for block in blocks[:-1]:
            ordered.append(kept(block, ordered[-1:]))
        return ordered + blocks[-1:]

    def across(pairs):
        cores = [(2 * s + c, 2 * d + 1 - c) for s, d in pairs for c in range(2)]
        return lax.ppermute(feats, ("train", "sub"), cores)

    gathered = [across(pairs) for pairs in feature_rounds]

    weights = pl.pallas_call(
        queries_kernel,
        out_shape=jax.ShapeDtypeStruct((count, entries), BF16),
        in_specs=[vmem] * 4,
        out_specs=vmem,
        scratch_shapes=[pltpu.VMEM((entries, count), F32)],
        compiler_params=params,
        cost_estimate=pl.CostEstimate(
            flops=4 * PACK * count * entries * rank, bytes_accessed=4 * count * entries, transcendentals=0
        ),
        name="queries",
    )(queries, basis_in, basis_out, eigen)

    mine = pl.pallas_call(
        functools.partial(pack_kernel, feature_rounds[::-1]),
        out_shape=jax.ShapeDtypeStruct((train_size, rank, tokens), BF16),
        in_specs=[vmem] * (1 + len(gathered)) + [anywhere],
        out_specs=vmem,
        compiler_params=params,
        name="pack",
    )(feats, *gathered[::-1], weights)
    theirs = lax.ppermute(mine, "sub", [(0, 1), (1, 0)])

    rows = tokens // layer_size

    def scored(targets, after):
        own, *away = pl.pallas_call(
            functools.partial(scores_kernel, layer_size, targets),
            out_shape=[
                jax.ShapeDtypeStruct((len(targets), rows, count), BF16 if k else F32)
                for k in range(layer_size)
            ],
            in_specs=[vmem] * 3 + [anywhere] * len(after),
            out_specs=[vmem] * layer_size,
            scratch_shapes=[pltpu.VMEM((tokens, count), F32)],
            compiler_params=params,
            cost_estimate=pl.CostEstimate(
                flops=2 * len(targets) * tokens * entries * count,
                bytes_accessed=2 * count * entries,
                transcendentals=0,
            ),
            name="scores",
        )(weights, mine, theirs, *after)
        return own, [
            lax.ppermute(block, "layer", [(l, (l + k) % layer_size) for l in range(layer_size)])
            for k, block in enumerate(away, 1)
        ]

    def summed(places, dtype, own, others, after):
        return pl.pallas_call(
            functools.partial(layers_kernel, layer_size, places),
            out_shape=jax.ShapeDtypeStruct((rows, count), dtype),
            in_specs=[vmem] * layer_size + [anywhere] * len(after),
            out_specs=vmem,
            compiler_params=params,
            name="layers",
        )(own, *others, *after)

    def table(rounds, lead):
        lists = [lead(j) + [d for pairs in rounds for s, d in pairs if s == j] for j in range(train_size)]
        length = max(len(targets) for targets in lists)
        return lists, [
            [targets[i] if i < len(targets) else j for j, targets in enumerate(lists)] for i in range(length)
        ]

    first_lists, first_targets = table(score_rounds[:first], lambda j: [])
    last_lists, last_targets = table(score_rounds[first:], lambda j: [j])
    first_terms = scored(first_targets, [])
    last_terms = scored(last_targets, first_terms[:1])
    arrivals, after = [], []
    for number, pairs in enumerate(score_rounds):
        lists, terms = (first_lists, first_terms) if number < first else (last_lists, last_terms)
        if number == first:
            home = summed([0] * train_size, F32, *last_terms, after)
            after = [home]
        targets = dict(pairs)
        places = [lists[j].index(targets[j]) if j in targets else 0 for j in range(train_size)]
        block = summed(places, BF16, *terms, after)
        after = [block]
        arrivals.append(lax.ppermute(block, "train", pairs))
    if first >= len(score_rounds):
        home = summed([0] * train_size, F32, *last_terms, after)

    total = pl.pallas_call(
        functools.partial(place_kernel, train_size, score_rounds),
        out_shape=jax.ShapeDtypeStruct((rows * train_size, count), F32),
        in_specs=[vmem] * (1 + len(arrivals)),
        out_specs=vmem,
        compiler_params=params,
        name="place",
    )(home, *in_order(arrivals))
    return total.reshape(rows, train_size, 1, count)


def solution(mesh):
    placed = (
        P("layer", ("parts", "train"), None),
        P("layer", ("parts", "train"), None),
        P("layer", None, None),
        P("layer", None, None),
        P("layer", None, None),
        P("layer", None, None),
        P("layer", None, None),
        P("layer", ("parts", "train", "sub"), None),
    )
    return jax.shard_map(
        body,
        mesh=mesh,
        in_specs=placed,
        out_specs=P(("parts", "train", "layer"), None, "sub", None),
        check_vma=False,
    )
```

```python
import functools

import jax
import jax.numpy as jnp
from jax import lax
from jax.experimental import pallas as pl
from jax.experimental.pallas import tpu as pltpu
from jax.sharding import PartitionSpec as P

F32 = jnp.float32
BF16 = jnp.bfloat16
PACK = 4


def plan(train_size):
    if train_size == 4:
        return FEATURE_ROUNDS, SCORE_ROUNDS, FIRST
    rounds = [
        tuple((j, j ^ offset) for j in range(train_size)) for offset in range(train_size - 1, 0, -1)
    ]
    return rounds, rounds, train_size // 2


FEATURE_ROUNDS = [((0, 2), (1, 3), (2, 0), (3, 1)), ((0, 3), (1, 2), (2, 1), (3, 0)), ((0, 1), (1, 0), (2, 3), (3, 2))]
SCORE_ROUNDS = [((0, 1), (1, 2), (2, 3), (3, 0)), ((0, 2), (1, 3), (2, 0), (3, 1)), ((0, 3), (1, 0), (2, 1), (3, 2))]
FIRST = 2


def lookup(index, values):
    found = jnp.int32(values[0])
    for place, value in enumerate(values[1:], 1):
        found = jnp.where(index == place, jnp.int32(value), found)
    return found


def sources_of(pairs, train_size):
    return [next((s for s, d in pairs if d == j), -1) for j in range(train_size)]


def nt(left, right):
    return lax.dot_general(left, right, (((1,), (1,)), ((), ())), preferred_element_type=F32)


def two_terms(matrix):
    high = matrix.astype(BF16)
    return jnp.concatenate([high, (matrix - high.astype(F32)).astype(BF16)], axis=1)


def block_diagonal(matrix):
    rank = matrix.shape[0]
    wide = jnp.concatenate([matrix] * PACK, axis=1)
    tall = jnp.concatenate([wide] * PACK, axis=0)
    rows = lax.broadcasted_iota(jnp.int32, tall.shape, 0) // rank
    columns = lax.broadcasted_iota(jnp.int32, tall.shape, 1) // rank
    return jnp.where(rows == columns, tall, 0.0)


def features_kernel(chunks, *refs):
    sides, (feats, rows, proj, basis, sems) = (refs[0:3], refs[3:6]), refs[6:]
    core = lax.axis_index("sub")
    step = rows.shape[0] // chunks

    def copies(rows_hbm, proj_hbm, basis_hbm):
        pieces = [pl.ds(chunk * step, step) for chunk in range(chunks)]
        pairs = [(rows_hbm.at[0, piece], rows.at[piece]) for piece in pieces]
        pairs += [(proj_hbm.at[0], proj), (basis_hbm.at[0], basis)]
        return [pltpu.make_async_copy(*pair, sems.at[i]) for i, pair in enumerate(pairs)]

    for number, side in enumerate(sides):
        @pl.when(core == number)
        def _():
            for copy in copies(*side):
                copy.start()

    for copy in copies(*sides[0]):
        copy.wait()
    total = nt(proj[...], rows[...])
    feats[...] = jnp.dot(
        two_terms(basis[...].T),
        jnp.concatenate([total.astype(BF16)] * 2, axis=0),
        preferred_element_type=F32,
    ).astype(BF16)


def pack_kernel(rounds, *refs):
    own, arrivals, out = refs[0], refs[1:1 + len(rounds)], refs[-1]
    train_size = out.shape[0]
    here = lax.axis_index("train")
    out[here] = own[...]
    for pairs, arrival in zip(rounds, arrivals):
        sources = sources_of(pairs, train_size)
        source = lookup(here, sources)
        if min(sources) >= 0:
            out[source] = arrival[...]
        else:
            @pl.when(source >= 0)
            def _():
                out[source] = arrival[...]


def score_block(side_in, side_out, weights):
    rank, tokens = side_in.shape
    side_in = side_in.astype(F32)
    side_out = side_out.reshape(rank // 16, 16, tokens)
    total = None
    span = rank // 4
    for part in range(4):
        products = []
        for b in range(part * span, (part + 1) * span):
            row = jnp.broadcast_to(side_in[b:b + 1, :], (16, tokens)).astype(BF16)
            products.append((side_out * row[None]).reshape(rank, tokens))
        width = span * rank
        term = jnp.dot(
            weights[:, part * width:(part + 1) * width],
            jnp.concatenate(products, axis=0),
            preferred_element_type=F32,
        )
        total = term if total is None else total + term
    return total.T


def queries_kernel(queries, basis_in, basis_out, eigen, *refs):
    weights, half = refs[-2:]
    rank = basis_in.shape[0]
    width = PACK * rank
    groups = rank // PACK
    right = block_diagonal(basis_in[...].T).astype(BF16)
    for part in range(groups):
        half[part * width:(part + 1) * width, :] = nt(
            right, queries[:, part * width:(part + 1) * width]
        )
    left = block_diagonal(basis_out[...]).astype(BF16)
    spectrum = eigen[...]
    inverse = (1.0 / (spectrum + 0.1 * jnp.mean(spectrum))).T
    for part in range(groups):
        columns = range(part * PACK, (part + 1) * PACK)
        matrix = jnp.concatenate(
            [half[pl.ds(b, rank, stride=rank), :] for b in columns], axis=0
        )
        turned = jnp.dot(matrix.T.astype(BF16), left, preferred_element_type=F32)
        scale = jnp.concatenate([inverse[b:b + 1, :] for b in columns], axis=1)
        weights[:, part * width:(part + 1) * width] = (turned * scale).astype(BF16)


def scores_kernel(layer_size, targets, weights, mine, theirs, *refs):
    own, away, scores = refs[-layer_size - 1], refs[-layer_size:-1], refs[-1]
    place, layer, core = (lax.axis_index(name) for name in ("train", "layer", "sub"))
    rows = own.shape[1]
    for i, target in enumerate(targets):
        slot = lookup(place, target)
        here, there = mine[slot], theirs[slot]
        mine_in = (core == 0) == (slot == place)
        scores[...] = score_block(
            jnp.where(mine_in, here, there), jnp.where(mine_in, there, here), weights
        )
        for k, block in enumerate((own, *away)):
            first = pl.multiple_of(lax.rem(layer + k, layer_size) * rows, rows)
            block[i] = scores[pl.ds(first, rows), :].astype(block.dtype)


def layers_kernel(layer_size, places, own, *refs):
    which = places[0] if len(set(places)) == 1 else lookup(lax.axis_index("train"), places)
    total = own[which]
    for other in refs[:layer_size - 1]:
        total = total + other[which].astype(F32)
    refs[-1][...] = total.astype(refs[-1].dtype)


def keep_kernel(block, *refs):
    refs[-1][...] = block[...]


def place_kernel(train_size, rounds, own, *refs):
    arrivals, out = refs[:-1], refs[-1]
    here = lax.axis_index("train")
    rows = own.shape[0]
    out[pl.ds(here, rows, stride=train_size), :] = own[...]
    for pairs, arrival in zip(rounds, arrivals):
        sources = sources_of(pairs, train_size)
        source = lookup(here, sources)
        if min(sources) >= 0:
            out[pl.ds(source, rows, stride=train_size), :] = arrival[...].astype(F32)
        else:
            @pl.when(source >= 0)
            def _():
                out[pl.ds(source, rows, stride=train_size), :] = arrival[...].astype(F32)


def body(inputs, out_grads, proj_in, proj_out, basis_in, basis_out, eigen, queries):
    train_size, layer_size = lax.axis_size("train"), lax.axis_size("layer")
    tokens, width = inputs.shape[1:]
    count, entries = queries.shape[1:]
    rank = proj_in.shape[1]
    chunks = 4
    vmem, hbm = pl.BlockSpec(memory_space=pltpu.VMEM), pl.BlockSpec(memory_space=pltpu.HBM)
    anywhere = pl.BlockSpec(memory_space=pl.ANY)
    params = pltpu.CompilerParams(vmem_limit_bytes=32 << 20)

    sources = (inputs, proj_in, basis_in, out_grads, proj_out, basis_out)
    feats = pl.pallas_call(
        functools.partial(features_kernel, chunks),
        out_shape=jax.ShapeDtypeStruct((rank, tokens), BF16),
        in_specs=[hbm] * len(sources),
        out_specs=vmem,
        scratch_shapes=[
            pltpu.VMEM((tokens, width), BF16),
            pltpu.VMEM((rank, width), BF16),
            pltpu.VMEM((rank, rank), F32),
            pltpu.SemaphoreType.DMA((chunks + 2,)),
        ],
        compiler_params=params,
        cost_estimate=pl.CostEstimate(
            flops=2 * tokens * rank * width, bytes_accessed=2 * width * (tokens + rank), transcendentals=0
        ),
        name="features",
    )(*[pltpu.with_memory_space_constraint(value, pltpu.HBM) for value in sources])

    feature_rounds, score_rounds, first = plan(train_size)

    def kept(block, after):
        return pl.pallas_call(
            keep_kernel,
            out_shape=jax.ShapeDtypeStruct(block.shape, block.dtype),
            in_specs=[vmem] + [anywhere] * len(after),
            out_specs=vmem,
            compiler_params=params,
            name="keep",
        )(block, *after)

    def in_order(blocks):
        ordered = []
        for block in blocks[:-1]:
            ordered.append(kept(block, ordered[-1:]))
        return ordered + blocks[-1:]

    def across(pairs):
        cores = [(2 * s + c, 2 * d + 1 - c) for s, d in pairs for c in range(2)]
        return lax.ppermute(feats, ("train", "sub"), cores)

    gathered = [across(pairs) for pairs in feature_rounds]

    weights = pl.pallas_call(
        queries_kernel,
        out_shape=jax.ShapeDtypeStruct((count, entries), BF16),
        in_specs=[vmem] * 4,
        out_specs=vmem,
        scratch_shapes=[pltpu.VMEM((entries, count), F32)],
        compiler_params=params,
        cost_estimate=pl.CostEstimate(
            flops=4 * PACK * count * entries * rank, bytes_accessed=4 * count * entries, transcendentals=0
        ),
        name="queries",
    )(queries[0], basis_in[0], basis_out[0], eigen[0])

    mine = pl.pallas_call(
        functools.partial(pack_kernel, feature_rounds),
        out_shape=jax.ShapeDtypeStruct((train_size, rank, tokens), BF16),
        in_specs=[vmem] * (1 + len(gathered)) + [anywhere],
        out_specs=vmem,
        compiler_params=params,
        name="pack",
    )(feats, *gathered, weights)
    theirs = lax.ppermute(mine, "sub", [(0, 1), (1, 0)])

    rows = tokens // layer_size

    def scored(targets, after):
        own, *away = pl.pallas_call(
            functools.partial(scores_kernel, layer_size, targets),
            out_shape=[
                jax.ShapeDtypeStruct((len(targets), rows, count), BF16 if k else F32)
                for k in range(layer_size)
            ],
            in_specs=[vmem] * 3 + [anywhere] * len(after),
            out_specs=[vmem] * layer_size,
            scratch_shapes=[pltpu.VMEM((tokens, count), F32)],
            compiler_params=params,
            cost_estimate=pl.CostEstimate(
                flops=2 * len(targets) * tokens * entries * count,
                bytes_accessed=2 * count * entries,
                transcendentals=0,
            ),
            name="scores",
        )(weights, mine, theirs, *after)
        return own, [
            lax.ppermute(block, "layer", [(l, (l + k) % layer_size) for l in range(layer_size)])
            for k, block in enumerate(away, 1)
        ]

    def summed(places, dtype, own, others, after):
        return pl.pallas_call(
            functools.partial(layers_kernel, layer_size, places),
            out_shape=jax.ShapeDtypeStruct((rows, count), dtype),
            in_specs=[vmem] * layer_size + [anywhere] * len(after),
            out_specs=vmem,
            compiler_params=params,
            name="layers",
        )(own, *others, *after)

    def table(rounds, lead):
        lists = [lead(j) + [d for pairs in rounds for s, d in pairs if s == j] for j in range(train_size)]
        length = max(len(targets) for targets in lists)
        return lists, [
            [targets[i] if i < len(targets) else j for j, targets in enumerate(lists)] for i in range(length)
        ]

    first_lists, first_targets = table(score_rounds[:first], lambda j: [])
    last_lists, last_targets = table(score_rounds[first:], lambda j: [j])
    first_terms = scored(first_targets, [])
    last_terms = scored(last_targets, first_terms[:1])
    arrivals, after = [], []
    for number, pairs in enumerate(score_rounds):
        lists, terms = (first_lists, first_terms) if number < first else (last_lists, last_terms)
        if number == first:
            home = summed([0] * train_size, F32, *last_terms, after)
            after = [home]
        targets = dict(pairs)
        places = [lists[j].index(targets[j]) if j in targets else 0 for j in range(train_size)]
        block = summed(places, BF16, *terms, after)
        after = [block]
        arrivals.append(lax.ppermute(block, "train", pairs))
    if first >= len(score_rounds):
        home = summed([0] * train_size, F32, *last_terms, after)

    total = pl.pallas_call(
        functools.partial(place_kernel, train_size, score_rounds),
        out_shape=jax.ShapeDtypeStruct((rows * train_size, count), F32),
        in_specs=[vmem] * (1 + len(arrivals)),
        out_specs=vmem,
        compiler_params=params,
        name="place",
    )(home, *in_order(arrivals))
    return total.reshape(rows, train_size, 1, count)


def solution(mesh):
    placed = (
        P("layer", ("parts", "train"), None),
        P("layer", ("parts", "train"), None),
        P("layer", None, None),
        P("layer", None, None),
        P("layer", None, None),
        P("layer", None, None),
        P("layer", None, None),
        P("layer", ("parts", "train", "sub"), None),
    )
    return jax.shard_map(
        body,
        mesh=mesh,
        in_specs=placed,
        out_specs=P(("parts", "train", "layer"), None, "sub", None),
        check_vma=False,
    )
```

```python
import functools

import jax
import jax.numpy as jnp
from jax import lax
from jax.experimental import pallas as pl
from jax.experimental.pallas import tpu as pltpu
from jax.sharding import PartitionSpec as P

F32 = jnp.float32
BF16 = jnp.bfloat16
PACK = 4


def plan(train_size):
    if train_size == 4:
        return FEATURE_ROUNDS, SCORE_ROUNDS, FIRST
    rounds = [
        tuple((j, j ^ offset) for j in range(train_size)) for offset in range(train_size - 1, 0, -1)
    ]
    return rounds, rounds, train_size // 2


FEATURE_ROUNDS = [((0, 2), (1, 3), (2, 0), (3, 1)), ((0, 3), (1, 2), (2, 1), (3, 0)), ((0, 1), (1, 0), (2, 3), (3, 2))]
SCORE_ROUNDS = [((0, 1), (1, 2), (2, 3), (3, 0)), ((0, 2), (1, 3), (2, 0), (3, 1)), ((0, 3), (1, 0), (2, 1), (3, 2))]
FIRST = 2


def lookup(index, values):
    found = jnp.int32(values[0])
    for place, value in enumerate(values[1:], 1):
        found = jnp.where(index == place, jnp.int32(value), found)
    return found


def sources_of(pairs, train_size):
    return [next((s for s, d in pairs if d == j), -1) for j in range(train_size)]


def nt(left, right):
    return lax.dot_general(left, right, (((1,), (1,)), ((), ())), preferred_element_type=F32)


def two_terms(matrix):
    high = matrix.astype(BF16)
    return jnp.concatenate([high, (matrix - high.astype(F32)).astype(BF16)], axis=1)


def block_diagonal(matrix):
    rank = matrix.shape[0]
    wide = jnp.concatenate([matrix] * PACK, axis=1)
    tall = jnp.concatenate([wide] * PACK, axis=0)
    rows = lax.broadcasted_iota(jnp.int32, tall.shape, 0) // rank
    columns = lax.broadcasted_iota(jnp.int32, tall.shape, 1) // rank
    return jnp.where(rows == columns, tall, 0.0)


def features_kernel(chunks, *refs):
    sides, (feats, rows, proj, basis, sems) = (refs[0:3], refs[3:6]), refs[6:]
    core = lax.axis_index("sub")
    step = rows.shape[0] // chunks

    def copies(rows_hbm, proj_hbm, basis_hbm):
        pieces = [pl.ds(chunk * step, step) for chunk in range(chunks)]
        pairs = [(rows_hbm.at[0, piece], rows.at[piece]) for piece in pieces]
        pairs += [(proj_hbm.at[0], proj), (basis_hbm.at[0], basis)]
        return [pltpu.make_async_copy(*pair, sems.at[i]) for i, pair in enumerate(pairs)]

    for number, side in enumerate(sides):
        @pl.when(core == number)
        def _():
            for copy in copies(*side):
                copy.start()

    for copy in copies(*sides[0]):
        copy.wait()
    total = nt(proj[...], rows[...])
    feats[...] = jnp.dot(
        two_terms(basis[...].T),
        jnp.concatenate([total.astype(BF16)] * 2, axis=0),
        preferred_element_type=F32,
    ).astype(BF16)


def pack_kernel(rounds, *refs):
    own, arrivals, out = refs[0], refs[1:1 + len(rounds)], refs[-1]
    train_size = out.shape[0]
    here = lax.axis_index("train")
    out[here] = own[...]
    for pairs, arrival in zip(rounds, arrivals):
        sources = sources_of(pairs, train_size)
        source = lookup(here, sources)
        if min(sources) >= 0:
            out[source] = arrival[...]
        else:
            @pl.when(source >= 0)
            def _():
                out[source] = arrival[...]


def score_block(side_in, side_out, weights):
    rank, tokens = side_in.shape
    side_in = side_in.astype(F32)
    side_out = side_out.reshape(rank // 16, 16, tokens)
    total = None
    span = rank // 4
    for part in range(4):
        products = []
        for b in range(part * span, (part + 1) * span):
            row = jnp.broadcast_to(side_in[b:b + 1, :], (16, tokens)).astype(BF16)
            products.append((side_out * row[None]).reshape(rank, tokens))
        width = span * rank
        term = jnp.dot(
            weights[:, part * width:(part + 1) * width],
            jnp.concatenate(products, axis=0),
            preferred_element_type=F32,
        )
        total = term if total is None else total + term
    return total.T


def queries_kernel(queries, basis_in, basis_out, eigen, *refs):
    weights, half = refs[-2:]
    rank = basis_in.shape[0]
    width = PACK * rank
    groups = rank // PACK
    right = block_diagonal(basis_in[...].T).astype(BF16)
    for part in range(groups):
        half[part * width:(part + 1) * width, :] = nt(
            right, queries[:, part * width:(part + 1) * width]
        )
    left = block_diagonal(basis_out[...]).astype(BF16)
    spectrum = eigen[...]
    inverse = (1.0 / (spectrum + 0.1 * jnp.mean(spectrum))).T
    for part in range(groups):
        columns = range(part * PACK, (part + 1) * PACK)
        matrix = jnp.concatenate(
            [half[pl.ds(b, rank, stride=rank), :] for b in columns], axis=0
        )
        turned = jnp.dot(matrix.T.astype(BF16), left, preferred_element_type=F32)
        scale = jnp.concatenate([inverse[b:b + 1, :] for b in columns], axis=1)
        weights[:, part * width:(part + 1) * width] = (turned * scale).astype(BF16)


def scores_kernel(layer_size, targets, weights, mine, theirs, *refs):
    own, away, scores = refs[-layer_size - 1], refs[-layer_size:-1], refs[-1]
    place, layer, core = (lax.axis_index(name) for name in ("train", "layer", "sub"))
    rows = own.shape[1]
    for i, target in enumerate(targets):
        slot = lookup(place, target)
        here, there = mine[slot], theirs[slot]
        mine_in = (core == 0) == (slot == place)
        scores[...] = score_block(
            jnp.where(mine_in, here, there), jnp.where(mine_in, there, here), weights
        )
        for k, block in enumerate((own, *away)):
            first = pl.multiple_of(lax.rem(layer + k, layer_size) * rows, rows)
            block[i] = scores[pl.ds(first, rows), :].astype(block.dtype)


def layers_kernel(layer_size, places, own, *refs):
    which = places[0] if len(set(places)) == 1 else lookup(lax.axis_index("train"), places)
    total = own[which]
    for other in refs[:layer_size - 1]:
        total = total + other[which].astype(F32)
    refs[-1][...] = total.astype(refs[-1].dtype)


def keep_kernel(block, *refs):
    refs[-1][...] = block[...]


def place_kernel(train_size, rounds, own, *refs):
    arrivals, out = refs[:-1], refs[-1]
    here = lax.axis_index("train")
    rows = own.shape[0]
    out[pl.ds(here, rows, stride=train_size), :] = own[...]
    for pairs, arrival in zip(rounds, arrivals):
        sources = sources_of(pairs, train_size)
        source = lookup(here, sources)
        if min(sources) >= 0:
            out[pl.ds(source, rows, stride=train_size), :] = arrival[...].astype(F32)
        else:
            @pl.when(source >= 0)
            def _():
                out[pl.ds(source, rows, stride=train_size), :] = arrival[...].astype(F32)


def body(inputs, out_grads, proj_in, proj_out, basis_in, basis_out, eigen, queries):
    train_size, layer_size = lax.axis_size("train"), lax.axis_size("layer")
    tokens, width = inputs.shape[1:]
    count, entries = queries.shape[1:]
    rank = proj_in.shape[1]
    chunks = 2
    vmem, hbm = pl.BlockSpec(memory_space=pltpu.VMEM), pl.BlockSpec(memory_space=pltpu.HBM)
    anywhere = pl.BlockSpec(memory_space=pl.ANY)
    params = pltpu.CompilerParams(vmem_limit_bytes=32 << 20)

    sources = (inputs, proj_in, basis_in, out_grads, proj_out, basis_out)
    feats = pl.pallas_call(
        functools.partial(features_kernel, chunks),
        out_shape=jax.ShapeDtypeStruct((rank, tokens), BF16),
        in_specs=[hbm] * len(sources),
        out_specs=vmem,
        scratch_shapes=[
            pltpu.VMEM((tokens, width), BF16),
            pltpu.VMEM((rank, width), BF16),
            pltpu.VMEM((rank, rank), F32),
            pltpu.SemaphoreType.DMA((chunks + 2,)),
        ],
        compiler_params=params,
        cost_estimate=pl.CostEstimate(
            flops=2 * tokens * rank * width, bytes_accessed=2 * width * (tokens + rank), transcendentals=0
        ),
        name="features",
    )(*[pltpu.with_memory_space_constraint(value, pltpu.HBM) for value in sources])

    feature_rounds, score_rounds, first = plan(train_size)

    def kept(block, after):
        return pl.pallas_call(
            keep_kernel,
            out_shape=jax.ShapeDtypeStruct(block.shape, block.dtype),
            in_specs=[vmem] + [anywhere] * len(after),
            out_specs=vmem,
            compiler_params=params,
            name="keep",
        )(block, *after)

    def in_order(blocks):
        ordered = []
        for block in blocks[:-1]:
            ordered.append(kept(block, ordered[-1:]))
        return ordered + blocks[-1:]

    def across(pairs):
        cores = [(2 * s + c, 2 * d + 1 - c) for s, d in pairs for c in range(2)]
        return lax.ppermute(feats, ("train", "sub"), cores)

    gathered = [across(pairs) for pairs in feature_rounds]

    weights = pl.pallas_call(
        queries_kernel,
        out_shape=jax.ShapeDtypeStruct((count, entries), BF16),
        in_specs=[vmem] * 4,
        out_specs=vmem,
        scratch_shapes=[pltpu.VMEM((entries, count), F32)],
        compiler_params=params,
        cost_estimate=pl.CostEstimate(
            flops=4 * PACK * count * entries * rank, bytes_accessed=4 * count * entries, transcendentals=0
        ),
        name="queries",
    )(queries[0], basis_in[0], basis_out[0], eigen[0])

    mine = pl.pallas_call(
        functools.partial(pack_kernel, feature_rounds),
        out_shape=jax.ShapeDtypeStruct((train_size, rank, tokens), BF16),
        in_specs=[vmem] * (1 + len(gathered)) + [anywhere],
        out_specs=vmem,
        compiler_params=params,
        name="pack",
    )(feats, *gathered, weights)
    theirs = lax.ppermute(mine, "sub", [(0, 1), (1, 0)])

    rows = tokens // layer_size

    def scored(targets, after):
        own, *away = pl.pallas_call(
            functools.partial(scores_kernel, layer_size, targets),
            out_shape=[
                jax.ShapeDtypeStruct((len(targets), rows, count), BF16 if k else F32)
                for k in range(layer_size)
            ],
            in_specs=[vmem] * 3 + [anywhere] * len(after),
            out_specs=[vmem] * layer_size,
            scratch_shapes=[pltpu.VMEM((tokens, count), F32)],
            compiler_params=params,
            cost_estimate=pl.CostEstimate(
                flops=2 * len(targets) * tokens * entries * count,
                bytes_accessed=2 * count * entries,
                transcendentals=0,
            ),
            name="scores",
        )(weights, mine, theirs, *after)
        return own, [
            lax.ppermute(block, "layer", [(l, (l + k) % layer_size) for l in range(layer_size)])
            for k, block in enumerate(away, 1)
        ]

    def summed(places, dtype, own, others, after):
        return pl.pallas_call(
            functools.partial(layers_kernel, layer_size, places),
            out_shape=jax.ShapeDtypeStruct((rows, count), dtype),
            in_specs=[vmem] * layer_size + [anywhere] * len(after),
            out_specs=vmem,
            compiler_params=params,
            name="layers",
        )(own, *others, *after)

    def table(rounds, lead):
        lists = [lead(j) + [d for pairs in rounds for s, d in pairs if s == j] for j in range(train_size)]
        length = max(len(targets) for targets in lists)
        return lists, [
            [targets[i] if i < len(targets) else j for j, targets in enumerate(lists)] for i in range(length)
        ]

    first_lists, first_targets = table(score_rounds[:first], lambda j: [])
    last_lists, last_targets = table(score_rounds[first:], lambda j: [j])
    first_terms = scored(first_targets, [])
    last_terms = scored(last_targets, first_terms[:1])
    arrivals, after = [], []
    for number, pairs in enumerate(score_rounds):
        lists, terms = (first_lists, first_terms) if number < first else (last_lists, last_terms)
        if number == first:
            home = summed([0] * train_size, F32, *last_terms, after)
            after = [home]
        targets = dict(pairs)
        places = [lists[j].index(targets[j]) if j in targets else 0 for j in range(train_size)]
        block = summed(places, BF16, *terms, after)
        after = [block]
        arrivals.append(lax.ppermute(block, "train", pairs))
    if first >= len(score_rounds):
        home = summed([0] * train_size, F32, *last_terms, after)

    total = pl.pallas_call(
        functools.partial(place_kernel, train_size, score_rounds),
        out_shape=jax.ShapeDtypeStruct((rows * train_size, count), F32),
        in_specs=[vmem] * (1 + len(arrivals)),
        out_specs=vmem,
        compiler_params=params,
        name="place",
    )(home, *in_order(arrivals))
    return total.reshape(rows, train_size, 1, count)


def solution(mesh):
    placed = (
        P("layer", ("parts", "train"), None),
        P("layer", ("parts", "train"), None),
        P("layer", None, None),
        P("layer", None, None),
        P("layer", None, None),
        P("layer", None, None),
        P("layer", None, None),
        P("layer", ("parts", "train", "sub"), None),
    )
    return jax.shard_map(
        body,
        mesh=mesh,
        in_specs=placed,
        out_specs=P(("parts", "train", "layer"), None, "sub", None),
        check_vma=False,
    )
```
